128 devices in a mesh: gx: 8 (over z, core), gy: 16 (over x, y).
Axes of the slice: x: 4, y: 4, z: 4, core: 2. Of those that a mesh axis runs over, the one named last changes fastest.
Arguments:
- jac_cam: float32 [8, 16, 128, 18, 128], P('gx', 'gy'), may hold values from -6 to 6
- jac_pt: float32 [8, 16, 128, 6, 128], P('gx', 'gy'), may hold values from -6 to 6
- resid0: float32 [8, 16, 128, 2, 128], P('gx', 'gy'), may hold values from -40 to 40
- obs_count: int32 [8, 16, 128], P('gx', 'gy'), may hold values from 0 to 128, as said below
- tile_camera: int32 [8, 16, 128], P('gx', 'gy'), may hold values from 0 to 3
- tile_points: int32 [8, 16, 128], P('gx', 'gy'), may hold values from 0 to 143, as said below
- obs_camera: int32 [8, 16, 128, 128], P('gx', 'gy'), may hold values from 0 to 63
- obs_point: int32 [8, 16, 128, 128], P('gx', 'gy'), may hold values from 0 to 127
- cam_params: float32 [8, 16, 4, 9, 64], P('gx', 'gy'), may hold values from -6 to 6
- pt_params: float32 [8, 16, 16, 3, 128], P('gx', 'gy'), may hold values from -6 to 6
- cg_start: float32 [8, 16, 4, 9, 64], P('gx', 'gy'), may hold values from -1.5 to 1.5
Outputs:
- cam_out: float32 [8, 16, 4, 9, 64], P('gx', 'gy')
- pt_out: float32 [8, 16, 16, 3, 128], P('gx', 'gy')
- resid_out: float32 [8, 16, 128, 2, 128], P('gx', 'gy')
- costs: float32 [3], replicated
The draws below stay inside these ranges and needn't reach their ends.
Inputs may be any that keep to these rules, and one draw needn't show every extreme that they name: `obs_count`: on each device the tiles that hold observations come first, 16 or more of them, each with 64 or more observations in its first slots; some device has no tile without observations. `tile_points`: A slot (3 a + b) * 16 + q stands for point block q of the device a - 1 steps along gx and b - 1 steps along gy; it never names a device outside the grid.
All inputs are finite; a program needn't handle non-finite values.
Results may differ from the reference program's by a relative error of at most 0.0001.
Values sent between devices are 32-bit elements; how exact they have to be, the bound alone decides.
A program may use at most 64 MiB of HBM per device.

```python
import jax
import jax.numpy as jnp

CPAR = 9
CAMB = 64
PTS = 128
OBS_TILE = 128
LM_STEPS = 2
CG_ITERS = 2
CB_DEV = 4
PB_DEV = 16
TILES_DEV = 128
GRID_X = 8
GRID_Y = 16


def draw_obs_count(key, part):
    key = jax.random.fold_in(key, 5)
    key_live, key_busy, key_fill, key_full = jax.random.split(key, 4)
    devices_total = GRID_X * GRID_Y
    lowest = max(TILES_DEV // 8, 1)
    live = jax.random.randint(key_live, (devices_total,), lowest, TILES_DEV)
    busiest = jax.random.randint(key_busy, (), 0, devices_total)
    device_ids = jnp.arange(devices_total, dtype=jnp.int32)
    live = jnp.where(device_ids == busiest, TILES_DEV, live)
    filled = jax.random.randint(key_fill, (devices_total, TILES_DEV), OBS_TILE // 2, OBS_TILE + 1)
    full_tile = jax.random.randint(key_full, (), 0, TILES_DEV)
    tile_ids = jnp.arange(TILES_DEV, dtype=jnp.int32)
    filled = jnp.where((device_ids[:, None] == busiest) & (tile_ids[None, :] == full_tile), OBS_TILE, filled)
    filled = jnp.where(tile_ids[None, :] < live[:, None], filled, 0)
    return filled.reshape(GRID_X, GRID_Y, TILES_DEV).astype(jnp.int32)


def draw_tile_points(key, part):
    key = jax.random.fold_in(key, 7)
    key_home, key_east, key_north, key_block = jax.random.split(key, 4)
    shape_all = (GRID_X, GRID_Y, TILES_DEV)
    at_home = jax.random.randint(key_home, shape_all, 0, 2)
    along_x = jax.random.randint(key_east, shape_all, 0, 3)
    along_y = jax.random.randint(key_north, shape_all, 0, 3)
    along_x = jnp.where(at_home == 1, 1, along_x)
    along_y = jnp.where(at_home == 1, 1, along_y)
    row_ids = jnp.arange(GRID_X, dtype=jnp.int32)[:, None, None] + along_x - 1
    col_ids = jnp.arange(GRID_Y, dtype=jnp.int32)[None, :, None] + along_y - 1
    along_x = jnp.where((row_ids >= 0) & (row_ids < GRID_X), along_x, 1)
    along_y = jnp.where((col_ids >= 0) & (col_ids < GRID_Y), along_y, 1)
    block_ids = jax.random.randint(key_block, shape_all, 0, PB_DEV)
    chosen = (along_x * 3 + along_y) * PB_DEV + block_ids
    chosen = chosen.at[0, 0, 0].set(9 * PB_DEV - 1)
    chosen = chosen.at[GRID_X - 1, GRID_Y - 1, 0].set(0)
    return chosen.astype(jnp.int32)


def draw_resid0(key, part):
    key = jax.random.fold_in(key, 9)
    key_base = jax.random.fold_in(key, 0)
    shape_all = (GRID_X, GRID_Y, TILES_DEV, 2, OBS_TILE)
    east_ramp = jnp.arange(GRID_X, dtype=jnp.float32) / max(GRID_X - 1, 1)
    north_ramp = jnp.arange(GRID_Y, dtype=jnp.float32) / max(GRID_Y - 1, 1)
    ramp = jnp.exp(jnp.log(3.0) * (east_ramp[:, None] + north_ramp[None, :] - 1.0))
    base = jax.random.normal(key_base, shape_all, jnp.float32)
    return (base * ramp[:, :, None, None, None]).astype(jnp.float32)


def place_ends(array, stream_key, low, largest):
    index_at = [jax.random.randint(jax.random.fold_in(stream_key, axis), (), 0, length) for axis, length in enumerate(array.shape)]
    widest = array.shape.index(max(array.shape))
    beside = index_at[:widest] + [(index_at[widest] + 1) % array.shape[widest]] + index_at[widest + 1:]
    return array.at[tuple(index_at)].set(low).at[tuple(beside)].set(largest)


def shard_levels(stream_key, extent, cuts, least, largest):
    level, own = 1.0, jax.random.fold_in(stream_key, 6)
    for axis_at, blocks in cuts:
        heights = jnp.exp(jax.random.uniform(jax.random.fold_in(own, axis_at), (blocks,), jnp.float32, least / len(cuts), largest / len(cuts)))
        level = level * jnp.repeat(heights, extent[axis_at] // blocks).reshape([-1 if axis == axis_at else 1 for axis in range(len(extent))])
    return level


def centred(own_key, extent, deviation, reach, cuts=(), kind=jnp.bfloat16):
    array = jax.random.normal(own_key, extent, jnp.float32) * deviation
    if len(cuts) > 0:
        array = shard_levels(own_key, extent, cuts, -0.22, 0.18) * array
    return jnp.clip(array, min=-reach, max=reach).astype(kind)


def setup_inputs(seed: int = 0) -> dict:
    seeds = jax.random.split(jax.random.key(seed), 12)
    jac_cam = centred(seeds[0], (GRID_X, GRID_Y, TILES_DEV, 2 * CPAR, OBS_TILE), 1.0, 6.0, ((0, 8), (1, 16)), jnp.float32)
    jac_pt = centred(seeds[1], (GRID_X, GRID_Y, TILES_DEV, 6, OBS_TILE), 1.0, 6.0, ((0, 8), (1, 16)), jnp.float32)
    resid0 = draw_resid0(jax.random.fold_in(seeds[11], 71), 0)
    obs_count = draw_obs_count(jax.random.fold_in(seeds[11], 71), 0)
    tile_camera = place_ends(jax.random.randint(seeds[4], (GRID_X, GRID_Y, TILES_DEV), 0, CB_DEV), jax.random.fold_in(seeds[4], 1), 0, CB_DEV - 1).astype(jnp.int32)
    tile_points = draw_tile_points(jax.random.fold_in(seeds[11], 71), 0)
    obs_camera = place_ends(jax.random.randint(seeds[6], (GRID_X, GRID_Y, TILES_DEV, OBS_TILE), 0, CAMB), jax.random.fold_in(seeds[6], 1), 0, CAMB - 1).astype(jnp.int32)
    obs_point = place_ends(jax.random.randint(seeds[7], (GRID_X, GRID_Y, TILES_DEV, OBS_TILE), 0, PTS), jax.random.fold_in(seeds[7], 1), 0, PTS - 1).astype(jnp.int32)
    cam_params = centred(seeds[8], (GRID_X, GRID_Y, CB_DEV, CPAR, CAMB), 1.0, 6.0, ((0, 8), (1, 16)), jnp.float32)
    pt_params = centred(seeds[9], (GRID_X, GRID_Y, PB_DEV, 3, PTS), 1.0, 6.0, ((0, 8), (1, 16)), jnp.float32)
    cg_start = centred(seeds[10], (GRID_X, GRID_Y, CB_DEV, CPAR, CAMB), 0.1, 1.5, ((0, 8), (1, 16)), jnp.float32)
    return dict(jac_cam=jac_cam, jac_pt=jac_pt, resid0=resid0, obs_count=obs_count, tile_camera=tile_camera, tile_points=tile_points, obs_camera=obs_camera, obs_point=obs_point, cam_params=cam_params, pt_params=pt_params, cg_start=cg_start)


damping_first = 1.0
damping_ratio = 0.25
hess_pairs = ((0, 0), (0, 1), (0, 2), (1, 1), (1, 2), (2, 2))


def damped_inverse_apply(hess_cols, vector, damping):
    h_zero = hess_cols[0] + damping * (hess_cols[0] + 1.0)
    h_zero_one = hess_cols[1]
    h_zero_two = hess_cols[2]
    h_one = hess_cols[3] + damping * (hess_cols[3] + 1.0)
    h_one_two = hess_cols[4]
    h_two = hess_cols[5] + damping * (hess_cols[5] + 1.0)
    cof_zero = h_one * h_two - h_one_two * h_one_two
    cof_zero_one = h_zero_two * h_one_two - h_zero_one * h_two
    cof_zero_two = h_zero_one * h_one_two - h_zero_two * h_one
    cof_one = h_zero * h_two - h_zero_two * h_zero_two
    cof_one_two = h_zero_one * h_zero_two - h_zero * h_one_two
    cof_two = h_zero * h_one - h_zero_one * h_zero_one
    determ = h_zero * cof_zero + h_zero_one * cof_zero_one + h_zero_two * cof_zero_two
    out_zero = (cof_zero * vector[0] + cof_zero_one * vector[1] + cof_zero_two * vector[2]) / determ
    out_one = (cof_zero_one * vector[0] + cof_one * vector[1] + cof_one_two * vector[2]) / determ
    out_two = (cof_zero_two * vector[0] + cof_one_two * vector[1] + cof_two * vector[2]) / determ
    return out_zero, out_one, out_two


def reference(jac_cam, jac_pt, resid0, obs_count, tile_camera, tile_points, obs_camera, obs_point, cam_params, pt_params, cg_start):
    grid_rows, grid_cols, tile_total, _, slot_total = resid0.shape
    row_ids = jnp.arange(grid_rows, dtype=jnp.int32)[:, None, None, None]
    col_ids = jnp.arange(grid_cols, dtype=jnp.int32)[None, :, None, None]
    valid = (jnp.arange(slot_total, dtype=jnp.int32)[None, None, None, :] < obs_count[..., None]).astype(jnp.float32)
    cam_index = (((row_ids * grid_cols + col_ids) * CB_DEV + tile_camera[..., None]) * CAMB + obs_camera).astype(jnp.int32).reshape(-1)
    slot_ids = tile_points[..., None]
    step_x = slot_ids // (3 * PB_DEV)
    step_y = (slot_ids // PB_DEV) % 3
    block_ids = slot_ids % PB_DEV
    point_index = ((((row_ids + step_x - 1) * grid_cols + col_ids + step_y - 1) * PB_DEV + block_ids) * PTS + obs_point).astype(jnp.int32).reshape(-1)
    flat_valid = valid.reshape(-1)
    camera_jac = jnp.moveaxis(jac_cam.reshape(grid_rows, grid_cols, tile_total, 2, CPAR, slot_total), 5, 3).reshape(-1, 2, CPAR) * flat_valid[:, None, None]
    point_jac = jnp.moveaxis(jac_pt.reshape(grid_rows, grid_cols, tile_total, 2, 3, slot_total), 5, 3).reshape(-1, 2, 3) * flat_valid[:, None, None]
    resid = jnp.moveaxis(resid0, 4, 3).reshape(-1, 2) * flat_valid[:, None]
    camera_now = jnp.moveaxis(cam_params, 4, 3).reshape(-1, CPAR)
    point_now = jnp.moveaxis(pt_params, 4, 3).reshape(-1, 3)
    start = jnp.moveaxis(cg_start, 4, 3).reshape(-1, CPAR)
    cam_total = camera_now.shape[0]
    point_total = point_now.shape[0]

    def take_cams(vector):
        return vector[cam_index]

    def put_cams(values):
        return jnp.zeros((cam_total, values.shape[1]), jnp.float32).at[cam_index].add(values)

    def take_points(vector):
        return vector[point_index]

    def put_points(values):
        return jnp.zeros((point_total, values.shape[1]), jnp.float32).at[point_index].add(values)

    def apply_cam(values):
        return jnp.sum(camera_jac * values[:, None, :], axis=2)

    def to_points(moved):
        return jnp.sum(point_jac * moved[:, :, None], axis=1)

    cam_diag = put_cams(jnp.sum(camera_jac * camera_jac, axis=1))
    hess_terms = jnp.stack([jnp.sum(point_jac[:, :, row_pos] * point_jac[:, :, col_pos], axis=1) for row_pos, col_pos in hess_pairs], axis=1)
    point_hess = put_points(hess_terms)
    hess_cols = tuple(point_hess[:, column] for column in range(6))

    def reduced(moved, damping):
        owned = put_points(to_points(moved))
        solved = damped_inverse_apply(hess_cols, (owned[:, 0], owned[:, 1], owned[:, 2]), damping)
        nearby = take_points(jnp.stack(solved, axis=1))
        back = moved - jnp.sum(point_jac * nearby[:, None, :], axis=2)
        return put_cams(jnp.sum(camera_jac * back[:, :, None], axis=1))

    costs_list = [0.5 * jnp.sum(resid * resid)]
    for lm_step in range(LM_STEPS):
        damping = damping_first * damping_ratio ** lm_step
        cam_damp = damping * (cam_diag + 1.0)
        precond = cam_diag + cam_damp
        moved = resid + apply_cam(take_cams(start))
        cg_resid = -reduced(moved, damping) - cam_damp * start
        scaled = cg_resid / precond
        direction = scaled
        resid_dot = jnp.sum(cg_resid * scaled)
        update = start
        for cg_turn in range(CG_ITERS):
            curved = reduced(apply_cam(take_cams(direction)), damping) + cam_damp * direction
            step_size = resid_dot / jnp.sum(direction * curved)
            update = update + step_size * direction
            cg_resid = cg_resid - step_size * curved
            if cg_turn + 1 < CG_ITERS:
                scaled = cg_resid / precond
                fresh = jnp.sum(cg_resid * scaled)
                direction = scaled + (fresh / resid_dot) * direction
                resid_dot = fresh
        moved = resid + apply_cam(take_cams(update))
        owned = put_points(to_points(moved))
        solved = damped_inverse_apply(hess_cols, (owned[:, 0], owned[:, 1], owned[:, 2]), damping)
        point_step = -jnp.stack(solved, axis=1)
        resid = moved + jnp.sum(point_jac * take_points(point_step)[:, None, :], axis=2)
        camera_now = camera_now + update
        point_now = point_now + point_step
        start = update
        costs_list.append(0.5 * jnp.sum(resid * resid))
    cam_out = jnp.moveaxis(camera_now.reshape(grid_rows, grid_cols, CB_DEV, CAMB, CPAR), 4, 3)
    pt_out = jnp.moveaxis(point_now.reshape(grid_rows, grid_cols, PB_DEV, PTS, 3), 4, 3)
    resid_out = jnp.moveaxis(resid.reshape(grid_rows, grid_cols, tile_total, slot_total, 2), 4, 3)
    return cam_out, pt_out, resid_out, jnp.stack(costs_list)
```

```python
import jax
import jax.numpy as jnp
from jax import lax
from jax.experimental import pallas as pl
from jax.experimental.pallas import tpu as pltpu
from jax.sharding import PartitionSpec as P

MESH = pl.DeviceIdType.MESH
CPAR = 9
NBLK = 16
LANES = 128
TILES = 128
SLOTS = 9 * NBLK
GX = 8
GY = 16
STEPS = (1, 2, 4, 8, 16, 32, 64)
LAMBDAS = (1.0, 0.25)
PAIRS = ((0, 0), (0, 1), (0, 2), (1, 1), (1, 2), (2, 2))
OTHERS = (0, 1, 2, 3, 5, 6, 7, 8)
F32 = jnp.float32
BF16 = jnp.bfloat16
GATHER = lax.GatherDimensionNumbers(
    offset_dims=(),
    collapsed_slice_dims=(1,),
    start_index_map=(1,),
    operand_batching_dims=(0,),
    start_indices_batching_dims=(0,),
)


def pick(x, idx):
    return lax.gather(
        x, idx[:, :, None], GATHER, (1, 1), mode=lax.GatherScatterMode.PROMISE_IN_BOUNDS
    )


def lane_ids(rows):
    return lax.broadcasted_iota(jnp.int32, (rows, LANES), 1)


def sort_lanes(key):
    lane = lane_ids(key.shape[0])
    size = 2
    while size <= LANES:
        gap = size // 2
        while gap >= 1:
            other = pick(key, lane ^ gap)
            keep_low = ((lane & gap) == 0) == ((lane & size) == 0)
            key = jnp.where(keep_low, jnp.minimum(key, other), jnp.maximum(key, other))
            gap //= 2
        size *= 2
    return key


def last_at_most(seg, target):
    count = jnp.zeros_like(target)
    for step in (64, 32, 16, 8, 4, 2, 1):
        count = jnp.where(pick(seg, count + (step - 1)) <= target, count + step, count)
    return jnp.where(pick(seg, count) <= target, count + 1, count)


def column(row):
    return jnp.swapaxes(jnp.broadcast_to(row.astype(F32), (LANES, LANES)), 0, 1)


def invert(hess, damping):
    h00 = hess[0] + damping * (hess[0] + 1.0)
    h01, h02 = hess[1], hess[2]
    h11 = hess[3] + damping * (hess[3] + 1.0)
    h12 = hess[4]
    h22 = hess[5] + damping * (hess[5] + 1.0)
    c00 = h11 * h22 - h12 * h12
    c01 = h02 * h12 - h01 * h22
    c02 = h01 * h12 - h02 * h11
    c11 = h00 * h22 - h02 * h02
    c12 = h01 * h02 - h00 * h12
    c22 = h00 * h11 - h01 * h01
    det = h00 * c00 + h01 * c01 + h02 * c02
    return [c / det for c in (c00, c01, c02, c11, c12, c22)]


def apply_inverse(inv, y):
    return [
        inv[0] * y[0] + inv[1] * y[1] + inv[2] * y[2],
        inv[1] * y[0] + inv[3] * y[1] + inv[4] * y[2],
        inv[2] * y[0] + inv[4] * y[1] + inv[5] * y[2],
    ]


def lane_sum(x):
    while x.ndim > 2:
        x = jnp.sum(x, axis=0)
    return jnp.sum(x, axis=0, keepdims=True)


def kernel(
    slot_s,
    jc_h,
    jp_h,
    rs_h,
    obs_cam,
    obs_pt,
    count_r,
    tcam_r,
    tpts_r,
    start_r,
    upd_o,
    step_o,
    res_o,
    cost_o,
    jc,
    jp,
    rs,
    perm,
    endi,
    smask,
    hit_p,
    hit_c,
    pair_m,
    idx_c,
    onehot,
    zbuf,
    table,
    gg,
    bk,
    mv,
    contrib,
    recv_c,
    wsrc,
    recv_s,
    wsrc4,
    recv_s4,
    comb,
    hess_b,
    inv_b,
    ybuf,
    wbuf,
    camvec,
    camacc,
    ar_src,
    ar_mid,
    arx,
    ary,
    in_sem,
    cs_sem,
    cr_sem,
    ss_sem,
    sr_sem,
    s4s_sem,
    s4r_sem,
    axs_sem,
    axr_sem,
    ays_sem,
    ayr_sem,
):
    me_x = lax.axis_index("gx")
    me_y = lax.axis_index("gy")

    def at(dx, dy):
        return (lax.rem(me_x + (dx + GX), GX), lax.rem(me_y + (dy + GY), GY))

    barrier = pltpu.get_barrier_semaphore()
    peers = [(d, 0) for d in range(1, GX)] + [(0, d) for d in range(1, GY)]
    peers += [(-1, -1), (-1, 1), (1, -1), (1, 1)]
    for dx, dy in peers:
        pl.semaphore_signal(barrier, inc=1, device_id=at(dx, dy), device_id_type=MESH)

    copies = [
        pltpu.make_async_copy(rs_h.at[:, 0, :], rs.at[0], in_sem.at[0]),
        pltpu.make_async_copy(rs_h.at[:, 1, :], rs.at[1], in_sem.at[1]),
        pltpu.make_async_copy(jp_h, jp, in_sem.at[2]),
        pltpu.make_async_copy(jc_h, jc, in_sem.at[3]),
    ]
    for copy in copies:
        copy.start()

    lane = lane_ids(TILES)
    tcam = column(tcam_r[...]).astype(jnp.int32)
    parity = tcam & 1
    pair = tcam >> 1
    pair_m[...] = pair
    idx_c[...] = parity * 64 + obs_cam[...]
    for kind in range(2):
        ids = obs_pt[...] if kind == 0 else obs_cam[...]
        key = sort_lanes(ids * LANES + lane)
        perm[kind] = key & (LANES - 1)
        seg = key >> 7
        for i, d in enumerate(STEPS):
            same = (pltpu.roll(seg, d, axis=1) == seg) & (lane >= d)
            smask[kind, i] = jnp.where(same, 1.0, 0.0)
        target = lane if kind == 0 else lane & 63
        count = last_at_most(seg, target)
        last = jnp.maximum(count - 1, 0)
        endi[kind] = last
        found = (count > 0) & (pick(seg, last) == target)
        if kind == 0:
            hit_p[...] = jnp.where(found, 1.0, 0.0)
        else:
            here = found & ((lane >> 6) == parity)
            hit_c[0] = jnp.where(here & (pair == 0), 1.0, 0.0)
            hit_c[1] = jnp.where(here & (pair == 1), 1.0, 0.0)
    slot_row = lax.broadcasted_iota(jnp.int32, (SLOTS, TILES), 0)
    hot = jnp.where(slot_row == tpts_r[...], 1.0, 0.0).astype(BF16)
    for i in range(3):
        onehot[:, i * TILES : (i + 1) * TILES] = hot

    def summed(x, kind):
        x = pick(x, perm[kind])
        for i, d in enumerate(STEPS):
            x = x + pltpu.roll(x, d, axis=1) * smask[kind, i]
        return pick(x, endi[kind])

    def put_points(values, first):
        sums = jnp.concatenate([summed(v, 0) * hit_p[...] for v in values], axis=1)
        high = sums.astype(BF16)
        rest = sums - high.astype(F32)
        mid = rest.astype(BF16)
        low = (rest - mid.astype(F32)).astype(BF16)
        parts = jnp.concatenate([high, mid, low], axis=0)
        out = jnp.dot(onehot[...], parts, preferred_element_type=F32)
        for n in range(9):
            for m in range(3):
                contrib[n, first + m] = out[
                    n * NBLK : (n + 1) * NBLK, m * LANES : (m + 1) * LANES
                ]

    def put_cams(value_at):
        def one(group, carry):
            for j in range(3):
                k = group * 3 + j
                sums = summed(value_at(k), 1)
                top = lane_sum(sums * hit_c[0])
                bottom = lane_sum(sums * hit_c[1])
                camacc[k] = jnp.concatenate([top, bottom], axis=0)
            return carry

        lax.fori_loop(0, 3, one, 0)
        return camacc[...]

    def take_cams(vector, b):
        camvec[...] = vector
        rows = 32

        def one(chunk, carry):
            where = pl.ds(pl.multiple_of(chunk * rows, rows), rows)
            idx = idx_c[where, :]
            second = pair_m[where, :] == 1
            e0 = jnp.zeros((rows, LANES), F32)
            e1 = jnp.zeros((rows, LANES), F32)
            for k in range(CPAR):
                v = camvec[k]
                src = jnp.where(
                    second,
                    jnp.broadcast_to(v[1:2], (rows, LANES)),
                    jnp.broadcast_to(v[0:1], (rows, LANES)),
                )
                got = pick(src, idx)
                e0 = e0 + jc[k, where, :] * got
                e1 = e1 + jc[CPAR + k, where, :] * got
            gg[b, 0, where, :] = e0
            gg[b, 1, where, :] = e1
            return carry

        lax.fori_loop(0, TILES // rows, one, 0)

    def to_points(e0, e1):
        return [jp[m] * e0 + jp[3 + m] * e1 for m in range(3)]

    def collect_start(comps):
        for r, n in enumerate(OTHERS):
            a, b = divmod(n, 3)
            pltpu.make_async_remote_copy(
                src_ref=contrib.at[n, pl.ds(0, comps)],
                dst_ref=recv_c.at[r, pl.ds(0, comps)],
                send_sem=cs_sem.at[r],
                recv_sem=cr_sem.at[r],
                device_id=at(a - 1, b - 1),
                device_id_type=MESH,
            ).start()

    def collect_wait(comps):
        for r, n in enumerate(OTHERS):
            pltpu.make_async_copy(
                contrib.at[n, pl.ds(0, comps)], recv_c.at[r, pl.ds(0, comps)], cr_sem.at[r]
            ).wait()
        for r, n in enumerate(OTHERS):
            pltpu.make_async_copy(
                contrib.at[n, pl.ds(0, comps)], recv_c.at[r, pl.ds(0, comps)], cs_sem.at[r]
            ).wait()
        total = []
        for m in range(comps):
            s = contrib[4, m]
            for r in range(8):
                s = s + recv_c[r, m]
            total.append(s)
        return total

    def spread_start(values, src, dst, send_sem, recv_sem):
        for m, v in enumerate(values):
            src[m] = v
            dst[4, m] = v
        for r, n in enumerate(OTHERS):
            a, b = divmod(n, 3)
            pltpu.make_async_remote_copy(
                src_ref=src,
                dst_ref=dst.at[8 - n],
                send_sem=send_sem.at[r],
                recv_sem=recv_sem.at[r],
                device_id=at(a - 1, b - 1),
                device_id_type=MESH,
            ).start()

    def spread_wait(src, dst, send_sem, recv_sem):
        for r, n in enumerate(OTHERS):
            pltpu.make_async_copy(src, dst.at[8 - n], recv_sem.at[r]).wait()
        for r, n in enumerate(OTHERS):
            pltpu.make_async_copy(src, dst.at[8 - n], send_sem.at[r]).wait()

    def take_points(src):
        def one(chunk, carry):
            for i in range(8):
                t = chunk * 8 + i
                slot = slot_s[t]
                n = slot >> 4
                q = slot & 15
                for m in range(3):
                    table[m, pl.ds(t, 1), :] = src[n, m, pl.ds(q, 1), :]
            return carry

        lax.fori_loop(0, TILES // 8, one, 0)
        return [pick(table[m], obs_pt[...]) for m in range(3)]

    def eliminate(e0, e1, b, src):
        near = take_points(src)
        bk[b, 0] = e0 - (jp[0] * near[0] + jp[1] * near[1] + jp[2] * near[2])
        bk[b, 1] = e1 - (jp[3] * near[0] + jp[4] * near[1] + jp[5] * near[2])
        return put_cams(lambda k: jc[k] * bk[b, 0] + jc[CPAR + k] * bk[b, 1])

    def reduce_x_start(a, rows):
        ar_src[a] = jnp.concatenate(rows + [jnp.zeros((8 - len(rows), LANES), F32)], axis=0)
        arx[a, me_x] = ar_src[a]
        for d in range(1, GX):
            pltpu.make_async_remote_copy(
                src_ref=ar_src.at[a],
                dst_ref=arx.at[a, me_x],
                send_sem=axs_sem.at[a, d],
                recv_sem=axr_sem.at[a, d],
                device_id=at(d, 0),
                device_id_type=MESH,
            ).start()

    def reduce_y_start(a):
        for d in range(1, GX):
            pltpu.make_async_copy(ar_src.at[a], arx.at[a, 0], axr_sem.at[a, d]).wait()
        ar_mid[a] = jnp.sum(arx[a], axis=0)
        ary[a, me_y] = ar_mid[a]
        for d in range(1, GY):
            pltpu.make_async_remote_copy(
                src_ref=ar_mid.at[a],
                dst_ref=ary.at[a, me_y],
                send_sem=ays_sem.at[a, d],
                recv_sem=ayr_sem.at[a, d],
                device_id=at(0, d),
                device_id_type=MESH,
            ).start()

    def reduce_wait(a):
        for d in range(1, GY):
            pltpu.make_async_copy(ar_mid.at[a], ary.at[a, 0], ayr_sem.at[a, d]).wait()
        total = jnp.sum(jnp.sum(ary[a], axis=0), axis=1, keepdims=True)
        wide = jnp.broadcast_to(total, (8, LANES))
        return [wide[i : i + 1] for i in range(8)]

    def reduce_drain(a):
        for d in range(1, GX):
            pltpu.make_async_copy(ar_src.at[a], arx.at[a, 0], axs_sem.at[a, d]).wait()
        for d in range(1, GY):
            pltpu.make_async_copy(ar_mid.at[a], ary.at[a, 0], ays_sem.at[a, d]).wait()

    valid = jnp.where(lane < column(count_r[...]).astype(jnp.int32), 1.0, 0.0)
    for copy in copies:
        copy.wait()
    for k in range(2):
        rs[k] = rs[k] * valid
    for k in range(6):
        jp[k] = jp[k] * valid
    for k in range(18):
        jc[k] = jc[k] * valid

    start = start_r[...]
    take_cams(start, 0)

    for c, (i, j) in enumerate(PAIRS):
        zbuf[c] = jp[i] * jp[j] + jp[3 + i] * jp[3 + j]
    for m, v in enumerate(to_points(rs[0], rs[1])):
        zbuf[6 + m] = v
    for m, v in enumerate(to_points(gg[0, 0], gg[0, 1])):
        zbuf[9 + m] = v

    def first_points(group, carry):
        put_points([zbuf[group * 3 + m] for m in range(3)], group * 3)
        return carry

    lax.fori_loop(0, 4, first_points, 0)
    pl.semaphore_wait(barrier, len(peers))
    collect_start(12)
    diag = put_cams(lambda k: jc[k] * jc[k] + jc[CPAR + k] * jc[CPAR + k])
    cost_row = lane_sum(rs[...] * rs[...])
    owned = collect_wait(12)
    for c in range(6):
        hess_b[c] = owned[c]
    y_start = owned[9:12]
    ybuf[0] = jnp.stack([owned[6 + m] + owned[9 + m] for m in range(3)])

    update = start
    upd_sum = jnp.zeros_like(start)
    step_sum = jnp.zeros((3, NBLK, LANES), F32)
    for k in range(2):
        mv[k] = rs[k] + gg[0, k]

    for step in range(2):
        damping = LAMBDAS[step]
        last = step == 1
        cam_damp = damping * (diag + 1.0)
        precond = diag + cam_damp
        if step == 0:
            inv = invert([hess_b[c] for c in range(6)], damping)
            for c in range(6):
                inv_b[c] = inv[c]
            w0 = apply_inverse(inv, [ybuf[0, m] for m in range(3)])
            wbuf[0] = jnp.stack(w0)
            spread_start(w0, wsrc, recv_s, ss_sem, sr_sem)
            spread_wait(wsrc, recv_s, ss_sem, sr_sem)
            sums = eliminate(mv[0], mv[1], 0, recv_s)
        else:
            sums = eliminate(mv[0], mv[1], 0, comb)
        r0 = -sums - cam_damp * update
        z0 = r0 / precond

        def operator(vector, b):
            take_cams(vector, b)
            put_points(to_points(gg[b, 0], gg[b, 1]), 0)
            collect_start(3)

        def operator_finish(vector, b):
            y = collect_wait(3)
            ybuf[b] = jnp.stack(y)
            w = apply_inverse([inv_b[c] for c in range(6)], y)
            wbuf[b] = jnp.stack(w)
            spread_start(w, wsrc, recv_s, ss_sem, sr_sem)

        def operator_end(vector, b):
            spread_wait(wsrc, recv_s, ss_sem, sr_sem)
            return eliminate(gg[b, 0], gg[b, 1], b, recv_s) + cam_damp * vector

        operator(z0, 1)
        operator_finish(z0, 1)
        c0 = operator_end(z0, 1)
        u = c0 / precond
        first = 2 * step
        reduce_x_start(
            first, [lane_sum(r0 * z0), lane_sum(z0 * c0), lane_sum(c0 * u), cost_row]
        )
        operator(u, 2)
        reduce_y_start(first)
        operator_finish(u, 2)
        q = operator_end(u, 2)
        dots = reduce_wait(first)
        resid_dot, curve, square = dots[0], dots[1], dots[2]
        cost_o[pl.ds(step, 1), :] = 0.5 * dots[3]
        alpha = resid_dot / curve
        beta = (resid_dot - 2.0 * alpha * curve + alpha * alpha * square) / resid_dot
        r1 = r0 - alpha * c0
        z1 = r1 / precond
        d1 = z1 + beta * z0
        sd1 = (1.0 + beta) * c0 - alpha * q
        rows = [lane_sum(r1 * z1), lane_sum(d1 * sd1)]
        if last:
            near = bk[0] + alpha * bk[1]
            turn = (1.0 + beta) * bk[1] - alpha * bk[2]
            rows += [lane_sum(near * near), lane_sum(near * turn), lane_sum(turn * turn)]
        second = first + 1
        reduce_x_start(second, rows)
        if not last:
            hess = [hess_b[c] for c in range(6)]
            inv = invert(hess, LAMBDAS[1])
            for c in range(6):
                inv_b[c] = inv[c]
            scale = [damping * (hess[c] + 1.0) for c in (0, 3, 5)]
            held = []
            for b in range(3):
                held.append([scale[m] * wbuf[b, m] + ybuf[b, m] for m in range(3)])
            base = [
                scale[m] * wbuf[0, m] + y_start[m] + alpha * held[1][m] for m in range(3)
            ]
            move = [(1.0 + beta) * held[1][m] - alpha * held[2][m] for m in range(3)]
            spread_start(apply_inverse(inv, base) + apply_inverse(inv, move), wsrc4, recv_s4, s4s_sem, s4r_sem)
        reduce_y_start(second)
        if not last:
            spread_wait(wsrc4, recv_s4, s4s_sem, s4r_sem)
        dots = reduce_wait(second)
        alpha1 = dots[0] / dots[1]
        ca = alpha + alpha1 * (1.0 + beta)
        cb = -(alpha1 * alpha)
        update = update + alpha * z0 + alpha1 * d1
        upd_sum = upd_sum + update
        step_sum = step_sum - (wbuf[0] + ca * wbuf[1] + cb * wbuf[2])
        if not last:
            for r in range(2):
                res = bk[0, r] + ca * bk[1, r] + cb * bk[2, r]
                rs[r] = res
                mv[r] = res + (gg[0, r] + ca * gg[1, r] + cb * gg[2, r])
            cost_row = lane_sum(rs[...] * rs[...])
            for n in range(9):
                for m in range(3):
                    comb[n, m] = recv_s4[n, m] + alpha1 * recv_s4[n, 3 + m]
            wbuf[0] = wsrc4[0:3] + alpha1 * wsrc4[3:6]
        else:
            for r in range(2):
                res_o[r] = bk[0, r] + ca * bk[1, r] + cb * bk[2, r]
            cost_o[pl.ds(2, 1), :] = 0.5 * (
                dots[2] + 2.0 * alpha1 * dots[3] + alpha1 * alpha1 * dots[4]
            )
    upd_o[...] = upd_sum
    step_o[...] = step_sum
    cost_o[pl.ds(3, 5), :] = jnp.zeros((5, LANES), F32)
    for a in range(4):
        reduce_drain(a)


def body(
    jac_cam,
    jac_pt,
    resid0,
    obs_count,
    tile_camera,
    tile_points,
    obs_camera,
    obs_point,
    cam_params,
    pt_params,
    cg_start,
):
    start = jnp.transpose(
        cg_start[0, 0].reshape(2, 2, CPAR, 64), (2, 0, 1, 3)
    ).reshape(CPAR, 2, LANES)
    vmem = pl.BlockSpec(memory_space=pltpu.VMEM)
    hbm = pl.BlockSpec(memory_space=pl.ANY)
    big = (TILES, LANES)
    blk = (NBLK, LANES)
    dma = pltpu.SemaphoreType.DMA
    upd, steps, res, costs = pl.pallas_call(
        kernel,
        out_shape=[
            jax.ShapeDtypeStruct((CPAR, 2, LANES), F32),
            jax.ShapeDtypeStruct((3,) + blk, F32),
            jax.ShapeDtypeStruct((2,) + big, F32),
            jax.ShapeDtypeStruct((8, LANES), F32),
        ],
        in_specs=[pl.BlockSpec(memory_space=pltpu.SMEM)] + [hbm] * 3 + [vmem] * 6,
        out_specs=[vmem] * 4,
        scratch_shapes=[
            pltpu.VMEM((18,) + big, F32),
            pltpu.VMEM((6,) + big, F32),
            pltpu.VMEM((2,) + big, F32),
            pltpu.VMEM((2,) + big, jnp.int32),
            pltpu.VMEM((2,) + big, jnp.int32),
            pltpu.VMEM((2, 7) + big, F32),
            pltpu.VMEM(big, F32),
            pltpu.VMEM((2,) + big, F32),
            pltpu.VMEM(big, jnp.int32),
            pltpu.VMEM(big, jnp.int32),
            pltpu.VMEM((SLOTS, 3 * TILES), BF16),
            pltpu.VMEM((12,) + big, F32),
            pltpu.VMEM((3,) + big, F32),
            pltpu.VMEM((3, 2) + big, F32),
            pltpu.VMEM((3, 2) + big, F32),
            pltpu.VMEM((2,) + big, F32),
            pltpu.VMEM((9, 12) + blk, F32),
            pltpu.VMEM((8, 12) + blk, F32),
            pltpu.VMEM((3,) + blk, F32),
            pltpu.VMEM((9, 3) + blk, F32),
            pltpu.VMEM((6,) + blk, F32),
            pltpu.VMEM((9, 6) + blk, F32),
            pltpu.VMEM((9, 3) + blk, F32),
            pltpu.VMEM((6,) + blk, F32),
            pltpu.VMEM((6,) + blk, F32),
            pltpu.VMEM((3, 3) + blk, F32),
            pltpu.VMEM((3, 3) + blk, F32),
            pltpu.VMEM((CPAR, 2, LANES), F32),
            pltpu.VMEM((CPAR, 2, LANES), F32),
            pltpu.VMEM((4, 8, LANES), F32),
            pltpu.VMEM((4, 8, LANES), F32),
            pltpu.VMEM((4, GX, 8, LANES), F32),
            pltpu.VMEM((4, GY, 8, LANES), F32),
            dma((4,)),
            dma((8,)),
            dma((8,)),
            dma((8,)),
            dma((8,)),
            dma((8,)),
            dma((8,)),
            dma((4, GX)),
            dma((4, GX)),
            dma((4, GY)),
            dma((4, GY)),
        ],
        compiler_params=pltpu.CompilerParams(
            collective_id=0, has_side_effects=True, vmem_limit_bytes=48 * 1024 * 1024
        ),
    )(
        tile_points[0, 0],
        jnp.transpose(jac_cam[0, 0], (1, 0, 2)),
        jnp.transpose(jac_pt[0, 0], (1, 0, 2)),
        resid0[0, 0],
        obs_camera[0, 0],
        obs_point[0, 0],
        obs_count[0],
        tile_camera[0],
        tile_points[0],
        start,
    )
    moved = jnp.transpose(upd.reshape(CPAR, 2, 2, 64), (1, 2, 0, 3)).reshape(4, CPAR, 64)
    cam_out = cam_params + moved[None, None]
    pt_out = pt_params + jnp.transpose(steps, (1, 0, 2))[None, None]
    res_out = jnp.transpose(res, (1, 0, 2))[None, None]
    return cam_out, pt_out, res_out, costs[:3, 0]


def solution(mesh):
    wide = P("gx", "gy", None, None, None)
    in_specs = (
        wide,
        wide,
        wide,
        P("gx", "gy", None),
        P("gx", "gy", None),
        P("gx", "gy", None),
        P("gx", "gy", None, None),
        P("gx", "gy", None, None),
        wide,
        wide,
        wide,
    )
    out_specs = (wide, wide, wide, P())
    return jax.shard_map(body, mesh=mesh, in_specs=in_specs, out_specs=out_specs, check_vma=False)
```

```python
import jax
import jax.numpy as jnp
from jax import lax
from jax.experimental import pallas as pl
from jax.experimental.pallas import tpu as pltpu
from jax.sharding import PartitionSpec as P

MESH = pl.DeviceIdType.MESH
CPAR = 9
NBLK = 16
LANES = 128
TILES = 128
SLOTS = 9 * NBLK
GX = 8
GY = 16
STEPS = (1, 2, 4, 8, 16, 32, 64)
LAMBDAS = (1.0, 0.25)
PAIRS = ((0, 0), (0, 1), (0, 2), (1, 1), (1, 2), (2, 2))
OTHERS = (0, 1, 2, 3, 5, 6, 7, 8)
ORDER = tuple((OTHERS.index(n), n) for n in (0, 2, 6, 8, 3, 5, 1, 7))
F32 = jnp.float32
BF16 = jnp.bfloat16
GATHER = lax.GatherDimensionNumbers(
    offset_dims=(),
    collapsed_slice_dims=(1,),
    start_index_map=(1,),
    operand_batching_dims=(0,),
    start_indices_batching_dims=(0,),
)


def pick(x, idx):
    return lax.gather(
        x, idx[:, :, None], GATHER, (1, 1), mode=lax.GatherScatterMode.PROMISE_IN_BOUNDS
    )


def lane_ids(rows):
    return lax.broadcasted_iota(jnp.int32, (rows, LANES), 1)


def sort_lanes(key):
    lane = lane_ids(key.shape[0])
    size = 2
    while size <= LANES:
        gap = size // 2
        while gap >= 1:
            other = pick(key, lane ^ gap)
            keep_low = ((lane & gap) == 0) == ((lane & size) == 0)
            key = jnp.where(keep_low, jnp.minimum(key, other), jnp.maximum(key, other))
            gap //= 2
        size *= 2
    return key


def last_at_most(seg, target):
    count = jnp.zeros_like(target)
    for step in (64, 32, 16, 8, 4, 2, 1):
        count = jnp.where(pick(seg, count + (step - 1)) <= target, count + step, count)
    return jnp.where(pick(seg, count) <= target, count + 1, count)


def column(row):
    return jnp.swapaxes(jnp.broadcast_to(row.astype(F32), (LANES, LANES)), 0, 1)


def invert(hess, damping):
    h00 = hess[0] + damping * (hess[0] + 1.0)
    h01, h02 = hess[1], hess[2]
    h11 = hess[3] + damping * (hess[3] + 1.0)
    h12 = hess[4]
    h22 = hess[5] + damping * (hess[5] + 1.0)
    c00 = h11 * h22 - h12 * h12
    c01 = h02 * h12 - h01 * h22
    c02 = h01 * h12 - h02 * h11
    c11 = h00 * h22 - h02 * h02
    c12 = h01 * h02 - h00 * h12
    c22 = h00 * h11 - h01 * h01
    det = h00 * c00 + h01 * c01 + h02 * c02
    return [c / det for c in (c00, c01, c02, c11, c12, c22)]


def apply_inverse(inv, y):
    return [
        inv[0] * y[0] + inv[1] * y[1] + inv[2] * y[2],
        inv[1] * y[0] + inv[3] * y[1] + inv[4] * y[2],
        inv[2] * y[0] + inv[4] * y[1] + inv[5] * y[2],
    ]


def lane_sum(x):
    while x.ndim > 2:
        x = jnp.sum(x, axis=0)
    return jnp.sum(x, axis=0, keepdims=True)


def kernel(
    slot_s,
    jc_h,
    jp_h,
    rs_h,
    obs_cam,
    obs_pt,
    count_r,
    tcam_r,
    tpts_r,
    start_r,
    upd_o,
    step_o,
    res_o,
    cost_o,
    jc,
    jp,
    rs,
    perm,
    endi,
    smask,
    hit_p,
    hit_c,
    pair_m,
    idx_c,
    onehot,
    zbuf,
    table,
    gg,
    bk,
    mv,
    contrib,
    recv_c,
    wsrc,
    recv_s,
    wsrc_w,
    recv_w,
    hess_b,
    inv_b,
    ybuf,
    wbuf,
    camvec,
    camacc,
    ar_src,
    arx,
    in_sem,
    cs_sem,
    cr_sem,
    ss_sem,
    sr_sem,
    ws_sem,
    wr_sem,
    as_sem,
    ar_sem,
):
    me_x = lax.axis_index("gx")
    me_y = lax.axis_index("gy")

    def at(dx, dy):
        return (lax.rem(me_x + (dx + GX), GX), lax.rem(me_y + (dy + GY), GY))

    me = me_x * GY + me_y
    here = {}
    for n in OTHERS:
        a, b = divmod(n, 3)
        x, y = me_x + (a - 1), me_y + (b - 1)
        here[n] = (x >= 0) & (x < GX) & (y >= 0) & (y < GY)

    def to_all(act):
        def row(j, carry):
            dy = lax.rem(j + 5, GY - 1) + 1
            for dx in (4, 3, 5, 2, 6, 1, 7, 0):
                act(dx, dy)
            return carry

        lax.fori_loop(0, GY - 1, row, 0)
        for dx in (4, 3, 5, 2, 6, 1, 7):
            act(dx, 0)

    for r, n in enumerate(OTHERS):

        @pl.when(jnp.logical_not(here[n]))
        def _(r=r, n=n):
            recv_c[r] = jnp.zeros_like(recv_c[r])
            recv_s[n] = jnp.zeros_like(recv_s[n])
            recv_w[n] = jnp.zeros_like(recv_w[n])

    barrier = pltpu.get_barrier_semaphore()
    to_all(
        lambda dx, dy: pl.semaphore_signal(
            barrier, inc=1, device_id=at(dx, dy), device_id_type=MESH
        )
    )

    copies = [
        pltpu.make_async_copy(rs_h.at[:, 0, :], rs.at[0], in_sem.at[0]),
        pltpu.make_async_copy(rs_h.at[:, 1, :], rs.at[1], in_sem.at[1]),
        pltpu.make_async_copy(jp_h, jp, in_sem.at[2]),
        pltpu.make_async_copy(jc_h, jc, in_sem.at[3]),
    ]
    for copy in copies:
        copy.start()

    lane = lane_ids(TILES)
    tcam = column(tcam_r[...]).astype(jnp.int32)
    parity = tcam & 1
    pair = tcam >> 1
    pair_m[...] = pair
    idx_c[...] = parity * 64 + obs_cam[...]

    def order(kind):
        ids = obs_pt[...] if kind == 0 else obs_cam[...]
        key = sort_lanes(ids * LANES + lane)
        perm[kind] = key & (LANES - 1)
        seg = key >> 7
        for i, d in enumerate(STEPS):
            same = (pltpu.roll(seg, d, axis=1) == seg) & (lane >= d)
            smask[kind, i] = jnp.where(same, 1.0, 0.0)
        target = lane if kind == 0 else lane & 63
        count = last_at_most(seg, target)
        last = jnp.maximum(count - 1, 0)
        endi[kind] = last
        found = (count > 0) & (pick(seg, last) == target)
        if kind == 0:
            hit_p[...] = jnp.where(found, 1.0, 0.0)
        else:
            mine = found & ((lane >> 6) == parity)
            hit_c[0] = jnp.where(mine & (pair == 0), 1.0, 0.0)
            hit_c[1] = jnp.where(mine & (pair == 1), 1.0, 0.0)

    order(0)
    slot_row = lax.broadcasted_iota(jnp.int32, (SLOTS, TILES), 0)
    hot = jnp.where(slot_row == tpts_r[...], 1.0, 0.0).astype(BF16)
    for i in range(3):
        onehot[:, i * TILES : (i + 1) * TILES] = hot

    def summed(x, kind):
        x = pick(x, perm[kind])
        for i, d in enumerate(STEPS):
            x = x + pltpu.roll(x, d, axis=1) * smask[kind, i]
        return pick(x, endi[kind])

    def put_points(values, first):
        sums = jnp.concatenate([summed(v, 0) * hit_p[...] for v in values], axis=1)
        high = sums.astype(BF16)
        rest = sums - high.astype(F32)
        mid = rest.astype(BF16)
        low = (rest - mid.astype(F32)).astype(BF16)
        parts = jnp.concatenate([high, mid, low], axis=0)
        out = jnp.dot(onehot[...], parts, preferred_element_type=F32)
        for n in range(9):
            for m in range(3):
                contrib[n, first + m] = out[
                    n * NBLK : (n + 1) * NBLK, m * LANES : (m + 1) * LANES
                ]

    def put_cams(value_at):
        def one(group, carry):
            for j in range(3):
                k = group * 3 + j
                sums = summed(value_at(k), 1)
                top = lane_sum(sums * hit_c[0])
                bottom = lane_sum(sums * hit_c[1])
                camacc[k] = jnp.concatenate([top, bottom], axis=0)
            return carry

        lax.fori_loop(0, 3, one, 0)
        return camacc[...]

    def take_cams(vector, b):
        camvec[...] = vector
        rows = 32

        def one(chunk, carry):
            where = pl.ds(pl.multiple_of(chunk * rows, rows), rows)
            idx = idx_c[where, :]
            second = pair_m[where, :] == 1
            e0 = jnp.zeros((rows, LANES), F32)
            e1 = jnp.zeros((rows, LANES), F32)
            for k in range(CPAR):
                v = camvec[k]
                src = jnp.where(
                    second,
                    jnp.broadcast_to(v[1:2], (rows, LANES)),
                    jnp.broadcast_to(v[0:1], (rows, LANES)),
                )
                got = pick(src, idx)
                e0 = e0 + jc[k, where, :] * got
                e1 = e1 + jc[CPAR + k, where, :] * got
            gg[b, 0, where, :] = e0
            gg[b, 1, where, :] = e1
            return carry

        lax.fori_loop(0, TILES // rows, one, 0)

    def to_points(e0, e1):
        return [jp[m] * e0 + jp[3 + m] * e1 for m in range(3)]

    def collect_start(comps):
        for r, n in ORDER:
            a, b = divmod(n, 3)

            @pl.when(here[n])
            def _(r=r, n=n, a=a, b=b):
                pltpu.make_async_remote_copy(
                    src_ref=contrib.at[n, pl.ds(0, comps)],
                    dst_ref=recv_c.at[r, pl.ds(0, comps)],
                    send_sem=cs_sem.at[r],
                    recv_sem=cr_sem.at[r],
                    device_id=at(a - 1, b - 1),
                    device_id_type=MESH,
                ).start()

    def collect_wait(comps):
        for sem, flip in ((cr_sem, True), (cs_sem, False)):
            for r, n in enumerate(OTHERS):

                @pl.when(here[8 - n] if flip else here[n])
                def _(r=r, n=n, sem=sem):
                    pltpu.make_async_copy(
                        contrib.at[n, pl.ds(0, comps)], recv_c.at[r, pl.ds(0, comps)], sem.at[r]
                    ).wait()

        total = []
        for m in range(comps):
            s = contrib[4, m]
            for r in range(8):
                s = s + recv_c[r, m]
            total.append(s)
        return total

    def spread_start(values, src, dst, send_sem, recv_sem):
        for m, v in enumerate(values):
            src[m] = v
            dst[4, m] = v
        for r, n in ORDER:
            a, b = divmod(n, 3)

            @pl.when(here[n])
            def _(r=r, n=n, a=a, b=b):
                pltpu.make_async_remote_copy(
                    src_ref=src,
                    dst_ref=dst.at[8 - n],
                    send_sem=send_sem.at[r],
                    recv_sem=recv_sem.at[r],
                    device_id=at(a - 1, b - 1),
                    device_id_type=MESH,
                ).start()

    def spread_wait(src, dst, send_sem, recv_sem):
        for sem, flip in ((recv_sem, True), (send_sem, False)):
            for r, n in enumerate(OTHERS):

                @pl.when(here[8 - n] if flip else here[n])
                def _(r=r, n=n, sem=sem):
                    pltpu.make_async_copy(src, dst.at[8 - n], sem.at[r]).wait()

    def take_points(src, first=0):
        def one(chunk, carry):
            for i in range(8):
                t = chunk * 8 + i
                slot = slot_s[t]
                n = slot >> 4
                q = slot & 15
                for m in range(3):
                    table[m, pl.ds(t, 1), :] = src[n, first + m, pl.ds(q, 1), :]
            return carry

        lax.fori_loop(0, TILES // 8, one, 0)
        return [pick(table[m], obs_pt[...]) for m in range(3)]

    def eliminate(e0, e1, near, b):
        bk[b, 0] = e0 - (jp[0] * near[0] + jp[1] * near[1] + jp[2] * near[2])
        bk[b, 1] = e1 - (jp[3] * near[0] + jp[4] * near[1] + jp[5] * near[2])

    def back_to_cams(b):
        return put_cams(lambda k: jc[k] * bk[b, 0] + jc[CPAR + k] * bk[b, 1])

    def total_start(a, rows):
        held = jnp.concatenate(rows + [jnp.zeros((8 - len(rows), LANES), F32)], axis=0)
        sums = jnp.sum(held, axis=1, keepdims=True)
        lane8 = lane_ids(8)
        own = lax.broadcasted_iota(jnp.int32, (8, LANES), 0)
        row = jnp.sum(jnp.where(lane8 == own, sums, 0.0), axis=0, keepdims=True)
        ar_src[a] = row
        arx[a, pl.ds(me, 1), :] = row

        def send(dx, dy):
            pltpu.make_async_remote_copy(
                src_ref=ar_src.at[a],
                dst_ref=arx.at[a, pl.ds(me, 1)],
                send_sem=as_sem.at[a],
                recv_sem=ar_sem.at[a],
                device_id=at(dx, dy),
                device_id_type=MESH,
            ).start()

        to_all(send)

    def total_wait(a):
        pltpu.make_async_copy(
            arx.at[a, pl.ds(0, 127)], arx.at[a, pl.ds(0, 127)], ar_sem.at[a]
        ).wait()
        row = jnp.sum(arx[a], axis=0, keepdims=True)
        lane1 = lane_ids(1)
        return [
            jnp.sum(jnp.where(lane1 == i, row, 0.0), axis=1, keepdims=True) for i in range(8)
        ]

    def total_drain(a):
        pltpu.make_async_copy(
            arx.at[a, pl.ds(0, 127)], arx.at[a, pl.ds(0, 127)], as_sem.at[a]
        ).wait()

    valid = jnp.where(lane < column(count_r[...]).astype(jnp.int32), 1.0, 0.0)
    for copy in copies:
        copy.wait()
    for k in range(2):
        rs[k] = rs[k] * valid
    for k in range(6):
        jp[k] = jp[k] * valid
    for k in range(18):
        jc[k] = jc[k] * valid

    start = start_r[...]
    take_cams(start, 0)

    for c, (i, j) in enumerate(PAIRS):
        zbuf[c] = jp[i] * jp[j] + jp[3 + i] * jp[3 + j]
    for m, v in enumerate(to_points(rs[0], rs[1])):
        zbuf[6 + m] = v
    for m, v in enumerate(to_points(gg[0, 0], gg[0, 1])):
        zbuf[9 + m] = v

    def first_points(group, carry):
        put_points([zbuf[group * 3 + m] for m in range(3)], group * 3)
        return carry

    lax.fori_loop(0, 4, first_points, 0)
    pl.semaphore_wait(barrier, GX * GY - 1)
    collect_start(12)
    order(1)
    diag = put_cams(lambda k: jc[k] * jc[k] + jc[CPAR + k] * jc[CPAR + k])
    cost_row = lane_sum(rs[...] * rs[...])
    owned = collect_wait(12)
    for c in range(6):
        hess_b[c] = owned[c]
    y_start = owned[9:12]
    ybuf[0] = jnp.stack([owned[6 + m] + owned[9 + m] for m in range(3)])

    update = start
    upd_sum = jnp.zeros_like(start)
    step_sum = jnp.zeros((3, NBLK, LANES), F32)
    for k in range(2):
        mv[k] = rs[k] + gg[0, k]

    def weighted(w):
        h = [hess_b[c] for c in range(6)]
        return [
            h[0] * w[0] + h[1] * w[1] + h[2] * w[2],
            h[1] * w[0] + h[3] * w[1] + h[4] * w[2],
            h[2] * w[0] + h[4] * w[1] + h[5] * w[2],
        ]

    def inner(u, v):
        return lane_sum(u[0] * v[0] + u[1] * v[1] + u[2] * v[2])

    def three(buf, b):
        return [buf[b, m] for m in range(3)]

    def mix(p, u, q, v):
        return [p * u[m] + q * v[m] for m in range(3)]

    inv = invert([hess_b[c] for c in range(6)], LAMBDAS[0])
    for c in range(6):
        inv_b[c] = inv[c]
    w0 = apply_inverse(inv, three(ybuf, 0))
    wbuf[0] = jnp.stack(w0)
    spread_start(w0, wsrc, recv_s, ss_sem, sr_sem)
    spread_wait(wsrc, recv_s, ss_sem, sr_sem)
    near = take_points(recv_s)

    for step in range(2):
        damping = LAMBDAS[step]
        last = step == 1
        cam_damp = damping * (diag + 1.0)
        precond = diag + cam_damp
        eliminate(mv[0], mv[1], near, 0)
        r0 = -back_to_cams(0) - cam_damp * update
        z0 = r0 / precond

        take_cams(z0, 1)
        put_points(to_points(gg[1, 0], gg[1, 1]), 0)
        collect_start(3)
        y = collect_wait(3)
        ybuf[1] = jnp.stack(y)
        w = apply_inverse([inv_b[c] for c in range(6)], y)
        wbuf[1] = jnp.stack(w)
        spread_start(w, wsrc, recv_s, ss_sem, sr_sem)
        spread_wait(wsrc, recv_s, ss_sem, sr_sem)
        near = take_points(recv_s)
        eliminate(gg[1, 0], gg[1, 1], near, 1)
        c0 = back_to_cams(1) + cam_damp * z0
        u = c0 / precond
        first = 2 * step
        total_start(first, [lane_sum(r0 * z0), lane_sum(z0 * c0), lane_sum(c0 * u), cost_row])

        take_cams(u, 2)
        put_points(to_points(gg[2, 0], gg[2, 1]), 0)
        collect_start(3)
        y = collect_wait(3)
        ybuf[2] = jnp.stack(y)
        w = apply_inverse([inv_b[c] for c in range(6)], y)
        wbuf[2] = jnp.stack(w)

        dots = total_wait(first)
        resid_dot, curve, square = dots[0], dots[1], dots[2]
        cost_o[pl.ds(step, 1), :] = jnp.broadcast_to(0.5 * dots[3], (1, LANES))
        alpha = resid_dot / curve
        beta = (resid_dot - 2.0 * alpha * curve + alpha * alpha * square) / resid_dot
        more = 1.0 + beta
        z1 = (r0 - alpha * c0) / precond
        d1 = z1 + beta * z0
        turn = [more * gg[1, r] - alpha * gg[2, r] for r in range(2)]
        y_turn = mix(more, three(ybuf, 1), -alpha, three(ybuf, 2))
        w_turn = mix(more, three(wbuf, 1), -alpha, three(wbuf, 2))
        turn_sq = lane_sum(turn[0] * turn[0] + turn[1] * turn[1])
        yw = inner(y_turn, w_turn)
        rows = [
            lane_sum((r0 - alpha * c0) * z1),
            turn_sq - yw + lane_sum(cam_damp * (d1 * d1)),
        ]
        if last:
            base = [mv[r] + alpha * gg[1, r] for r in range(2)]
            y_base = mix(1.0, three(ybuf, 0), alpha, three(ybuf, 1))
            w_base = mix(1.0, three(wbuf, 0), alpha, three(wbuf, 1))
            hw_base = weighted(w_base)
            hw_turn = weighted(w_turn)
            rows += [
                lane_sum(base[0] * base[0] + base[1] * base[1])
                - 2.0 * inner(y_base, w_base)
                + inner(w_base, hw_base),
                lane_sum(base[0] * turn[0] + base[1] * turn[1])
                - inner(y_base, w_turn)
                - inner(y_turn, w_base)
                + inner(w_base, hw_turn),
                turn_sq - 2.0 * yw + inner(w_turn, hw_turn),
            ]
        second = first + 1
        total_start(second, rows)
        if not last:
            hess = [hess_b[c] for c in range(6)]
            inv = invert(hess, LAMBDAS[1])
            for c in range(6):
                inv_b[c] = inv[c]
            scale = [damping * (hess[c] + 1.0) for c in (0, 3, 5)]
            held = []
            for b in range(3):
                held.append([scale[m] * wbuf[b, m] + ybuf[b, m] for m in range(3)])
            y_fix = [
                scale[m] * wbuf[0, m] + y_start[m] + alpha * held[1][m] for m in range(3)
            ]
            y_move = mix(more, held[1], -alpha, held[2])
            w_fix = apply_inverse(inv, y_fix)
            w_move = apply_inverse(inv, y_move)
            spread_start(w + w_fix + w_move, wsrc_w, recv_w, ws_sem, wr_sem)
            spread_wait(wsrc_w, recv_w, ws_sem, wr_sem)
            near = take_points(recv_w)
            eliminate(gg[2, 0], gg[2, 1], near, 2)
            near_fix = take_points(recv_w, 3)
            near_move = take_points(recv_w, 6)
        else:
            spread_start(w, wsrc, recv_s, ss_sem, sr_sem)
            spread_wait(wsrc, recv_s, ss_sem, sr_sem)
            near = take_points(recv_s)
            eliminate(gg[2, 0], gg[2, 1], near, 2)
        dots = total_wait(second)
        alpha1 = dots[0] / dots[1]
        ca = alpha + alpha1 * more
        cb = -(alpha1 * alpha)
        update = update + alpha * z0 + alpha1 * d1
        upd_sum = upd_sum + update
        step_sum = step_sum - (wbuf[0] + ca * wbuf[1] + cb * wbuf[2])
        if not last:
            for r in range(2):
                res = bk[0, r] + ca * bk[1, r] + cb * bk[2, r]
                rs[r] = res
                mv[r] = res + (gg[0, r] + ca * gg[1, r] + cb * gg[2, r])
            cost_row = lane_sum(rs[...] * rs[...])
            near = [near_fix[m] + alpha1 * near_move[m] for m in range(3)]
            ybuf[0] = jnp.stack(mix(1.0, y_fix, alpha1, y_move))
            wbuf[0] = jnp.stack(mix(1.0, w_fix, alpha1, w_move))
        else:
            for r in range(2):
                res_o[r] = bk[0, r] + ca * bk[1, r] + cb * bk[2, r]
            cost_o[pl.ds(2, 1), :] = jnp.broadcast_to(
                0.5 * (dots[2] + 2.0 * alpha1 * dots[3] + alpha1 * alpha1 * dots[4]), (1, LANES)
            )
    upd_o[...] = upd_sum
    step_o[...] = step_sum
    cost_o[pl.ds(3, 5), :] = jnp.zeros((5, LANES), F32)
    for a in range(4):
        total_drain(a)


def body(
    jac_cam,
    jac_pt,
    resid0,
    obs_count,
    tile_camera,
    tile_points,
    obs_camera,
    obs_point,
    cam_params,
    pt_params,
    cg_start,
):
    start = jnp.transpose(
        cg_start[0, 0].reshape(2, 2, CPAR, 64), (2, 0, 1, 3)
    ).reshape(CPAR, 2, LANES)
    vmem = pl.BlockSpec(memory_space=pltpu.VMEM)
    hbm = pl.BlockSpec(memory_space=pl.ANY)
    big = (TILES, LANES)
    blk = (NBLK, LANES)
    dma = pltpu.SemaphoreType.DMA
    upd, steps, res, costs = pl.pallas_call(
        kernel,
        out_shape=[
            jax.ShapeDtypeStruct((CPAR, 2, LANES), F32),
            jax.ShapeDtypeStruct((3,) + blk, F32),
            jax.ShapeDtypeStruct((2,) + big, F32),
            jax.ShapeDtypeStruct((8, LANES), F32),
        ],
        in_specs=[pl.BlockSpec(memory_space=pltpu.SMEM)] + [hbm] * 3 + [vmem] * 6,
        out_specs=[vmem] * 4,
        scratch_shapes=[
            pltpu.VMEM((18,) + big, F32),
            pltpu.VMEM((6,) + big, F32),
            pltpu.VMEM((2,) + big, F32),
            pltpu.VMEM((2,) + big, jnp.int32),
            pltpu.VMEM((2,) + big, jnp.int32),
            pltpu.VMEM((2, 7) + big, F32),
            pltpu.VMEM(big, F32),
            pltpu.VMEM((2,) + big, F32),
            pltpu.VMEM(big, jnp.int32),
            pltpu.VMEM(big, jnp.int32),
            pltpu.VMEM((SLOTS, 3 * TILES), BF16),
            pltpu.VMEM((12,) + big, F32),
            pltpu.VMEM((3,) + big, F32),
            pltpu.VMEM((3, 2) + big, F32),
            pltpu.VMEM((3, 2) + big, F32),
            pltpu.VMEM((2,) + big, F32),
            pltpu.VMEM((9, 12) + blk, F32),
            pltpu.VMEM((8, 12) + blk, F32),
            pltpu.VMEM((3,) + blk, F32),
            pltpu.VMEM((9, 3) + blk, F32),
            pltpu.VMEM((9,) + blk, F32),
            pltpu.VMEM((9, 9) + blk, F32),
            pltpu.VMEM((6,) + blk, F32),
            pltpu.VMEM((6,) + blk, F32),
            pltpu.VMEM((3, 3) + blk, F32),
            pltpu.VMEM((3, 3) + blk, F32),
            pltpu.VMEM((CPAR, 2, LANES), F32),
            pltpu.VMEM((CPAR, 2, LANES), F32),
            pltpu.VMEM((4, 1, LANES), F32),
            pltpu.VMEM((4, GX * GY, LANES), F32),
            dma((4,)),
            dma((8,)),
            dma((8,)),
            dma((8,)),
            dma((8,)),
            dma((8,)),
            dma((8,)),
            dma((4,)),
            dma((4,)),
        ],
        compiler_params=pltpu.CompilerParams(
            collective_id=0, has_side_effects=True, vmem_limit_bytes=48 * 1024 * 1024
        ),
    )(
        tile_points[0, 0],
        jnp.transpose(jac_cam[0, 0], (1, 0, 2)),
        jnp.transpose(jac_pt[0, 0], (1, 0, 2)),
        resid0[0, 0],
        obs_camera[0, 0],
        obs_point[0, 0],
        obs_count[0],
        tile_camera[0],
        tile_points[0],
        start,
    )
    moved = jnp.transpose(upd.reshape(CPAR, 2, 2, 64), (1, 2, 0, 3)).reshape(4, CPAR, 64)
    cam_out = cam_params + moved[None, None]
    pt_out = pt_params + jnp.transpose(steps, (1, 0, 2))[None, None]
    res_out = jnp.transpose(res, (1, 0, 2))[None, None]
    return cam_out, pt_out, res_out, costs[:3, 0]


def solution(mesh):
    wide = P("gx", "gy", None, None, None)
    in_specs = (
        wide,
        wide,
        wide,
        P("gx", "gy", None),
        P("gx", "gy", None),
        P("gx", "gy", None),
        P("gx", "gy", None, None),
        P("gx", "gy", None, None),
        wide,
        wide,
        wide,
    )
    out_specs = (wide, wide, wide, P())
    return jax.shard_map(body, mesh=mesh, in_specs=in_specs, out_specs=out_specs, check_vma=False)
```

```python
import jax
import jax.numpy as jnp
from jax import lax
from jax.experimental import pallas as pl
from jax.experimental.pallas import tpu as pltpu
from jax.sharding import PartitionSpec as P

MESH = pl.DeviceIdType.MESH
CPAR = 9
NBLK = 16
LANES = 128
TILES = 128
SLOTS = 9 * NBLK
GX = 8
GY = 16
PAD = 64
STEPS = (1, 2, 4, 8, 16, 32, 64)
LAMBDAS = (1.0, 0.25)
PAIRS = ((0, 0), (0, 1), (0, 2), (1, 1), (1, 2), (2, 2))
OTHERS = (0, 1, 2, 3, 5, 6, 7, 8)
ORDER = tuple((OTHERS.index(n), n) for n in (0, 2, 6, 8, 3, 5, 1, 7))
F32 = jnp.float32
BF16 = jnp.bfloat16
GATHER = lax.GatherDimensionNumbers(
    offset_dims=(),
    collapsed_slice_dims=(1,),
    start_index_map=(1,),
    operand_batching_dims=(0,),
    start_indices_batching_dims=(0,),
)


def pick(x, idx):
    return lax.gather(
        x, idx[:, :, None], GATHER, (1, 1), mode=lax.GatherScatterMode.PROMISE_IN_BOUNDS
    )


def lane_ids(rows):
    return lax.broadcasted_iota(jnp.int32, (rows, LANES), 1)


def sort_lanes(key):
    lane = lane_ids(key.shape[0])
    size = 2
    while size <= LANES:
        gap = size // 2
        while gap >= 1:
            other = pick(key, lane ^ gap)
            keep_low = ((lane & gap) == 0) == ((lane & size) == 0)
            key = jnp.where(keep_low, jnp.minimum(key, other), jnp.maximum(key, other))
            gap //= 2
        size *= 2
    return key


def last_at_most(seg, target):
    count = jnp.zeros_like(target)
    for step in (64, 32, 16, 8, 4, 2, 1):
        count = jnp.where(pick(seg, count + (step - 1)) <= target, count + step, count)
    return jnp.where(pick(seg, count) <= target, count + 1, count)


def column(row):
    return jnp.swapaxes(jnp.broadcast_to(row.astype(F32), (LANES, LANES)), 0, 1)


def invert(hess, damping):
    h00 = hess[0] + damping * (hess[0] + 1.0)
    h01, h02 = hess[1], hess[2]
    h11 = hess[3] + damping * (hess[3] + 1.0)
    h12 = hess[4]
    h22 = hess[5] + damping * (hess[5] + 1.0)
    c00 = h11 * h22 - h12 * h12
    c01 = h02 * h12 - h01 * h22
    c02 = h01 * h12 - h02 * h11
    c11 = h00 * h22 - h02 * h02
    c12 = h01 * h02 - h00 * h12
    c22 = h00 * h11 - h01 * h01
    det = h00 * c00 + h01 * c01 + h02 * c02
    return [c / det for c in (c00, c01, c02, c11, c12, c22)]


def apply_inverse(inv, y):
    return [
        inv[0] * y[0] + inv[1] * y[1] + inv[2] * y[2],
        inv[1] * y[0] + inv[3] * y[1] + inv[4] * y[2],
        inv[2] * y[0] + inv[4] * y[1] + inv[5] * y[2],
    ]


def lane_sum(x):
    while x.ndim > 2:
        x = jnp.sum(x, axis=0)
    return jnp.sum(x, axis=0, keepdims=True)


def kernel(
    slot_s,
    jc_h,
    jp_h,
    rs_h,
    cam_h,
    pt_h,
    count_h,
    tcam_h,
    tpts_h,
    start_h,
    upd_o,
    step_o,
    res_o,
    cost_o,
    jc,
    jp,
    rs,
    obs_cam,
    obs_pt,
    count_r,
    tcam_r,
    tpts_r,
    start_r,
    jct,
    jpt,
    seg_t,
    scan_a,
    scan_b,
    perm,
    endi,
    smask,
    hit_p,
    hit_c,
    pair_m,
    idx_c,
    onehot,
    table,
    gg,
    bk,
    mv,
    contrib,
    recv_c,
    contrib_y,
    recv_y,
    wsrc,
    recv_s,
    wsrc_w,
    recv_w,
    wsrc_2,
    recv_2,
    hess_b,
    inv_b,
    ybuf,
    wbuf,
    camvec,
    camacc,
    ar_src,
    arx,
    in_sem,
    cs_sem,
    cr_sem,
    ys_sem,
    yr_sem,
    ss_sem,
    sr_sem,
    ws_sem,
    wr_sem,
    s2_sem,
    r2_sem,
    as_sem,
    ar_sem,
):
    me_x = lax.axis_index("gx")
    me_y = lax.axis_index("gy")

    def at(dx, dy):
        return (lax.rem(me_x + (dx + GX), GX), lax.rem(me_y + (dy + GY), GY))

    me = me_x * GY + me_y
    here = {}
    for n in OTHERS:
        a, b = divmod(n, 3)
        x, y = me_x + (a - 1), me_y + (b - 1)
        here[n] = (x >= 0) & (x < GX) & (y >= 0) & (y < GY)

    def to_all(act):
        def row(j, carry):
            dy = lax.rem(j + 5, GY - 1) + 1
            for dx in (4, 3, 5, 2, 6, 1, 7, 0):
                act(dx, dy)
            return carry

        lax.fori_loop(0, GY - 1, row, 0)
        for dx in (4, 3, 5, 2, 6, 1, 7):
            act(dx, 0)

    pairs = [
        (pt_h, obs_pt),
        (jp_h, jp),
        (jc_h, jc),
        (cam_h, obs_cam),
        (rs_h.at[:, 0, :], rs.at[0]),
        (rs_h.at[:, 1, :], rs.at[1]),
        (tcam_h, tcam_r),
        (count_h, count_r),
        (tpts_h, tpts_r),
        (start_h, start_r),
    ]
    copies = [
        pltpu.make_async_copy(src, dst, in_sem.at[i]) for i, (src, dst) in enumerate(pairs)
    ]
    for copy in copies:
        copy.start()

    for r, n in enumerate(OTHERS):

        @pl.when(jnp.logical_not(here[n]))
        def _(r=r, n=n):
            recv_c[r] = jnp.zeros_like(recv_c[r])
            recv_s[n] = jnp.zeros_like(recv_s[n])
            recv_w[n] = jnp.zeros_like(recv_w[n])
            recv_2[n] = jnp.zeros_like(recv_2[n])
            recv_y[r] = jnp.zeros_like(recv_y[r])

    barrier = pltpu.get_barrier_semaphore()
    to_all(
        lambda dx, dy: pl.semaphore_signal(
            barrier, inc=1, device_id=at(dx, dy), device_id_type=MESH
        )
    )

    seg_t[0:PAD, :] = jnp.full((PAD, LANES), -1.0, F32)
    for k in range(CPAR):
        scan_a[k, 0:PAD, :] = jnp.zeros((PAD, LANES), F32)
        scan_b[k, 0:PAD, :] = jnp.zeros((PAD, LANES), F32)
    lane = lane_ids(TILES)

    def order(kind, ids, target):
        key = sort_lanes(ids * LANES + lane)
        perm[kind] = key & (LANES - 1)
        seg = key >> 7
        count = last_at_most(seg, target)
        last = jnp.maximum(count - 1, 0)
        endi[kind] = last
        found = (count > 0) & (pick(seg, last) == target)
        seg_t[PAD : PAD + LANES, :] = jnp.swapaxes(seg.astype(F32), 0, 1)
        for i, d in enumerate(STEPS):
            same = seg_t[PAD : PAD + LANES, :] == seg_t[PAD - d : PAD + LANES - d, :]
            smask[kind, i] = jnp.where(same, 1.0, 0.0)
        return found

    def sorted_t(x, kind):
        return jnp.swapaxes(pick(x, perm[kind]), 0, 1)

    def summed(values, kind):
        count = len(values)
        src, dst = scan_a, scan_b
        for k in range(count):
            src[k, PAD : PAD + LANES, :] = values[k]
        for i, d in enumerate(STEPS):
            for k in range(count):
                dst[k, PAD : PAD + LANES, :] = (
                    src[k, PAD : PAD + LANES, :]
                    + src[k, PAD - d : PAD + LANES - d, :] * smask[kind, i]
                )
            src, dst = dst, src
        return [
            pick(jnp.swapaxes(src[k, PAD : PAD + LANES, :], 0, 1), endi[kind])
            for k in range(count)
        ]

    def put_points(values, first, dest):
        sums = jnp.concatenate([v * hit_p[...] for v in summed(values, 0)], axis=1)
        high = sums.astype(BF16)
        rest = sums - high.astype(F32)
        mid = rest.astype(BF16)
        low = (rest - mid.astype(F32)).astype(BF16)
        parts = jnp.concatenate([high, mid, low], axis=0)
        out = jnp.dot(onehot[...], parts, preferred_element_type=F32)
        for n in range(9):
            for m in range(3):
                dest[n, first + m] = out[
                    n * NBLK : (n + 1) * NBLK, m * LANES : (m + 1) * LANES
                ]

    def put_cams(values):
        for k, sums in enumerate(summed(values, 1)):
            top = lane_sum(sums * hit_c[0])
            bottom = lane_sum(sums * hit_c[1])
            camacc[k] = jnp.concatenate([top, bottom], axis=0)
        return camacc[...]

    def take_cams(vector, b):
        camvec[...] = vector
        rows = 32

        def one(chunk, carry):
            where = pl.ds(pl.multiple_of(chunk * rows, rows), rows)
            idx = idx_c[where, :]
            second = pair_m[where, :] == 1
            e0 = jnp.zeros((rows, LANES), F32)
            e1 = jnp.zeros((rows, LANES), F32)
            for k in range(CPAR):
                v = camvec[k]
                src = jnp.where(
                    second,
                    jnp.broadcast_to(v[1:2], (rows, LANES)),
                    jnp.broadcast_to(v[0:1], (rows, LANES)),
                )
                got = pick(src, idx)
                e0 = e0 + jc[k, where, :] * got
                e1 = e1 + jc[CPAR + k, where, :] * got
            gg[b, 0, where, :] = e0
            gg[b, 1, where, :] = e1
            return carry

        lax.fori_loop(0, TILES // rows, one, 0)

    def to_points(e0, e1):
        t0, t1 = sorted_t(e0, 0), sorted_t(e1, 0)
        return [jpt[m] * t0 + jpt[3 + m] * t1 for m in range(3)]

    def collect_start(comps, src, dst, send_sem, recv_sem):
        for r, n in ORDER:
            a, b = divmod(n, 3)

            @pl.when(here[n])
            def _(r=r, n=n, a=a, b=b):
                pltpu.make_async_remote_copy(
                    src_ref=src.at[n, pl.ds(0, comps)],
                    dst_ref=dst.at[r, pl.ds(0, comps)],
                    send_sem=send_sem.at[r],
                    recv_sem=recv_sem.at[r],
                    device_id=at(a - 1, b - 1),
                    device_id_type=MESH,
                ).start()

    def collect_wait(comps, src, dst, send_sem, recv_sem):
        for sem, flip in ((recv_sem, True), (send_sem, False)):
            for r, n in enumerate(OTHERS):

                @pl.when(here[8 - n] if flip else here[n])
                def _(r=r, n=n, sem=sem):
                    pltpu.make_async_copy(
                        src.at[n, pl.ds(0, comps)], dst.at[r, pl.ds(0, comps)], sem.at[r]
                    ).wait()

        total = []
        for m in range(comps):
            s = src[4, m]
            for r in range(8):
                s = s + dst[r, m]
            total.append(s)
        return total

    pts = (contrib, recv_c, cs_sem, cr_sem)
    pts_y = (contrib_y, recv_y, ys_sem, yr_sem)
    out_s = (wsrc, recv_s, ss_sem, sr_sem)
    out_w = (wsrc_w, recv_w, ws_sem, wr_sem)
    out_2 = (wsrc_2, recv_2, s2_sem, r2_sem)

    def spread_start(values, src, dst, send_sem, recv_sem):
        for m, v in enumerate(values):
            src[m] = v
            dst[4, m] = v
        for r, n in ORDER:
            a, b = divmod(n, 3)

            @pl.when(here[n])
            def _(r=r, n=n, a=a, b=b):
                pltpu.make_async_remote_copy(
                    src_ref=src,
                    dst_ref=dst.at[8 - n],
                    send_sem=send_sem.at[r],
                    recv_sem=recv_sem.at[r],
                    device_id=at(a - 1, b - 1),
                    device_id_type=MESH,
                ).start()

    def spread_wait(src, dst, send_sem, recv_sem):
        for sem, flip in ((recv_sem, True), (send_sem, False)):
            for r, n in enumerate(OTHERS):

                @pl.when(here[8 - n] if flip else here[n])
                def _(r=r, n=n, sem=sem):
                    pltpu.make_async_copy(src, dst.at[8 - n], sem.at[r]).wait()

    def take_points(src, first=0):
        def one(chunk, carry):
            for i in range(8):
                t = chunk * 8 + i
                slot = slot_s[t]
                n = slot >> 4
                q = slot & 15
                for m in range(3):
                    table[m, pl.ds(t, 1), :] = src[n, first + m, pl.ds(q, 1), :]
            return carry

        lax.fori_loop(0, TILES // 8, one, 0)
        return [pick(table[m], obs_pt[...]) for m in range(3)]

    def eliminate(e0, e1, near, b):
        bk[b, 0] = e0 - (jp[0] * near[0] + jp[1] * near[1] + jp[2] * near[2])
        bk[b, 1] = e1 - (jp[3] * near[0] + jp[4] * near[1] + jp[5] * near[2])

    def back_to_cams(b):
        t0, t1 = sorted_t(bk[b, 0], 1), sorted_t(bk[b, 1], 1)
        return put_cams([jct[k] * t0 + jct[CPAR + k] * t1 for k in range(CPAR)])

    def total_start(a, rows):
        held = jnp.concatenate(rows + [jnp.zeros((8 - len(rows), LANES), F32)], axis=0)
        sums = jnp.sum(held, axis=1, keepdims=True)
        lane8 = lane_ids(8)
        own = lax.broadcasted_iota(jnp.int32, (8, LANES), 0)
        row = jnp.sum(jnp.where(lane8 == own, sums, 0.0), axis=0, keepdims=True)
        ar_src[a] = row
        arx[a, pl.ds(me, 1), :] = row

        def send(dx, dy):
            pltpu.make_async_remote_copy(
                src_ref=ar_src.at[a],
                dst_ref=arx.at[a, pl.ds(me, 1)],
                send_sem=as_sem.at[a],
                recv_sem=ar_sem.at[a],
                device_id=at(dx, dy),
                device_id_type=MESH,
            ).start()

        to_all(send)

    def total_wait(a):
        pltpu.make_async_copy(
            arx.at[a, pl.ds(0, 127)], arx.at[a, pl.ds(0, 127)], ar_sem.at[a]
        ).wait()
        row = jnp.sum(arx[a], axis=0, keepdims=True)
        lane1 = lane_ids(1)
        return [
            jnp.sum(jnp.where(lane1 == i, row, 0.0), axis=1, keepdims=True) for i in range(8)
        ]

    def total_drain(a):
        pltpu.make_async_copy(
            arx.at[a, pl.ds(0, 127)], arx.at[a, pl.ds(0, 127)], as_sem.at[a]
        ).wait()

    copies[0].wait()
    hit_p[...] = jnp.where(order(0, obs_pt[...], lane), 1.0, 0.0)
    for copy in copies[1:]:
        copy.wait()
    slot_row = lax.broadcasted_iota(jnp.int32, (SLOTS, TILES), 0)
    hot = jnp.where(slot_row == tpts_r[...], 1.0, 0.0).astype(BF16)
    for i in range(3):
        onehot[:, i * TILES : (i + 1) * TILES] = hot
    tcam = column(tcam_r[...]).astype(jnp.int32)
    parity = tcam & 1
    pair = tcam >> 1
    pair_m[...] = pair
    idx_c[...] = parity * 64 + obs_cam[...]

    valid = jnp.where(lane < column(count_r[...]).astype(jnp.int32), 1.0, 0.0)
    for k in range(2):
        rs[k] = rs[k] * valid
    for k in range(6):
        jp[k] = jp[k] * valid
        jpt[k] = sorted_t(jp[k], 0)
    for k in range(18):
        jc[k] = jc[k] * valid
    square = [jpt[i] * jpt[j] + jpt[3 + i] * jpt[3 + j] for i, j in PAIRS]
    put_points(square[0:3], 0, contrib)
    put_points(square[3:6], 3, contrib)

    start = jnp.concatenate(
        [
            jnp.concatenate([start_r[:, 2 * p, :], start_r[:, 2 * p + 1, :]], axis=1)[:, None, :]
            for p in range(2)
        ],
        axis=1,
    )
    take_cams(start, 0)
    for k in range(2):
        mv[k] = rs[k] + gg[0, k]
    put_points(to_points(mv[0], mv[1]), 6, contrib)
    pl.semaphore_wait(barrier, GX * GY - 1)
    collect_start(9, *pts)
    put_points(to_points(gg[0, 0], gg[0, 1]), 0, contrib_y)
    collect_start(3, *pts_y)
    found = order(1, obs_cam[...], lane & 63)
    mine = found & ((lane >> 6) == parity)
    hit_c[0] = jnp.where(mine & (pair == 0), 1.0, 0.0)
    hit_c[1] = jnp.where(mine & (pair == 1), 1.0, 0.0)
    for k in range(18):
        jct[k] = sorted_t(jc[k], 1)
    diag = put_cams([jct[k] * jct[k] + jct[CPAR + k] * jct[CPAR + k] for k in range(CPAR)])
    cost_row = lane_sum(rs[...] * rs[...])
    owned = collect_wait(9, *pts)
    for c in range(6):
        hess_b[c] = owned[c]
    ybuf[0] = jnp.stack(owned[6:9])

    update = start
    upd_sum = jnp.zeros_like(start)
    step_sum = jnp.zeros((3, NBLK, LANES), F32)

    def weighted(w):
        h = [hess_b[c] for c in range(6)]
        return [
            h[0] * w[0] + h[1] * w[1] + h[2] * w[2],
            h[1] * w[0] + h[3] * w[1] + h[4] * w[2],
            h[2] * w[0] + h[4] * w[1] + h[5] * w[2],
        ]

    def inner(u, v):
        return lane_sum(u[0] * v[0] + u[1] * v[1] + u[2] * v[2])

    def three(buf, b):
        return [buf[b, m] for m in range(3)]

    def mix(p, u, q, v):
        return [p * u[m] + q * v[m] for m in range(3)]

    inv = invert([hess_b[c] for c in range(6)], LAMBDAS[0])
    for c in range(6):
        inv_b[c] = inv[c]
    w0 = apply_inverse(inv, three(ybuf, 0))
    wbuf[0] = jnp.stack(w0)
    spread_start(w0, *out_s)
    spread_wait(*out_s)
    near = take_points(recv_s)

    for step in range(2):
        damping = LAMBDAS[step]
        last = step == 1
        cam_damp = damping * (diag + 1.0)
        precond = diag + cam_damp
        if step == 0:
            eliminate(mv[0], mv[1], near, 0)
        r0 = -back_to_cams(0) - cam_damp * update
        z0 = r0 / precond

        take_cams(z0, 1)
        put_points(to_points(gg[1, 0], gg[1, 1]), 0, contrib)
        collect_start(3, *pts)
        if last:
            spread_wait(*out_2)
            near = take_points(recv_2)
            for r in range(2):
                shift = jp[3 * r] * near[0] + jp[3 * r + 1] * near[1] + jp[3 * r + 2] * near[2]
                res = rs[r] - cb * shift
                rs[r] = res
                mv[r] = mv[r] + res
            cost_row = lane_sum(rs[...] * rs[...])
        y = collect_wait(3, *pts)
        ybuf[1] = jnp.stack(y)
        w = apply_inverse([inv_b[c] for c in range(6)], y)
        wbuf[1] = jnp.stack(w)
        spread_start(w, *out_s)
        spread_wait(*out_s)
        near = take_points(recv_s)
        eliminate(gg[1, 0], gg[1, 1], near, 1)
        c0 = back_to_cams(1) + cam_damp * z0
        u = c0 / precond
        first = 2 * step
        total_start(first, [lane_sum(r0 * z0), lane_sum(z0 * c0), lane_sum(c0 * u), cost_row])

        take_cams(u, 2)
        put_points(to_points(gg[2, 0], gg[2, 1]), 0, contrib)
        collect_start(3, *pts)
        y = collect_wait(3, *pts)
        ybuf[2] = jnp.stack(y)
        w = apply_inverse([inv_b[c] for c in range(6)], y)
        wbuf[2] = jnp.stack(w)

        dots = total_wait(first)
        resid_dot, curve, square = dots[0], dots[1], dots[2]
        cost_o[pl.ds(step, 1), :] = jnp.broadcast_to(0.5 * dots[3], (1, LANES))
        alpha = resid_dot / curve
        beta = (resid_dot - 2.0 * alpha * curve + alpha * alpha * square) / resid_dot
        more = 1.0 + beta
        z1 = (r0 - alpha * c0) / precond
        d1 = z1 + beta * z0
        turn = [more * gg[1, r] - alpha * gg[2, r] for r in range(2)]
        y_turn = mix(more, three(ybuf, 1), -alpha, three(ybuf, 2))
        w_turn = mix(more, three(wbuf, 1), -alpha, three(wbuf, 2))
        turn_sq = lane_sum(turn[0] * turn[0] + turn[1] * turn[1])
        yw = inner(y_turn, w_turn)
        rows = [
            lane_sum((r0 - alpha * c0) * z1),
            turn_sq - yw + lane_sum(cam_damp * (d1 * d1)),
        ]
        if last:
            base = [mv[r] + alpha * gg[1, r] for r in range(2)]
            y_base = mix(1.0, three(ybuf, 0), alpha, three(ybuf, 1))
            w_base = mix(1.0, three(wbuf, 0), alpha, three(wbuf, 1))
            hw_base = weighted(w_base)
            hw_turn = weighted(w_turn)
            rows += [
                lane_sum(base[0] * base[0] + base[1] * base[1])
                - 2.0 * inner(y_base, w_base)
                + inner(w_base, hw_base),
                lane_sum(base[0] * turn[0] + base[1] * turn[1])
                - inner(y_base, w_turn)
                - inner(y_turn, w_base)
                + inner(w_base, hw_turn),
                turn_sq - 2.0 * yw + inner(w_turn, hw_turn),
            ]
        second = first + 1
        total_start(second, rows)
        if not last:
            hess = [hess_b[c] for c in range(6)]
            inv = invert(hess, LAMBDAS[1])
            for c in range(6):
                inv_b[c] = inv[c]
            scale = [damping * (hess[c] + 1.0) for c in (0, 3, 5)]
            held = []
            for b in range(3):
                held.append([scale[m] * wbuf[b, m] + ybuf[b, m] for m in range(3)])
            y_start = collect_wait(3, *pts_y)
            y_fix = [
                scale[m] * wbuf[0, m] + y_start[m] + alpha * held[1][m] for m in range(3)
            ]
            y_move = mix(more, held[1], -alpha, held[2])
            w_fix = apply_inverse(inv, y_fix)
            w_move = apply_inverse(inv, y_move)
            spread_start(w_fix + mix(1.0, w_move, -alpha, w), *out_w)
            spread_start(w, *out_2)
            spread_wait(*out_w)
            near_fix = take_points(recv_w)
            near_move = take_points(recv_w, 3)
        else:
            spread_start(w, *out_s)
            spread_wait(*out_s)
            near = take_points(recv_s)
            eliminate(gg[2, 0], gg[2, 1], near, 2)
        dots = total_wait(second)
        alpha1 = dots[0] / dots[1]
        ca = alpha + alpha1 * more
        cb = -(alpha1 * alpha)
        update = update + alpha * z0 + alpha1 * d1
        upd_sum = upd_sum + update
        step_sum = step_sum - (wbuf[0] + ca * wbuf[1] + cb * wbuf[2])
        if not last:
            near = [near_fix[m] + alpha1 * near_move[m] for m in range(3)]
            for r in range(2):
                rs[r] = bk[0, r] + ca * bk[1, r] + cb * gg[2, r]
                mv[r] = gg[0, r] + ca * gg[1, r] + cb * gg[2, r]
            eliminate(rs[0] + mv[0], rs[1] + mv[1], near, 0)
            ybuf[0] = jnp.stack(mix(1.0, y_fix, alpha1, y_move))
            wbuf[0] = jnp.stack(mix(1.0, w_fix, alpha1, w_move))
        else:
            for r in range(2):
                res_o[r] = bk[0, r] + ca * bk[1, r] + cb * bk[2, r]
            cost_o[pl.ds(2, 1), :] = jnp.broadcast_to(
                0.5 * (dots[2] + 2.0 * alpha1 * dots[3] + alpha1 * alpha1 * dots[4]), (1, LANES)
            )
    upd_o[...] = upd_sum
    step_o[...] = step_sum
    cost_o[pl.ds(3, 5), :] = jnp.zeros((5, LANES), F32)
    for a in range(4):
        total_drain(a)


def body(
    jac_cam,
    jac_pt,
    resid0,
    obs_count,
    tile_camera,
    tile_points,
    obs_camera,
    obs_point,
    cam_params,
    pt_params,
    cg_start,
):
    vmem = pl.BlockSpec(memory_space=pltpu.VMEM)
    hbm = pl.BlockSpec(memory_space=pl.ANY)
    big = (TILES, LANES)
    blk = (NBLK, LANES)
    dma = pltpu.SemaphoreType.DMA
    upd, steps, res, costs = pl.pallas_call(
        kernel,
        out_shape=[
            jax.ShapeDtypeStruct((CPAR, 2, LANES), F32),
            jax.ShapeDtypeStruct((3,) + blk, F32),
            jax.ShapeDtypeStruct((2,) + big, F32),
            jax.ShapeDtypeStruct((8, LANES), F32),
        ],
        in_specs=[pl.BlockSpec(memory_space=pltpu.SMEM)] + [hbm] * 9,
        out_specs=[vmem] * 4,
        scratch_shapes=[
            pltpu.VMEM((18,) + big, F32),
            pltpu.VMEM((6,) + big, F32),
            pltpu.VMEM((2,) + big, F32),
            pltpu.VMEM(big, jnp.int32),
            pltpu.VMEM(big, jnp.int32),
            pltpu.VMEM((1, LANES), jnp.int32),
            pltpu.VMEM((1, LANES), jnp.int32),
            pltpu.VMEM((1, LANES), jnp.int32),
            pltpu.VMEM((CPAR, 4, 64), F32),
            pltpu.VMEM((18,) + big, F32),
            pltpu.VMEM((6,) + big, F32),
            pltpu.VMEM((PAD + LANES, LANES), F32),
            pltpu.VMEM((CPAR, PAD + LANES, LANES), F32),
            pltpu.VMEM((CPAR, PAD + LANES, LANES), F32),
            pltpu.VMEM((2,) + big, jnp.int32),
            pltpu.VMEM((2,) + big, jnp.int32),
            pltpu.VMEM((2, 7) + big, F32),
            pltpu.VMEM(big, F32),
            pltpu.VMEM((2,) + big, F32),
            pltpu.VMEM(big, jnp.int32),
            pltpu.VMEM(big, jnp.int32),
            pltpu.VMEM((SLOTS, 3 * TILES), BF16),
            pltpu.VMEM((3,) + big, F32),
            pltpu.VMEM((3, 2) + big, F32),
            pltpu.VMEM((3, 2) + big, F32),
            pltpu.VMEM((2,) + big, F32),
            pltpu.VMEM((9, 9) + blk, F32),
            pltpu.VMEM((8, 9) + blk, F32),
            pltpu.VMEM((9, 3) + blk, F32),
            pltpu.VMEM((8, 3) + blk, F32),
            pltpu.VMEM((3,) + blk, F32),
            pltpu.VMEM((9, 3) + blk, F32),
            pltpu.VMEM((6,) + blk, F32),
            pltpu.VMEM((9, 6) + blk, F32),
            pltpu.VMEM((3,) + blk, F32),
            pltpu.VMEM((9, 3) + blk, F32),
            pltpu.VMEM((6,) + blk, F32),
            pltpu.VMEM((6,) + blk, F32),
            pltpu.VMEM((3, 3) + blk, F32),
            pltpu.VMEM((3, 3) + blk, F32),
            pltpu.VMEM((CPAR, 2, LANES), F32),
            pltpu.VMEM((CPAR, 2, LANES), F32),
            pltpu.VMEM((4, 1, LANES), F32),
            pltpu.VMEM((4, GX * GY, LANES), F32),
            dma((10,)),
        ]
        + [dma((8,))] * 10
        + [dma((4,))] * 2,
        compiler_params=pltpu.CompilerParams(
            collective_id=0, has_side_effects=True, vmem_limit_bytes=62 * 1024 * 1024
        ),
    )(
        tile_points[0, 0],
        jnp.transpose(jac_cam[0, 0], (1, 0, 2)),
        jnp.transpose(jac_pt[0, 0], (1, 0, 2)),
        resid0[0, 0],
        obs_camera[0, 0],
        obs_point[0, 0],
        obs_count[0],
        tile_camera[0],
        tile_points[0],
        jnp.transpose(cg_start[0, 0], (1, 0, 2)),
    )
    moved = jnp.transpose(upd.reshape(CPAR, 2, 2, 64), (1, 2, 0, 3)).reshape(4, CPAR, 64)
    cam_out = cam_params + moved[None, None]
    pt_out = pt_params + jnp.transpose(steps, (1, 0, 2))[None, None]
    res_out = jnp.transpose(res, (1, 0, 2))[None, None]
    return cam_out, pt_out, res_out, costs[:3, 0]


def solution(mesh):
    wide = P("gx", "gy", None, None, None)
    in_specs = (
        wide,
        wide,
        wide,
        P("gx", "gy", None),
        P("gx", "gy", None),
        P("gx", "gy", None),
        P("gx", "gy", None, None),
        P("gx", "gy", None, None),
        wide,
        wide,
        wide,
    )
    out_specs = (wide, wide, wide, P())
    return jax.shard_map(body, mesh=mesh, in_specs=in_specs, out_specs=out_specs, check_vma=False)
```

```python
import jax
import jax.numpy as jnp
from jax import lax
from jax.experimental import pallas as pl
from jax.experimental.pallas import tpu as pltpu
from jax.sharding import PartitionSpec as P

MESH = pl.DeviceIdType.MESH
CPAR = 9
NBLK = 16
LANES = 128
TILES = 128
SLOTS = 9 * NBLK
GX = 8
GY = 16
PAD = 64
STEPS = (1, 2, 4, 8, 16, 32, 64)
LAMBDAS = (1.0, 0.25)
PAIRS = ((0, 0), (0, 1), (0, 2), (1, 1), (1, 2), (2, 2))
OTHERS = (0, 1, 2, 3, 5, 6, 7, 8)
ORDER = tuple((OTHERS.index(n), n) for n in (0, 2, 6, 8, 3, 5, 1, 7))
F32 = jnp.float32
BF16 = jnp.bfloat16
GATHER = lax.GatherDimensionNumbers(
    offset_dims=(),
    collapsed_slice_dims=(1,),
    start_index_map=(1,),
    operand_batching_dims=(0,),
    start_indices_batching_dims=(0,),
)


def pick(x, idx):
    return lax.gather(
        x, idx[:, :, None], GATHER, (1, 1), mode=lax.GatherScatterMode.PROMISE_IN_BOUNDS
    )


def lane_ids(rows):
    return lax.broadcasted_iota(jnp.int32, (rows, LANES), 1)


def sort_lanes(key):
    flat = jnp.swapaxes(key.astype(F32), 0, 1).reshape(16, 8, LANES)
    regs = [flat[v] for v in range(16)]
    sub = lax.broadcasted_iota(jnp.int32, (8, LANES), 0)
    before = None
    size = 2
    while size <= LANES:
        if size >= 16:
            bit = size // 16
            sign = jnp.where((sub & bit) == 0, 1.0, -1.0)
            turn = sign if before is None else sign * before
            regs = [x * turn for x in regs]
            before = sign
        gap = size // 2
        while gap >= 1:
            if gap < 16:
                for v in range(16):
                    if v & gap == 0:
                        low = jnp.minimum(regs[v], regs[v + gap])
                        high = jnp.maximum(regs[v], regs[v + gap])
                        up = size >= 16 or v & size == 0
                        regs[v], regs[v + gap] = (low, high) if up else (high, low)
            else:
                g = gap // 16
                first = (sub & g) == 0
                for v in range(16):
                    x = regs[v]
                    other = jnp.where(
                        first, pltpu.roll(x, 8 - g, axis=0), pltpu.roll(x, g, axis=0)
                    )
                    regs[v] = jnp.where(first, jnp.minimum(x, other), jnp.maximum(x, other))
            gap //= 2
        size *= 2
    rows = jnp.swapaxes(jnp.concatenate(regs, axis=0), 0, 1)
    lane = lane_ids(LANES)
    return pick(rows, (lane & 15) * 8 + (lane >> 4)).astype(jnp.int32)


def last_at_most(seg, target):
    count = jnp.zeros_like(target)
    for step in (64, 32, 16, 8, 4, 2, 1):
        count = jnp.where(pick(seg, count + (step - 1)) <= target, count + step, count)
    return jnp.where(pick(seg, count) <= target, count + 1, count)


def column(row):
    return jnp.swapaxes(jnp.broadcast_to(row.astype(F32), (LANES, LANES)), 0, 1)


def invert(hess, damping):
    h00 = hess[0] + damping * (hess[0] + 1.0)
    h01, h02 = hess[1], hess[2]
    h11 = hess[3] + damping * (hess[3] + 1.0)
    h12 = hess[4]
    h22 = hess[5] + damping * (hess[5] + 1.0)
    c00 = h11 * h22 - h12 * h12
    c01 = h02 * h12 - h01 * h22
    c02 = h01 * h12 - h02 * h11
    c11 = h00 * h22 - h02 * h02
    c12 = h01 * h02 - h00 * h12
    c22 = h00 * h11 - h01 * h01
    det = h00 * c00 + h01 * c01 + h02 * c02
    return [c / det for c in (c00, c01, c02, c11, c12, c22)]


def apply_inverse(inv, y):
    return [
        inv[0] * y[0] + inv[1] * y[1] + inv[2] * y[2],
        inv[1] * y[0] + inv[3] * y[1] + inv[4] * y[2],
        inv[2] * y[0] + inv[4] * y[1] + inv[5] * y[2],
    ]


def lane_sum(x):
    while x.ndim > 2:
        x = jnp.sum(x, axis=0)
    return jnp.sum(x, axis=0, keepdims=True)


def kernel(
    slot_s,
    jc_h,
    jp_h,
    rs_h,
    cam_h,
    pt_h,
    count_h,
    tcam_h,
    tpts_h,
    start_h,
    cpar_h,
    ppar_h,
    cam_o,
    pt_o,
    res_o,
    cost_o,
    jc,
    jp,
    rs,
    rs_in,
    obs_cam,
    obs_pt,
    count_r,
    tcam_r,
    tpts_r,
    start_r,
    cam_r,
    pt_r,
    jct,
    jpt,
    seg_t,
    scan_a,
    scan_b,
    perm,
    endi,
    smask,
    hit_p,
    hit_c,
    pair_m,
    idx_c,
    onehot,
    table,
    gg,
    bk,
    mv,
    contrib,
    recv_c,
    contrib_y,
    recv_y,
    wsrc,
    recv_s,
    wsrc_w,
    recv_w,
    wsrc_2,
    recv_2,
    hess_b,
    inv_b,
    ybuf,
    wbuf,
    camvec,
    camacc,
    ar_src,
    arx,
    px_src,
    px_dst,
    py_src,
    py_dst,
    in_sem,
    cs_sem,
    cr_sem,
    ys_sem,
    yr_sem,
    ss_sem,
    sr_sem,
    ws_sem,
    wr_sem,
    s2_sem,
    r2_sem,
    as_sem,
    ar_sem,
    pxs_sem,
    pxr_sem,
    pys_sem,
    pyr_sem,
):
    me_x = lax.axis_index("gx")
    me_y = lax.axis_index("gy")

    def at(dx, dy):
        return (lax.rem(me_x + (dx + GX), GX), lax.rem(me_y + (dy + GY), GY))

    me = me_x * GY + me_y
    here = {}
    for n in OTHERS:
        a, b = divmod(n, 3)
        x, y = me_x + (a - 1), me_y + (b - 1)
        here[n] = (x >= 0) & (x < GX) & (y >= 0) & (y < GY)

    def to_all(act):
        def row(j, carry):
            dy = lax.rem(j + 5, GY - 1) + 1
            for dx in (4, 3, 5, 2, 6, 1, 7, 0):
                act(dx, dy)
            return carry

        lax.fori_loop(0, GY - 1, row, 0)
        for dx in (4, 3, 5, 2, 6, 1, 7):
            act(dx, 0)

    pairs = [
        (pt_h, obs_pt),
        (jp_h, jp),
        (jc_h, jc),
        (cam_h, obs_cam),
        (rs_h, rs_in),
        (tcam_h, tcam_r),
        (count_h, count_r),
        (tpts_h, tpts_r),
        (start_h, start_r),
        (cpar_h, cam_r),
        (ppar_h, pt_r),
    ]
    copies = [
        pltpu.make_async_copy(src, dst, in_sem.at[i]) for i, (src, dst) in enumerate(pairs)
    ]
    for copy in copies:
        copy.start()

    for r, n in enumerate(OTHERS):

        @pl.when(jnp.logical_not(here[n]))
        def _(r=r, n=n):
            recv_c[r] = jnp.zeros_like(recv_c[r])
            recv_s[n] = jnp.zeros_like(recv_s[n])
            recv_w[n] = jnp.zeros_like(recv_w[n])
            recv_2[n] = jnp.zeros_like(recv_2[n])
            recv_y[r] = jnp.zeros_like(recv_y[r])

    barrier = pltpu.get_barrier_semaphore()
    to_all(
        lambda dx, dy: pl.semaphore_signal(
            barrier, inc=1, device_id=at(dx, dy), device_id_type=MESH
        )
    )

    seg_t[0:PAD, :] = jnp.full((PAD, LANES), -1.0, F32)
    for k in range(CPAR):
        scan_a[k, 0:PAD, :] = jnp.zeros((PAD, LANES), F32)
        scan_b[k, 0:PAD, :] = jnp.zeros((PAD, LANES), F32)
    lane = lane_ids(TILES)

    def order(kind, ids, target):
        key = sort_lanes(ids * LANES + lane)
        perm[kind] = key & (LANES - 1)
        seg = key >> 7
        count = last_at_most(seg, target)
        last = jnp.maximum(count - 1, 0)
        endi[kind] = last
        found = (count > 0) & (pick(seg, last) == target)
        seg_t[PAD : PAD + LANES, :] = jnp.swapaxes(seg.astype(F32), 0, 1)
        for i, d in enumerate(STEPS):
            same = seg_t[PAD : PAD + LANES, :] == seg_t[PAD - d : PAD + LANES - d, :]
            smask[kind, i] = jnp.where(same, 1.0, 0.0)
        return found

    def sorted_t(x, kind):
        return jnp.swapaxes(pick(x, perm[kind]), 0, 1)

    def summed(values, kind):
        count = len(values)
        src, dst = scan_a, scan_b
        for k in range(count):
            src[k, PAD : PAD + LANES, :] = values[k]
        for i, d in enumerate(STEPS):
            for k in range(count):
                dst[k, PAD : PAD + LANES, :] = (
                    src[k, PAD : PAD + LANES, :]
                    + src[k, PAD - d : PAD + LANES - d, :] * smask[kind, i]
                )
            src, dst = dst, src
        return [
            pick(jnp.swapaxes(src[k, PAD : PAD + LANES, :], 0, 1), endi[kind])
            for k in range(count)
        ]

    def put_points(values, first, dest):
        sums = jnp.concatenate([v * hit_p[...] for v in summed(values, 0)], axis=1)
        high = sums.astype(BF16)
        rest = sums - high.astype(F32)
        mid = rest.astype(BF16)
        low = (rest - mid.astype(F32)).astype(BF16)
        parts = jnp.concatenate([high, mid, low], axis=0)
        out = jnp.dot(onehot[...], parts, preferred_element_type=F32)
        for n in range(9):
            for m in range(3):
                dest[n, first + m] = out[
                    n * NBLK : (n + 1) * NBLK, m * LANES : (m + 1) * LANES
                ]

    def put_cams(values):
        for k, sums in enumerate(summed(values, 1)):
            top = lane_sum(sums * hit_c[0])
            bottom = lane_sum(sums * hit_c[1])
            camacc[k] = jnp.concatenate([top, bottom], axis=0)
        return camacc[...]

    def take_cams(vector, b):
        camvec[...] = vector
        rows = 32

        def one(chunk, carry):
            where = pl.ds(pl.multiple_of(chunk * rows, rows), rows)
            idx = idx_c[where, :]
            second = pair_m[where, :] == 1
            e0 = jnp.zeros((rows, LANES), F32)
            e1 = jnp.zeros((rows, LANES), F32)
            for k in range(CPAR):
                v = camvec[k]
                src = jnp.where(
                    second,
                    jnp.broadcast_to(v[1:2], (rows, LANES)),
                    jnp.broadcast_to(v[0:1], (rows, LANES)),
                )
                got = pick(src, idx)
                e0 = e0 + jc[k, where, :] * got
                e1 = e1 + jc[CPAR + k, where, :] * got
            gg[b, 0, where, :] = e0
            gg[b, 1, where, :] = e1
            return carry

        lax.fori_loop(0, TILES // rows, one, 0)

    def to_points(e0, e1):
        t0, t1 = sorted_t(e0, 0), sorted_t(e1, 0)
        return [jpt[m] * t0 + jpt[3 + m] * t1 for m in range(3)]

    def collect_start(comps, src, dst, send_sem, recv_sem):
        for r, n in ORDER:
            a, b = divmod(n, 3)

            @pl.when(here[n])
            def _(r=r, n=n, a=a, b=b):
                pltpu.make_async_remote_copy(
                    src_ref=src.at[n, pl.ds(0, comps)],
                    dst_ref=dst.at[r, pl.ds(0, comps)],
                    send_sem=send_sem.at[r],
                    recv_sem=recv_sem.at[r],
                    device_id=at(a - 1, b - 1),
                    device_id_type=MESH,
                ).start()

    def collect_wait(comps, src, dst, send_sem, recv_sem):
        for sem, flip in ((recv_sem, True), (send_sem, False)):
            for r, n in enumerate(OTHERS):

                @pl.when(here[8 - n] if flip else here[n])
                def _(r=r, n=n, sem=sem):
                    pltpu.make_async_copy(
                        src.at[n, pl.ds(0, comps)], dst.at[r, pl.ds(0, comps)], sem.at[r]
                    ).wait()

        total = []
        for m in range(comps):
            s = src[4, m]
            for r in range(8):
                s = s + dst[r, m]
            total.append(s)
        return total

    pts = (contrib, recv_c, cs_sem, cr_sem)
    pts_y = (contrib_y, recv_y, ys_sem, yr_sem)
    out_s = (wsrc, recv_s, ss_sem, sr_sem)
    out_w = (wsrc_w, recv_w, ws_sem, wr_sem)
    out_2 = (wsrc_2, recv_2, s2_sem, r2_sem)

    def spread_start(values, src, dst, send_sem, recv_sem):
        for m, v in enumerate(values):
            src[m] = v
            dst[4, m] = v
        for r, n in ORDER:
            a, b = divmod(n, 3)

            @pl.when(here[n])
            def _(r=r, n=n, a=a, b=b):
                pltpu.make_async_remote_copy(
                    src_ref=src,
                    dst_ref=dst.at[8 - n],
                    send_sem=send_sem.at[r],
                    recv_sem=recv_sem.at[r],
                    device_id=at(a - 1, b - 1),
                    device_id_type=MESH,
                ).start()

    def spread_wait(src, dst, send_sem, recv_sem):
        for sem, flip in ((recv_sem, True), (send_sem, False)):
            for r, n in enumerate(OTHERS):

                @pl.when(here[8 - n] if flip else here[n])
                def _(r=r, n=n, sem=sem):
                    pltpu.make_async_copy(src, dst.at[8 - n], sem.at[r]).wait()

    def take_points(src, first=0):
        def one(chunk, carry):
            for i in range(8):
                t = chunk * 8 + i
                slot = slot_s[t]
                n = slot >> 4
                q = slot & 15
                for m in range(3):
                    table[m, pl.ds(t, 1), :] = src[n, first + m, pl.ds(q, 1), :]
            return carry

        lax.fori_loop(0, TILES // 8, one, 0)
        return [pick(table[m], obs_pt[...]) for m in range(3)]

    def eliminate(e0, e1, near, b):
        bk[b, 0] = e0 - (jp[0] * near[0] + jp[1] * near[1] + jp[2] * near[2])
        bk[b, 1] = e1 - (jp[3] * near[0] + jp[4] * near[1] + jp[5] * near[2])

    def back_to_cams(b):
        t0, t1 = sorted_t(bk[b, 0], 1), sorted_t(bk[b, 1], 1)
        return put_cams([jct[k] * t0 + jct[CPAR + k] * t1 for k in range(CPAR)])

    def lane_row(rows):
        held = jnp.concatenate(rows + [jnp.zeros((8 - len(rows), LANES), F32)], axis=0)
        sums = jnp.sum(held, axis=1, keepdims=True)
        own = lax.broadcasted_iota(jnp.int32, (8, LANES), 0)
        return jnp.sum(jnp.where(lane_ids(8) == own, sums, 0.0), axis=0, keepdims=True)

    def apart(row):
        lane1 = lane_ids(1)
        return [
            jnp.sum(jnp.where(lane1 == i, row, 0.0), axis=1, keepdims=True) for i in range(8)
        ]

    def pass_start(src, dst, spot, peers, send_sem, recv_sem):
        for dx, dy in peers:
            pltpu.make_async_remote_copy(
                src_ref=src,
                dst_ref=dst.at[pl.ds(spot, 1)],
                send_sem=send_sem,
                recv_sem=recv_sem,
                device_id=at(dx, dy),
                device_id_type=MESH,
            ).start()

    def hidden_start(a, rows):
        row = lane_row(rows)
        px_src[a] = row
        px_dst[a, pl.ds(me_x, 1), :] = row
        peers = [(d, 0) for d in (4, 3, 5, 2, 6, 1, 7)]
        pass_start(px_src.at[a], px_dst.at[a], me_x, peers, pxs_sem.at[a], pxr_sem.at[a])

    def hidden_turn(a):
        rest = px_dst.at[a, pl.ds(0, GX - 1)]
        pltpu.make_async_copy(rest, rest, pxr_sem.at[a]).wait()
        row = jnp.sum(px_dst[a], axis=0, keepdims=True)
        py_src[a] = row
        py_dst[a, pl.ds(me_y, 1), :] = row
        peers = [(0, d) for d in (8, 7, 9, 6, 10, 5, 11, 4, 12, 3, 13, 2, 14, 1, 15)]
        pass_start(py_src.at[a], py_dst.at[a], me_y, peers, pys_sem.at[a], pyr_sem.at[a])

    def hidden_wait(a):
        rest = py_dst.at[a, pl.ds(0, GY - 1)]
        pltpu.make_async_copy(rest, rest, pyr_sem.at[a]).wait()
        return apart(jnp.sum(py_dst[a], axis=0, keepdims=True))

    def hidden_drain(a):
        rest = px_dst.at[a, pl.ds(0, GX - 1)]
        pltpu.make_async_copy(rest, rest, pxs_sem.at[a]).wait()
        rest = py_dst.at[a, pl.ds(0, GY - 1)]
        pltpu.make_async_copy(rest, rest, pys_sem.at[a]).wait()

    def total_start(a, rows):
        row = lane_row(rows)
        ar_src[a] = row
        arx[a, pl.ds(me, 1), :] = row

        def send(dx, dy):
            pltpu.make_async_remote_copy(
                src_ref=ar_src.at[a],
                dst_ref=arx.at[a, pl.ds(me, 1)],
                send_sem=as_sem.at[a],
                recv_sem=ar_sem.at[a],
                device_id=at(dx, dy),
                device_id_type=MESH,
            ).start()

        to_all(send)

    def total_wait(a):
        pltpu.make_async_copy(
            arx.at[a, pl.ds(0, 127)], arx.at[a, pl.ds(0, 127)], ar_sem.at[a]
        ).wait()
        return apart(jnp.sum(arx[a], axis=0, keepdims=True))

    def total_drain(a):
        pltpu.make_async_copy(
            arx.at[a, pl.ds(0, 127)], arx.at[a, pl.ds(0, 127)], as_sem.at[a]
        ).wait()

    copies[0].wait()
    hit_p[...] = jnp.where(order(0, obs_pt[...], lane), 1.0, 0.0)
    for copy in copies[1:]:
        copy.wait()
    slot_row = lax.broadcasted_iota(jnp.int32, (SLOTS, TILES), 0)
    hot = jnp.where(slot_row == tpts_r[...], 1.0, 0.0).astype(BF16)
    for i in range(3):
        onehot[:, i * TILES : (i + 1) * TILES] = hot
    tcam = column(tcam_r[...]).astype(jnp.int32)
    parity = tcam & 1
    pair = tcam >> 1
    pair_m[...] = pair
    idx_c[...] = parity * 64 + obs_cam[...]

    valid = jnp.where(lane < column(count_r[...]).astype(jnp.int32), 1.0, 0.0)
    for k in range(2):
        rs[k] = rs_in[pl.ds(k, TILES, stride=2), :] * valid
    for k in range(6):
        jp[k] = jp[k] * valid
        jpt[k] = sorted_t(jp[k], 0)
    for k in range(18):
        jc[k] = jc[k] * valid
    square = [jpt[i] * jpt[j] + jpt[3 + i] * jpt[3 + j] for i, j in PAIRS]
    put_points(square[0:3], 0, contrib)
    put_points(square[3:6], 3, contrib)

    start = jnp.concatenate(
        [
            jnp.concatenate([start_r[:, 2 * p, :], start_r[:, 2 * p + 1, :]], axis=1)[:, None, :]
            for p in range(2)
        ],
        axis=1,
    )
    take_cams(start, 0)
    for k in range(2):
        mv[k] = rs[k] + gg[0, k]
    put_points(to_points(mv[0], mv[1]), 6, contrib)
    pl.semaphore_wait(barrier, GX * GY - 1)
    collect_start(9, *pts)
    put_points(to_points(gg[0, 0], gg[0, 1]), 0, contrib_y)
    collect_start(3, *pts_y)
    found = order(1, obs_cam[...], lane & 63)
    mine = found & ((lane >> 6) == parity)
    hit_c[0] = jnp.where(mine & (pair == 0), 1.0, 0.0)
    hit_c[1] = jnp.where(mine & (pair == 1), 1.0, 0.0)
    for k in range(18):
        jct[k] = sorted_t(jc[k], 1)
    diag = put_cams([jct[k] * jct[k] + jct[CPAR + k] * jct[CPAR + k] for k in range(CPAR)])
    cost_row = lane_sum(rs[...] * rs[...])
    owned = collect_wait(9, *pts)
    for c in range(6):
        hess_b[c] = owned[c]
    ybuf[0] = jnp.stack(owned[6:9])

    costs = []
    update = start
    upd_sum = jnp.zeros_like(start)
    step_sum = jnp.zeros((3, NBLK, LANES), F32)

    def weighted(w):
        h = [hess_b[c] for c in range(6)]
        return [
            h[0] * w[0] + h[1] * w[1] + h[2] * w[2],
            h[1] * w[0] + h[3] * w[1] + h[4] * w[2],
            h[2] * w[0] + h[4] * w[1] + h[5] * w[2],
        ]

    def inner(u, v):
        return lane_sum(u[0] * v[0] + u[1] * v[1] + u[2] * v[2])

    def three(buf, b):
        return [buf[b, m] for m in range(3)]

    def mix(p, u, q, v):
        return [p * u[m] + q * v[m] for m in range(3)]

    inv = invert([hess_b[c] for c in range(6)], LAMBDAS[0])
    for c in range(6):
        inv_b[c] = inv[c]
    w0 = apply_inverse(inv, three(ybuf, 0))
    wbuf[0] = jnp.stack(w0)
    spread_start(w0, *out_s)
    spread_wait(*out_s)
    near = take_points(recv_s)

    for step in range(2):
        damping = LAMBDAS[step]
        last = step == 1
        cam_damp = damping * (diag + 1.0)
        precond = diag + cam_damp
        if step == 0:
            eliminate(mv[0], mv[1], near, 0)
        r0 = -back_to_cams(0) - cam_damp * update
        z0 = r0 / precond

        take_cams(z0, 1)
        put_points(to_points(gg[1, 0], gg[1, 1]), 0, contrib)
        collect_start(3, *pts)
        if last:
            spread_wait(*out_2)
            near = take_points(recv_2)
            for r in range(2):
                shift = jp[3 * r] * near[0] + jp[3 * r + 1] * near[1] + jp[3 * r + 2] * near[2]
                res = rs[r] - cb * shift
                rs[r] = res
                mv[r] = mv[r] + res
            cost_row = lane_sum(rs[...] * rs[...])
        y = collect_wait(3, *pts)
        ybuf[1] = jnp.stack(y)
        w = apply_inverse([inv_b[c] for c in range(6)], y)
        wbuf[1] = jnp.stack(w)
        spread_start(w, *out_s)
        spread_wait(*out_s)
        near = take_points(recv_s)
        eliminate(gg[1, 0], gg[1, 1], near, 1)
        c0 = back_to_cams(1) + cam_damp * z0
        u = c0 / precond
        hidden_start(step, [lane_sum(r0 * z0), lane_sum(z0 * c0), lane_sum(c0 * u), cost_row])
        take_cams(u, 2)
        put_points(to_points(gg[2, 0], gg[2, 1]), 0, contrib)
        collect_start(3, *pts)
        hidden_turn(step)
        y = collect_wait(3, *pts)
        ybuf[2] = jnp.stack(y)
        w = apply_inverse([inv_b[c] for c in range(6)], y)
        wbuf[2] = jnp.stack(w)
        if last:
            spread_start(w, *out_s)

        dots = hidden_wait(step)
        resid_dot, curve, square = dots[0], dots[1], dots[2]
        costs.append(0.5 * dots[3])
        alpha = resid_dot / curve
        beta = (resid_dot - 2.0 * alpha * curve + alpha * alpha * square) / resid_dot
        more = 1.0 + beta
        z1 = (r0 - alpha * c0) / precond
        d1 = z1 + beta * z0
        turn = [more * gg[1, r] - alpha * gg[2, r] for r in range(2)]
        y_turn = mix(more, three(ybuf, 1), -alpha, three(ybuf, 2))
        w_turn = mix(more, three(wbuf, 1), -alpha, three(wbuf, 2))
        turn_sq = lane_sum(turn[0] * turn[0] + turn[1] * turn[1])
        yw = inner(y_turn, w_turn)
        rows = [
            lane_sum((r0 - alpha * c0) * z1),
            turn_sq - yw + lane_sum(cam_damp * (d1 * d1)),
        ]
        if last:
            base = [mv[r] + alpha * gg[1, r] for r in range(2)]
            y_base = mix(1.0, three(ybuf, 0), alpha, three(ybuf, 1))
            w_base = mix(1.0, three(wbuf, 0), alpha, three(wbuf, 1))
            hw_base = weighted(w_base)
            hw_turn = weighted(w_turn)
            rows += [
                lane_sum(base[0] * base[0] + base[1] * base[1])
                - 2.0 * inner(y_base, w_base)
                + inner(w_base, hw_base),
                lane_sum(base[0] * turn[0] + base[1] * turn[1])
                - inner(y_base, w_turn)
                - inner(y_turn, w_base)
                + inner(w_base, hw_turn),
                turn_sq - 2.0 * yw + inner(w_turn, hw_turn),
            ]
        if not last:
            hess = [hess_b[c] for c in range(6)]
            inv = invert(hess, LAMBDAS[1])
            for c in range(6):
                inv_b[c] = inv[c]
            scale = [damping * (hess[c] + 1.0) for c in (0, 3, 5)]
            held = []
            for b in range(3):
                held.append([scale[m] * wbuf[b, m] + ybuf[b, m] for m in range(3)])
            y_start = collect_wait(3, *pts_y)
            y_fix = [
                scale[m] * wbuf[0, m] + y_start[m] + alpha * held[1][m] for m in range(3)
            ]
            y_move = mix(more, held[1], -alpha, held[2])
            w_fix = apply_inverse(inv, y_fix)
            w_move = apply_inverse(inv, y_move)
            spread_start(w_fix + mix(1.0, w_move, -alpha, w), *out_w)
            total_start(step, rows)
            spread_start(w, *out_2)
            spread_wait(*out_w)
            near_fix = take_points(recv_w)
            near_move = take_points(recv_w, 3)
        else:
            total_start(step, rows)
            spread_wait(*out_s)
            near = take_points(recv_s)
            eliminate(gg[2, 0], gg[2, 1], near, 2)
        dots = total_wait(step)
        alpha1 = dots[0] / dots[1]
        ca = alpha + alpha1 * more
        cb = -(alpha1 * alpha)
        update = update + alpha * z0 + alpha1 * d1
        upd_sum = upd_sum + update
        step_sum = step_sum - (wbuf[0] + ca * wbuf[1] + cb * wbuf[2])
        if not last:
            near = [near_fix[m] + alpha1 * near_move[m] for m in range(3)]
            for r in range(2):
                rs[r] = bk[0, r] + ca * bk[1, r] + cb * gg[2, r]
                mv[r] = gg[0, r] + ca * gg[1, r] + cb * gg[2, r]
            eliminate(rs[0] + mv[0], rs[1] + mv[1], near, 0)
            ybuf[0] = jnp.stack(mix(1.0, y_fix, alpha1, y_move))
            wbuf[0] = jnp.stack(mix(1.0, w_fix, alpha1, w_move))
        else:
            for r in range(2):
                res_o[pl.ds(r, TILES, stride=2), :] = bk[0, r] + ca * bk[1, r] + cb * bk[2, r]
            costs.append(0.5 * (dots[2] + 2.0 * alpha1 * dots[3] + alpha1 * alpha1 * dots[4]))
    for p in range(2):
        both = upd_sum[:, p, :]
        cam_o[:, 2 * p, :] = cam_r[:, 2 * p, :] + both[:, 0:64]
        cam_o[:, 2 * p + 1, :] = cam_r[:, 2 * p + 1, :] + both[:, 64:128]
    pt_o[...] = pt_r[...] + step_sum
    third = lax.broadcasted_iota(jnp.int32, (1, 3), 1)
    cost_o[...] = jnp.where(third == 0, costs[0], jnp.where(third == 1, costs[1], costs[2]))
    for a in range(2):
        hidden_drain(a)
        total_drain(a)


def hand_over(cam_i, pt_i, res_i, cost_i, cam_o, pt_o, res_o, cost_o):
    res_o[...] = res_i[...]
    cam_o[...] = cam_i[...]
    pt_o[...] = pt_i[...]
    cost_o[...] = cost_i[...]


def body(
    jac_cam,
    jac_pt,
    resid0,
    obs_count,
    tile_camera,
    tile_points,
    obs_camera,
    obs_point,
    cam_params,
    pt_params,
    cg_start,
):
    vmem = pl.BlockSpec(memory_space=pltpu.VMEM)
    hbm = pl.BlockSpec(memory_space=pltpu.HBM)
    big = (TILES, LANES)
    blk = (NBLK, LANES)
    dma = pltpu.SemaphoreType.DMA
    shapes = [
        jax.ShapeDtypeStruct((CPAR, 4, 64), F32),
        jax.ShapeDtypeStruct((3,) + blk, F32),
        jax.ShapeDtypeStruct((2 * TILES, LANES), F32),
        jax.ShapeDtypeStruct((1, 3), F32),
    ]
    results = pl.pallas_call(
        kernel,
        out_shape=shapes,
        in_specs=[pl.BlockSpec(memory_space=pltpu.SMEM)] + [hbm] * 11,
        out_specs=[vmem] * 4,
        scratch_shapes=[
            pltpu.VMEM((18,) + big, F32),
            pltpu.VMEM((6,) + big, F32),
            pltpu.VMEM((2,) + big, F32),
            pltpu.VMEM((2 * TILES, LANES), F32),
            pltpu.VMEM(big, jnp.int32),
            pltpu.VMEM(big, jnp.int32),
            pltpu.VMEM((1, LANES), jnp.int32),
            pltpu.VMEM((1, LANES), jnp.int32),
            pltpu.VMEM((1, LANES), jnp.int32),
            pltpu.VMEM((CPAR, 4, 64), F32),
            pltpu.VMEM((CPAR, 4, 64), F32),
            pltpu.VMEM((3,) + blk, F32),
            pltpu.VMEM((18,) + big, F32),
            pltpu.VMEM((6,) + big, F32),
            pltpu.VMEM((PAD + LANES, LANES), F32),
            pltpu.VMEM((CPAR, PAD + LANES, LANES), F32),
            pltpu.VMEM((CPAR, PAD + LANES, LANES), F32),
            pltpu.VMEM((2,) + big, jnp.int32),
            pltpu.VMEM((2,) + big, jnp.int32),
            pltpu.VMEM((2, 7) + big, F32),
            pltpu.VMEM(big, F32),
            pltpu.VMEM((2,) + big, F32),
            pltpu.VMEM(big, jnp.int32),
            pltpu.VMEM(big, jnp.int32),
            pltpu.VMEM((SLOTS, 3 * TILES), BF16),
            pltpu.VMEM((3,) + big, F32),
            pltpu.VMEM((3, 2) + big, F32),
            pltpu.VMEM((3, 2) + big, F32),
            pltpu.VMEM((2,) + big, F32),
            pltpu.VMEM((9, 9) + blk, F32),
            pltpu.VMEM((8, 9) + blk, F32),
            pltpu.VMEM((9, 3) + blk, F32),
            pltpu.VMEM((8, 3) + blk, F32),
            pltpu.VMEM((3,) + blk, F32),
            pltpu.VMEM((9, 3) + blk, F32),
            pltpu.VMEM((6,) + blk, F32),
            pltpu.VMEM((9, 6) + blk, F32),
            pltpu.VMEM((3,) + blk, F32),
            pltpu.VMEM((9, 3) + blk, F32),
            pltpu.VMEM((6,) + blk, F32),
            pltpu.VMEM((6,) + blk, F32),
            pltpu.VMEM((3, 3) + blk, F32),
            pltpu.VMEM((3, 3) + blk, F32),
            pltpu.VMEM((CPAR, 2, LANES), F32),
            pltpu.VMEM((CPAR, 2, LANES), F32),
            pltpu.VMEM((2, 1, LANES), F32),
            pltpu.VMEM((2, GX * GY, LANES), F32),
            pltpu.VMEM((2, 1, LANES), F32),
            pltpu.VMEM((2, GX, LANES), F32),
            pltpu.VMEM((2, 1, LANES), F32),
            pltpu.VMEM((2, GY, LANES), F32),
            dma((11,)),
        ]
        + [dma((8,))] * 10
        + [dma((2,))] * 6,
        compiler_params=pltpu.CompilerParams(
            collective_id=0, has_side_effects=True, vmem_limit_bytes=62 * 1024 * 1024
        ),
    )(
        tile_points[0, 0],
        jnp.transpose(jac_cam[0, 0], (1, 0, 2)),
        jnp.transpose(jac_pt[0, 0], (1, 0, 2)),
        resid0.reshape(2 * TILES, LANES),
        obs_camera[0, 0],
        obs_point[0, 0],
        obs_count[0],
        tile_camera[0],
        tile_points[0],
        jnp.transpose(cg_start[0, 0], (1, 0, 2)),
        jnp.transpose(cam_params[0, 0], (1, 0, 2)),
        jnp.transpose(pt_params[0, 0], (1, 0, 2)),
    )
    cam, pt, res, costs = pl.pallas_call(
        hand_over,
        out_shape=shapes,
        in_specs=[vmem] * 4,
        out_specs=[vmem] * 4,
    )(*results)
    cam_out = jnp.transpose(cam, (1, 0, 2))[None, None]
    pt_out = jnp.transpose(pt, (1, 0, 2))[None, None]
    return cam_out, pt_out, res.reshape(1, 1, TILES, 2, LANES), costs.reshape(3)


def solution(mesh):
    wide = P("gx", "gy", None, None, None)
    in_specs = (
        wide,
        wide,
        wide,
        P("gx", "gy", None),
        P("gx", "gy", None),
        P("gx", "gy", None),
        P("gx", "gy", None, None),
        P("gx", "gy", None, None),
        wide,
        wide,
        wide,
    )
    out_specs = (wide, wide, wide, P())
    return jax.shard_map(body, mesh=mesh, in_specs=in_specs, out_specs=out_specs, check_vma=False)
```

```python
import jax
import jax.numpy as jnp
from jax import lax
from jax.experimental import pallas as pl
from jax.experimental.pallas import tpu as pltpu
from jax.sharding import PartitionSpec as P

MESH = pl.DeviceIdType.MESH
CPAR = 9
NBLK = 16
LANES = 128
TILES = 128
SLOTS = 9 * NBLK
GX = 8
GY = 16
PAD = 64
STEPS = (1, 2, 4, 8, 16, 32, 64)
LAMBDAS = (1.0, 0.25)
PAIRS = ((0, 0), (0, 1), (0, 2), (1, 1), (1, 2), (2, 2))
OTHERS = (0, 1, 2, 3, 5, 6, 7, 8)
ORDER = tuple((OTHERS.index(n), n) for n in (0, 2, 6, 8, 3, 5, 1, 7))
F32 = jnp.float32
BF16 = jnp.bfloat16
GATHER = lax.GatherDimensionNumbers(
    offset_dims=(),
    collapsed_slice_dims=(1,),
    start_index_map=(1,),
    operand_batching_dims=(0,),
    start_indices_batching_dims=(0,),
)


def pick(x, idx):
    return lax.gather(
        x, idx[:, :, None], GATHER, (1, 1), mode=lax.GatherScatterMode.PROMISE_IN_BOUNDS
    )


def lane_ids(rows):
    return lax.broadcasted_iota(jnp.int32, (rows, LANES), 1)


def sort_lanes(key):
    flat = jnp.swapaxes(key.astype(F32), 0, 1).reshape(16, 8, LANES)
    regs = [flat[v] for v in range(16)]
    sub = lax.broadcasted_iota(jnp.int32, (8, LANES), 0)
    before = None
    size = 2
    while size <= LANES:
        if size >= 16:
            bit = size // 16
            sign = jnp.where((sub & bit) == 0, 1.0, -1.0)
            turn = sign if before is None else sign * before
            regs = [x * turn for x in regs]
            before = sign
        gap = size // 2
        while gap >= 1:
            if gap < 16:
                for v in range(16):
                    if v & gap == 0:
                        low = jnp.minimum(regs[v], regs[v + gap])
                        high = jnp.maximum(regs[v], regs[v + gap])
                        up = size >= 16 or v & size == 0
                        regs[v], regs[v + gap] = (low, high) if up else (high, low)
            else:
                g = gap // 16
                first = (sub & g) == 0
                for v in range(16):
                    x = regs[v]
                    other = jnp.where(
                        first, pltpu.roll(x, 8 - g, axis=0), pltpu.roll(x, g, axis=0)
                    )
                    regs[v] = jnp.where(first, jnp.minimum(x, other), jnp.maximum(x, other))
            gap //= 2
        size *= 2
    rows = jnp.swapaxes(jnp.concatenate(regs, axis=0), 0, 1)
    lane = lane_ids(LANES)
    return pick(rows, (lane & 15) * 8 + (lane >> 4)).astype(jnp.int32)


def last_at_most(seg, target):
    count = jnp.zeros_like(target)
    for step in (64, 32, 16, 8, 4, 2, 1):
        count = jnp.where(pick(seg, count + (step - 1)) <= target, count + step, count)
    return jnp.where(pick(seg, count) <= target, count + 1, count)


def column(row):
    return jnp.swapaxes(jnp.broadcast_to(row.astype(F32), (LANES, LANES)), 0, 1)


def invert(hess, damping):
    h00 = hess[0] + damping * (hess[0] + 1.0)
    h01, h02 = hess[1], hess[2]
    h11 = hess[3] + damping * (hess[3] + 1.0)
    h12 = hess[4]
    h22 = hess[5] + damping * (hess[5] + 1.0)
    c00 = h11 * h22 - h12 * h12
    c01 = h02 * h12 - h01 * h22
    c02 = h01 * h12 - h02 * h11
    c11 = h00 * h22 - h02 * h02
    c12 = h01 * h02 - h00 * h12
    c22 = h00 * h11 - h01 * h01
    det = h00 * c00 + h01 * c01 + h02 * c02
    return [c / det for c in (c00, c01, c02, c11, c12, c22)]


def apply_inverse(inv, y):
    return [
        inv[0] * y[0] + inv[1] * y[1] + inv[2] * y[2],
        inv[1] * y[0] + inv[3] * y[1] + inv[4] * y[2],
        inv[2] * y[0] + inv[4] * y[1] + inv[5] * y[2],
    ]


def lane_sum(x):
    while x.ndim > 2:
        x = jnp.sum(x, axis=0)
    return jnp.sum(x, axis=0, keepdims=True)


def kernel(
    slot_s,
    jc_h,
    jp_h,
    rs_h,
    cam_h,
    pt_h,
    count_h,
    tcam_h,
    tpts_h,
    start_h,
    cpar_h,
    ppar_h,
    cam_o,
    pt_o,
    res_o,
    cost_o,
    jc,
    jp,
    rs,
    rs_in,
    obs_cam,
    obs_pt,
    count_r,
    tcam_r,
    tpts_r,
    start_r,
    cam_r,
    pt_r,
    jct,
    jpt,
    seg_t,
    scan_a,
    scan_b,
    perm,
    endi,
    smask,
    hit_p,
    hit_c,
    pair_m,
    valid_m,
    idx_c,
    onehot,
    table,
    gg,
    bk,
    mv,
    contrib,
    recv_c,
    contrib_h,
    recv_h,
    contrib_y,
    recv_y,
    wsrc,
    recv_s,
    wsrc_w,
    recv_w,
    wsrc_2,
    recv_2,
    hess_b,
    inv_b,
    ybuf,
    wbuf,
    camvec,
    camacc,
    ar_src,
    arx,
    px_src,
    px_dst,
    py_src,
    py_dst,
    in_sem,
    row_s,
    cs_sem,
    cr_sem,
    hs_sem,
    hr_sem,
    ys_sem,
    yr_sem,
    ss_sem,
    sr_sem,
    ws_sem,
    wr_sem,
    s2_sem,
    r2_sem,
    as_sem,
    ar_sem,
    pxs_sem,
    pxr_sem,
    pys_sem,
    pyr_sem,
):
    me_x = lax.axis_index("gx")
    me_y = lax.axis_index("gy")

    def at(dx, dy):
        return (lax.rem(me_x + (dx + GX), GX), lax.rem(me_y + (dy + GY), GY))

    me = me_x * GY + me_y
    here = {}
    for n in OTHERS:
        a, b = divmod(n, 3)
        x, y = me_x + (a - 1), me_y + (b - 1)
        here[n] = (x >= 0) & (x < GX) & (y >= 0) & (y < GY)

    def to_all(act):
        def row(j, carry):
            dy = lax.rem(j + 5, GY - 1) + 1
            for dx in (4, 3, 5, 2, 6, 1, 7, 0):
                act(dx, dy)
            return carry

        lax.fori_loop(0, GY - 1, row, 0)
        for dx in (4, 3, 5, 2, 6, 1, 7):
            act(dx, 0)

    pairs = [
        (pt_h, obs_pt),
        (jp_h, jp),
        (jc_h, jc),
        (cam_h, obs_cam),
        (rs_h, rs_in),
        (tcam_h, tcam_r),
        (count_h, count_r),
        (tpts_h, tpts_r),
        (start_h, start_r),
        (cpar_h, cam_r),
        (ppar_h, pt_r),
    ]
    copies = [
        pltpu.make_async_copy(src, dst, in_sem.at[i]) for i, (src, dst) in enumerate(pairs)
    ]
    for copy in copies:
        copy.start()

    for r, n in enumerate(OTHERS):

        @pl.when(jnp.logical_not(here[n]))
        def _(r=r, n=n):
            recv_c[r] = jnp.zeros_like(recv_c[r])
            recv_h[r] = jnp.zeros_like(recv_h[r])
            recv_y[r] = jnp.zeros_like(recv_y[r])
            for buf in (recv_s, recv_w, recv_2):
                per = buf.shape[0] // 9
                buf[n * per : (n + 1) * per, :] = jnp.zeros((per, LANES), F32)

    barrier = pltpu.get_barrier_semaphore()
    greeted = [(-1, -1), (-1, 1), (1, -1), (1, 1)]
    greeted += [(0, d) for d in range(1, GY)] + [(d, 0) for d in range(1, GX)]
    for dx, dy in greeted:
        pl.semaphore_signal(barrier, inc=1, device_id=at(dx, dy), device_id_type=MESH)

    seg_t[0:PAD, :] = jnp.full((PAD, LANES), -1.0, F32)
    for k in range(CPAR):
        scan_a[k, 0:PAD, :] = jnp.zeros((PAD, LANES), F32)
        scan_b[k, 0:PAD, :] = jnp.zeros((PAD, LANES), F32)
    lane = lane_ids(TILES)

    def order(kind, ids, target):
        key = sort_lanes(ids * LANES + lane)
        perm[kind] = key & (LANES - 1)
        seg = key >> 7
        count = last_at_most(seg, target)
        last = jnp.maximum(count - 1, 0)
        endi[kind] = last
        found = (count > 0) & (pick(seg, last) == target)
        seg_t[PAD : PAD + LANES, :] = jnp.swapaxes(seg.astype(F32), 0, 1)
        for i, d in enumerate(STEPS):
            same = seg_t[PAD : PAD + LANES, :] == seg_t[PAD - d : PAD + LANES - d, :]
            smask[kind, i] = jnp.where(same, 1.0, 0.0)
        return found

    def sorted_t(x, kind):
        return jnp.swapaxes(pick(x, perm[kind]), 0, 1)

    def summed(values, kind):
        count = len(values)
        src, dst = scan_a, scan_b
        for k in range(count):
            src[k, PAD : PAD + LANES, :] = values[k]
        for i, d in enumerate(STEPS):
            for k in range(count):
                dst[k, PAD : PAD + LANES, :] = (
                    src[k, PAD : PAD + LANES, :]
                    + src[k, PAD - d : PAD + LANES - d, :] * smask[kind, i]
                )
            src, dst = dst, src
        return [
            pick(jnp.swapaxes(src[k, PAD : PAD + LANES, :], 0, 1), endi[kind])
            for k in range(count)
        ]

    def put_points(values, dest):
        sums = jnp.concatenate([v * hit_p[...] for v in summed(values, 0)], axis=1)
        high = sums.astype(BF16)
        rest = sums - high.astype(F32)
        mid = rest.astype(BF16)
        low = (rest - mid.astype(F32)).astype(BF16)
        parts = jnp.concatenate([high, mid, low], axis=0)
        out = jnp.dot(onehot[...], parts, preferred_element_type=F32)
        for n in range(9):
            for m in range(len(values)):
                dest[n, m] = out[n * NBLK : (n + 1) * NBLK, m * LANES : (m + 1) * LANES]

    def put_cams(values):
        for k, sums in enumerate(summed(values, 1)):
            top = lane_sum(sums * hit_c[0])
            bottom = lane_sum(sums * hit_c[1])
            camacc[k] = jnp.concatenate([top, bottom], axis=0)
        return camacc[...]

    def take_cams(vector, b):
        camvec[...] = vector
        rows = 32

        def one(chunk, carry):
            where = pl.ds(pl.multiple_of(chunk * rows, rows), rows)
            idx = idx_c[where, :]
            second = pair_m[where, :] == 1
            e0 = jnp.zeros((rows, LANES), F32)
            e1 = jnp.zeros((rows, LANES), F32)
            for k in range(CPAR):
                v = camvec[k]
                src = jnp.where(
                    second,
                    jnp.broadcast_to(v[1:2], (rows, LANES)),
                    jnp.broadcast_to(v[0:1], (rows, LANES)),
                )
                got = pick(src, idx)
                e0 = e0 + jc[k, where, :] * got
                e1 = e1 + jc[CPAR + k, where, :] * got
            gg[b, 0, where, :] = e0 * valid_m[where, :]
            gg[b, 1, where, :] = e1 * valid_m[where, :]
            return carry

        lax.fori_loop(0, TILES // rows, one, 0)

    def to_points(e0, e1):
        t0, t1 = sorted_t(e0, 0), sorted_t(e1, 0)
        return [jpt[m] * t0 + jpt[3 + m] * t1 for m in range(3)]

    def collect_start(comps, src, dst, send_sem, recv_sem):
        for r, n in ORDER:
            a, b = divmod(n, 3)

            @pl.when(here[n])
            def _(r=r, n=n, a=a, b=b):
                pltpu.make_async_remote_copy(
                    src_ref=src.at[n, pl.ds(0, comps)],
                    dst_ref=dst.at[r, pl.ds(0, comps)],
                    send_sem=send_sem.at[r],
                    recv_sem=recv_sem.at[r],
                    device_id=at(a - 1, b - 1),
                    device_id_type=MESH,
                ).start()

    def collect_wait(comps, src, dst, send_sem, recv_sem):
        for sem, flip in ((recv_sem, True), (send_sem, False)):
            for r, n in enumerate(OTHERS):

                @pl.when(here[8 - n] if flip else here[n])
                def _(r=r, n=n, sem=sem):
                    pltpu.make_async_copy(
                        src.at[n, pl.ds(0, comps)], dst.at[r, pl.ds(0, comps)], sem.at[r]
                    ).wait()

        total = []
        for m in range(comps):
            s = src[4, m]
            for r in range(8):
                s = s + dst[r, m]
            total.append(s)
        return total

    pts = (contrib, recv_c, cs_sem, cr_sem)
    pts_h = (contrib_h, recv_h, hs_sem, hr_sem)
    pts_y = (contrib_y, recv_y, ys_sem, yr_sem)
    out_s = (wsrc, recv_s, ss_sem, sr_sem)
    out_w = (wsrc_w, recv_w, ws_sem, wr_sem)
    out_2 = (wsrc_2, recv_2, s2_sem, r2_sem)

    def spread_start(values, src, dst, send_sem, recv_sem):
        per = src.shape[0]
        for m, v in enumerate(values):
            src[m * NBLK : (m + 1) * NBLK, :] = v
            dst[4 * per + m * NBLK : 4 * per + (m + 1) * NBLK, :] = v
        for r, n in ORDER:
            a, b = divmod(n, 3)

            @pl.when(here[n])
            def _(r=r, n=n, a=a, b=b):
                pltpu.make_async_remote_copy(
                    src_ref=src,
                    dst_ref=dst.at[pl.ds((8 - n) * per, per)],
                    send_sem=send_sem.at[r],
                    recv_sem=recv_sem.at[r],
                    device_id=at(a - 1, b - 1),
                    device_id_type=MESH,
                ).start()

    def spread_wait(src, dst, send_sem, recv_sem):
        per = src.shape[0]
        for sem, flip in ((recv_sem, True), (send_sem, False)):
            for r, n in enumerate(OTHERS):

                @pl.when(here[8 - n] if flip else here[n])
                def _(r=r, n=n, sem=sem):
                    pltpu.make_async_copy(
                        src, dst.at[pl.ds((8 - n) * per, per)], sem.at[r]
                    ).wait()

    def take_points(src, first=0):
        per = src.shape[0] // 9

        def one(chunk, carry):
            for i in range(16):
                t = chunk * 16 + i
                row = row_s[0 if per == 3 * NBLK else 1, t] + first * NBLK
                for m in range(3):
                    table[m, pl.ds(t, 1), :] = src[pl.ds(row + m * NBLK, 1), :]
            return carry

        lax.fori_loop(0, TILES // 16, one, 0)
        return [pick(table[m], obs_pt[...]) for m in range(3)]

    def eliminate(e0, e1, near, b):
        bk[b, 0] = e0 - (jp[0] * near[0] + jp[1] * near[1] + jp[2] * near[2])
        bk[b, 1] = e1 - (jp[3] * near[0] + jp[4] * near[1] + jp[5] * near[2])

    def back_to_cams(b):
        t0, t1 = sorted_t(bk[b, 0], 1), sorted_t(bk[b, 1], 1)
        return put_cams([jct[k] * t0 + jct[CPAR + k] * t1 for k in range(CPAR)])

    def lane_row(rows):
        held = jnp.concatenate(rows + [jnp.zeros((8 - len(rows), LANES), F32)], axis=0)
        sums = jnp.sum(held, axis=1, keepdims=True)
        own = lax.broadcasted_iota(jnp.int32, (8, LANES), 0)
        return jnp.sum(jnp.where(lane_ids(8) == own, sums, 0.0), axis=0, keepdims=True)

    def apart(row):
        lane1 = lane_ids(1)
        return [
            jnp.sum(jnp.where(lane1 == i, row, 0.0), axis=1, keepdims=True) for i in range(8)
        ]

    def pass_start(src, dst, spot, peers, send_sem, recv_sem):
        for dx, dy in peers:
            pltpu.make_async_remote_copy(
                src_ref=src,
                dst_ref=dst.at[pl.ds(spot, 1)],
                send_sem=send_sem,
                recv_sem=recv_sem,
                device_id=at(dx, dy),
                device_id_type=MESH,
            ).start()

    def hidden_start(a, rows):
        row = lane_row(rows)
        px_src[a] = row
        px_dst[a, pl.ds(me_x, 1), :] = row
        peers = [(d, 0) for d in (4, 3, 5, 2, 6, 1, 7)]
        pass_start(px_src.at[a], px_dst.at[a], me_x, peers, pxs_sem.at[a], pxr_sem.at[a])

    def hidden_turn(a):
        rest = px_dst.at[a, pl.ds(0, GX - 1)]
        pltpu.make_async_copy(rest, rest, pxr_sem.at[a]).wait()
        row = jnp.sum(px_dst[a], axis=0, keepdims=True)
        py_src[a] = row
        py_dst[a, pl.ds(me_y, 1), :] = row
        peers = [(0, d) for d in (8, 7, 9, 6, 10, 5, 11, 4, 12, 3, 13, 2, 14, 1, 15)]
        pass_start(py_src.at[a], py_dst.at[a], me_y, peers, pys_sem.at[a], pyr_sem.at[a])

    def hidden_wait(a):
        rest = py_dst.at[a, pl.ds(0, GY - 1)]
        pltpu.make_async_copy(rest, rest, pyr_sem.at[a]).wait()
        return apart(jnp.sum(py_dst[a], axis=0, keepdims=True))

    def hidden_drain(a):
        rest = px_dst.at[a, pl.ds(0, GX - 1)]
        pltpu.make_async_copy(rest, rest, pxs_sem.at[a]).wait()
        rest = py_dst.at[a, pl.ds(0, GY - 1)]
        pltpu.make_async_copy(rest, rest, pys_sem.at[a]).wait()

    def total_start(a, rows):
        row = lane_row(rows)
        ar_src[a] = row
        arx[a, pl.ds(me, 1), :] = row

        def send(dx, dy):
            pltpu.make_async_remote_copy(
                src_ref=ar_src.at[a],
                dst_ref=arx.at[a, pl.ds(me, 1)],
                send_sem=as_sem.at[a],
                recv_sem=ar_sem.at[a],
                device_id=at(dx, dy),
                device_id_type=MESH,
            ).start()

        to_all(send)

    def total_wait(a):
        pltpu.make_async_copy(
            arx.at[a, pl.ds(0, 127)], arx.at[a, pl.ds(0, 127)], ar_sem.at[a]
        ).wait()
        return apart(jnp.sum(arx[a], axis=0, keepdims=True))

    def total_drain(a):
        pltpu.make_async_copy(
            arx.at[a, pl.ds(0, 127)], arx.at[a, pl.ds(0, 127)], as_sem.at[a]
        ).wait()

    copies[0].wait()
    hit_p[...] = jnp.where(order(0, obs_pt[...], lane), 1.0, 0.0)
    for copy in copies[1:]:
        copy.wait()
    slot_row = lax.broadcasted_iota(jnp.int32, (SLOTS, TILES), 0)
    hot = jnp.where(slot_row == tpts_r[...], 1.0, 0.0).astype(BF16)
    for i in range(3):
        onehot[:, i * TILES : (i + 1) * TILES] = hot
    valid_m[...] = jnp.where(lane < column(count_r[...]).astype(jnp.int32), 1.0, 0.0)
    valid = valid_m[...]
    tcam = column(tcam_r[...]).astype(jnp.int32)
    parity = tcam & 1
    pair = tcam >> 1
    pair_m[...] = pair
    idx_c[...] = parity * 64 + obs_cam[...]

    for k in range(2):
        rs[k] = rs_in[pl.ds(k, TILES, stride=2), :] * valid
    for k in range(6):
        jp[k] = jp[k] * valid
        jpt[k] = sorted_t(jp[k], 0)
    square = [jpt[i] * jpt[j] + jpt[3 + i] * jpt[3 + j] for i, j in PAIRS]
    put_points(square, contrib_h)
    pl.semaphore_wait(barrier, len(greeted))
    collect_start(6, *pts_h)

    start = jnp.concatenate(
        [
            jnp.concatenate([start_r[:, 2 * p, :], start_r[:, 2 * p + 1, :]], axis=1)[:, None, :]
            for p in range(2)
        ],
        axis=1,
    )
    take_cams(start, 0)
    for k in range(2):
        mv[k] = rs[k] + gg[0, k]
    put_points(to_points(mv[0], mv[1]), contrib)
    collect_start(3, *pts)
    put_points(to_points(gg[0, 0], gg[0, 1]), contrib_y)
    collect_start(3, *pts_y)
    def rows_of(t, carry):
        slot = slot_s[t]
        n, q = slot >> 4, slot & 15
        row_s[0, t] = n * (3 * NBLK) + q
        row_s[1, t] = n * (6 * NBLK) + q
        return carry

    lax.fori_loop(0, TILES, rows_of, 0)
    found = order(1, obs_cam[...], lane & 63)
    mine = found & ((lane >> 6) == parity)
    hit_c[0] = jnp.where(mine & (pair == 0), 1.0, 0.0)
    hit_c[1] = jnp.where(mine & (pair == 1), 1.0, 0.0)
    for k in range(18):
        jct[k] = sorted_t(jc[k] * valid, 1)
    diag = put_cams([jct[k] * jct[k] + jct[CPAR + k] * jct[CPAR + k] for k in range(CPAR)])
    cost_row = lane_sum(rs[...] * rs[...])
    hess = collect_wait(6, *pts_h)
    for c in range(6):
        hess_b[c] = hess[c]
    inv = invert(hess, LAMBDAS[0])
    for c in range(6):
        inv_b[0, c] = inv[c]
    ybuf[0] = jnp.stack(collect_wait(3, *pts))

    costs = []
    update = start
    upd_sum = jnp.zeros_like(start)
    step_sum = jnp.zeros((3, NBLK, LANES), F32)

    def weighted(w):
        h = [hess_b[c] for c in range(6)]
        return [
            h[0] * w[0] + h[1] * w[1] + h[2] * w[2],
            h[1] * w[0] + h[3] * w[1] + h[4] * w[2],
            h[2] * w[0] + h[4] * w[1] + h[5] * w[2],
        ]

    def inner(u, v):
        return lane_sum(u[0] * v[0] + u[1] * v[1] + u[2] * v[2])

    def three(buf, b):
        return [buf[b, m] for m in range(3)]

    def mix(p, u, q, v):
        return [p * u[m] + q * v[m] for m in range(3)]

    w0 = apply_inverse(inv, three(ybuf, 0))
    wbuf[0] = jnp.stack(w0)
    spread_start(w0, *out_s)
    inv = invert(hess, LAMBDAS[1])
    for c in range(6):
        inv_b[1, c] = inv[c]
    spread_wait(*out_s)
    near = take_points(recv_s)

    for step in range(2):
        damping = LAMBDAS[step]
        last = step == 1
        cam_damp = damping * (diag + 1.0)
        precond = diag + cam_damp
        if step == 0:
            eliminate(mv[0], mv[1], near, 0)
        r0 = -back_to_cams(0) - cam_damp * update
        z0 = r0 / precond

        take_cams(z0, 1)
        put_points(to_points(gg[1, 0], gg[1, 1]), contrib)
        collect_start(3, *pts)
        if last:
            spread_wait(*out_2)
            near = take_points(recv_2)
            for r in range(2):
                shift = jp[3 * r] * near[0] + jp[3 * r + 1] * near[1] + jp[3 * r + 2] * near[2]
                res = rs[r] - cb * shift
                rs[r] = res
                mv[r] = mv[r] + res
            cost_row = lane_sum(rs[...] * rs[...])
        y = collect_wait(3, *pts)
        ybuf[1] = jnp.stack(y)
        w = apply_inverse([inv_b[step, c] for c in range(6)], y)
        wbuf[1] = jnp.stack(w)
        spread_start(w, *out_s)
        spread_wait(*out_s)
        near = take_points(recv_s)
        eliminate(gg[1, 0], gg[1, 1], near, 1)
        c0 = back_to_cams(1) + cam_damp * z0
        u = c0 / precond
        hidden_start(step, [lane_sum(r0 * z0), lane_sum(z0 * c0), lane_sum(c0 * u), cost_row])
        take_cams(u, 2)
        put_points(to_points(gg[2, 0], gg[2, 1]), contrib)
        collect_start(3, *pts)
        hidden_turn(step)
        y = collect_wait(3, *pts)
        ybuf[2] = jnp.stack(y)
        w = apply_inverse([inv_b[step, c] for c in range(6)], y)
        wbuf[2] = jnp.stack(w)
        if last:
            spread_start(w, *out_s)
        else:
            scale = [damping * (hess[c] + 1.0) for c in (0, 3, 5)]
            y_start = collect_wait(3, *pts_y)
            held = []
            for b in range(3):
                held.append([scale[m] * wbuf[b, m] + ybuf[b, m] for m in range(3)])
            held[0] = [scale[m] * wbuf[0, m] + y_start[m] for m in range(3)]
            moved = [apply_inverse([inv_b[1, c] for c in range(6)], y) for y in held]

        dots = hidden_wait(step)
        resid_dot, curve, square = dots[0], dots[1], dots[2]
        costs.append(0.5 * dots[3])
        alpha = resid_dot / curve
        beta = (resid_dot - 2.0 * alpha * curve + alpha * alpha * square) / resid_dot
        more = 1.0 + beta
        z1 = (r0 - alpha * c0) / precond
        d1 = z1 + beta * z0
        if not last:
            y_fix = mix(1.0, held[0], alpha, held[1])
            y_move = mix(more, held[1], -alpha, held[2])
            w_fix = mix(1.0, moved[0], alpha, moved[1])
            w_move = mix(more, moved[1], -alpha, moved[2])
            spread_start(w_fix + mix(1.0, w_move, -alpha, w), *out_w)
        turn = [more * gg[1, r] - alpha * gg[2, r] for r in range(2)]
        y_turn = mix(more, three(ybuf, 1), -alpha, three(ybuf, 2))
        w_turn = mix(more, three(wbuf, 1), -alpha, three(wbuf, 2))
        turn_sq = lane_sum(turn[0] * turn[0] + turn[1] * turn[1])
        yw = inner(y_turn, w_turn)
        rows = [
            lane_sum((r0 - alpha * c0) * z1),
            turn_sq - yw + lane_sum(cam_damp * (d1 * d1)),
        ]
        if last:
            base = [mv[r] + alpha * gg[1, r] for r in range(2)]
            y_base = mix(1.0, three(ybuf, 0), alpha, three(ybuf, 1))
            w_base = mix(1.0, three(wbuf, 0), alpha, three(wbuf, 1))
            hw_base = weighted(w_base)
            hw_turn = weighted(w_turn)
            rows += [
                lane_sum(base[0] * base[0] + base[1] * base[1])
                - 2.0 * inner(y_base, w_base)
                + inner(w_base, hw_base),
                lane_sum(base[0] * turn[0] + base[1] * turn[1])
                - inner(y_base, w_turn)
                - inner(y_turn, w_base)
                + inner(w_base, hw_turn),
                turn_sq - 2.0 * yw + inner(w_turn, hw_turn),
            ]
        total_start(step, rows)
        if not last:
            spread_start(w, *out_2)
            spread_wait(*out_w)
            near_fix = take_points(recv_w)
            near_move = take_points(recv_w, 3)
        else:
            spread_wait(*out_s)
            near = take_points(recv_s)
            eliminate(gg[2, 0], gg[2, 1], near, 2)
        dots = total_wait(step)
        alpha1 = dots[0] / dots[1]
        ca = alpha + alpha1 * more
        cb = -(alpha1 * alpha)
        update = update + alpha * z0 + alpha1 * d1
        upd_sum = upd_sum + update
        step_sum = step_sum - (wbuf[0] + ca * wbuf[1] + cb * wbuf[2])
        if not last:
            near = [near_fix[m] + alpha1 * near_move[m] for m in range(3)]
            for r in range(2):
                rs[r] = bk[0, r] + ca * bk[1, r] + cb * gg[2, r]
                mv[r] = gg[0, r] + ca * gg[1, r] + cb * gg[2, r]
            eliminate(rs[0] + mv[0], rs[1] + mv[1], near, 0)
            ybuf[0] = jnp.stack(mix(1.0, y_fix, alpha1, y_move))
            wbuf[0] = jnp.stack(mix(1.0, w_fix, alpha1, w_move))
        else:
            for r in range(2):
                res_o[pl.ds(r, TILES, stride=2), :] = bk[0, r] + ca * bk[1, r] + cb * bk[2, r]
            costs.append(0.5 * (dots[2] + 2.0 * alpha1 * dots[3] + alpha1 * alpha1 * dots[4]))
    for p in range(2):
        both = upd_sum[:, p, :]
        cam_o[:, 2 * p, :] = cam_r[:, 2 * p, :] + both[:, 0:64]
        cam_o[:, 2 * p + 1, :] = cam_r[:, 2 * p + 1, :] + both[:, 64:128]
    pt_o[...] = pt_r[...] + step_sum
    third = lax.broadcasted_iota(jnp.int32, (1, 3), 1)
    cost_o[...] = jnp.where(third == 0, costs[0], jnp.where(third == 1, costs[1], costs[2]))
    for a in range(2):
        hidden_drain(a)
        total_drain(a)


def hand_over(cam_i, pt_i, res_i, cost_i, cam_o, pt_o, res_o, cost_o):
    res_o[...] = res_i[...]
    cam_o[...] = cam_i[...]
    pt_o[...] = pt_i[...]
    cost_o[...] = cost_i[...]


def body(
    jac_cam,
    jac_pt,
    resid0,
    obs_count,
    tile_camera,
    tile_points,
    obs_camera,
    obs_point,
    cam_params,
    pt_params,
    cg_start,
):
    vmem = pl.BlockSpec(memory_space=pltpu.VMEM)
    hbm = pl.BlockSpec(memory_space=pltpu.HBM)
    big = (TILES, LANES)
    blk = (NBLK, LANES)
    dma = pltpu.SemaphoreType.DMA
    shapes = [
        jax.ShapeDtypeStruct((CPAR, 4, 64), F32),
        jax.ShapeDtypeStruct((3,) + blk, F32),
        jax.ShapeDtypeStruct((2 * TILES, LANES), F32),
        jax.ShapeDtypeStruct((1, 3), F32),
    ]
    results = pl.pallas_call(
        kernel,
        out_shape=shapes,
        in_specs=[pl.BlockSpec(memory_space=pltpu.SMEM)] + [hbm] * 11,
        out_specs=[vmem] * 4,
        scratch_shapes=[
            pltpu.VMEM((18,) + big, F32),
            pltpu.VMEM((6,) + big, F32),
            pltpu.VMEM((2,) + big, F32),
            pltpu.VMEM((2 * TILES, LANES), F32),
            pltpu.VMEM(big, jnp.int32),
            pltpu.VMEM(big, jnp.int32),
            pltpu.VMEM((1, LANES), jnp.int32),
            pltpu.VMEM((1, LANES), jnp.int32),
            pltpu.VMEM((1, LANES), jnp.int32),
            pltpu.VMEM((CPAR, 4, 64), F32),
            pltpu.VMEM((CPAR, 4, 64), F32),
            pltpu.VMEM((3,) + blk, F32),
            pltpu.VMEM((18,) + big, F32),
            pltpu.VMEM((6,) + big, F32),
            pltpu.VMEM((PAD + LANES, LANES), F32),
            pltpu.VMEM((CPAR, PAD + LANES, LANES), F32),
            pltpu.VMEM((CPAR, PAD + LANES, LANES), F32),
            pltpu.VMEM((2,) + big, jnp.int32),
            pltpu.VMEM((2,) + big, jnp.int32),
            pltpu.VMEM((2, 7) + big, F32),
            pltpu.VMEM(big, F32),
            pltpu.VMEM((2,) + big, F32),
            pltpu.VMEM(big, jnp.int32),
            pltpu.VMEM(big, F32),
            pltpu.VMEM(big, jnp.int32),
            pltpu.VMEM((SLOTS, 3 * TILES), BF16),
            pltpu.VMEM((3,) + big, F32),
            pltpu.VMEM((3, 2) + big, F32),
            pltpu.VMEM((3, 2) + big, F32),
            pltpu.VMEM((2,) + big, F32),
            pltpu.VMEM((9, 3) + blk, F32),
            pltpu.VMEM((8, 3) + blk, F32),
            pltpu.VMEM((9, 6) + blk, F32),
            pltpu.VMEM((8, 6) + blk, F32),
            pltpu.VMEM((9, 3) + blk, F32),
            pltpu.VMEM((8, 3) + blk, F32),
            pltpu.VMEM((3 * NBLK, LANES), F32),
            pltpu.VMEM((27 * NBLK, LANES), F32),
            pltpu.VMEM((6 * NBLK, LANES), F32),
            pltpu.VMEM((54 * NBLK, LANES), F32),
            pltpu.VMEM((3 * NBLK, LANES), F32),
            pltpu.VMEM((27 * NBLK, LANES), F32),
            pltpu.VMEM((6,) + blk, F32),
            pltpu.VMEM((2, 6) + blk, F32),
            pltpu.VMEM((3, 3) + blk, F32),
            pltpu.VMEM((3, 3) + blk, F32),
            pltpu.VMEM((CPAR, 2, LANES), F32),
            pltpu.VMEM((CPAR, 2, LANES), F32),
            pltpu.VMEM((2, 1, LANES), F32),
            pltpu.VMEM((2, GX * GY, LANES), F32),
            pltpu.VMEM((2, 1, LANES), F32),
            pltpu.VMEM((2, GX, LANES), F32),
            pltpu.VMEM((2, 1, LANES), F32),
            pltpu.VMEM((2, GY, LANES), F32),
            dma((11,)),
            pltpu.SMEM((2, LANES), jnp.int32),
        ]
        + [dma((8,))] * 12
        + [dma((2,))] * 6,
        compiler_params=pltpu.CompilerParams(
            collective_id=0, has_side_effects=True, vmem_limit_bytes=62 * 1024 * 1024
        ),
    )(
        tile_points[0, 0],
        jnp.transpose(jac_cam[0, 0], (1, 0, 2)),
        jnp.transpose(jac_pt[0, 0], (1, 0, 2)),
        resid0.reshape(2 * TILES, LANES),
        obs_camera[0, 0],
        obs_point[0, 0],
        obs_count[0],
        tile_camera[0],
        tile_points[0],
        jnp.transpose(cg_start[0, 0], (1, 0, 2)),
        jnp.transpose(cam_params[0, 0], (1, 0, 2)),
        jnp.transpose(pt_params[0, 0], (1, 0, 2)),
    )
    cam, pt, res, costs = pl.pallas_call(
        hand_over,
        out_shape=shapes,
        in_specs=[vmem] * 4,
        out_specs=[vmem] * 4,
    )(*results)
    cam_out = jnp.transpose(cam, (1, 0, 2))[None, None]
    pt_out = jnp.transpose(pt, (1, 0, 2))[None, None]
    return cam_out, pt_out, res.reshape(1, 1, TILES, 2, LANES), costs.reshape(3)


def solution(mesh):
    wide = P("gx", "gy", None, None, None)
    in_specs = (
        wide,
        wide,
        wide,
        P("gx", "gy", None),
        P("gx", "gy", None),
        P("gx", "gy", None),
        P("gx", "gy", None, None),
        P("gx", "gy", None, None),
        wide,
        wide,
        wide,
    )
    out_specs = (wide, wide, wide, P())
    return jax.shard_map(body, mesh=mesh, in_specs=in_specs, out_specs=out_specs, check_vma=False)
```

```python
import jax
import jax.numpy as jnp
from jax import lax
from jax.experimental import pallas as pl
from jax.experimental.pallas import tpu as pltpu
from jax.sharding import PartitionSpec as P

MESH = pl.DeviceIdType.MESH
CPAR = 9
NBLK = 16
LANES = 128
TILES = 128
SLOTS = 9 * NBLK
GX = 8
GY = 16
PAD = 64
STEPS = (1, 2, 4, 8, 16, 32, 64)
LAMBDAS = (1.0, 0.25)
PAIRS = ((0, 0), (0, 1), (0, 2), (1, 1), (1, 2), (2, 2))
OTHERS = (0, 1, 2, 3, 5, 6, 7, 8)
ORDER = tuple((OTHERS.index(n), n) for n in (0, 2, 6, 8, 3, 5, 1, 7))
F32 = jnp.float32
BF16 = jnp.bfloat16
GATHER = lax.GatherDimensionNumbers(
    offset_dims=(),
    collapsed_slice_dims=(1,),
    start_index_map=(1,),
    operand_batching_dims=(0,),
    start_indices_batching_dims=(0,),
)


def pick(x, idx):
    return lax.gather(
        x, idx[:, :, None], GATHER, (1, 1), mode=lax.GatherScatterMode.PROMISE_IN_BOUNDS
    )


def lane_ids(rows):
    return lax.broadcasted_iota(jnp.int32, (rows, LANES), 1)


def sort_lanes(key):
    flat = jnp.swapaxes(key.astype(F32), 0, 1).reshape(16, 8, LANES)
    regs = [flat[v] for v in range(16)]
    sub = lax.broadcasted_iota(jnp.int32, (8, LANES), 0)
    before = None
    size = 2
    while size <= LANES:
        if size >= 16:
            bit = size // 16
            sign = jnp.where((sub & bit) == 0, 1.0, -1.0)
            turn = sign if before is None else sign * before
            regs = [x * turn for x in regs]
            before = sign
        gap = size // 2
        while gap >= 1:
            if gap < 16:
                for v in range(16):
                    if v & gap == 0:
                        low = jnp.minimum(regs[v], regs[v + gap])
                        high = jnp.maximum(regs[v], regs[v + gap])
                        up = size >= 16 or v & size == 0
                        regs[v], regs[v + gap] = (low, high) if up else (high, low)
            else:
                g = gap // 16
                first = (sub & g) == 0
                for v in range(16):
                    x = regs[v]
                    other = jnp.where(
                        first, pltpu.roll(x, 8 - g, axis=0), pltpu.roll(x, g, axis=0)
                    )
                    regs[v] = jnp.where(first, jnp.minimum(x, other), jnp.maximum(x, other))
            gap //= 2
        size *= 2
    rows = jnp.swapaxes(jnp.concatenate(regs, axis=0), 0, 1)
    lane = lane_ids(LANES)
    return pick(rows, (lane & 15) * 8 + (lane >> 4)).astype(jnp.int32)


def last_at_most(seg, target):
    count = jnp.zeros_like(target)
    for step in (64, 32, 16, 8, 4, 2, 1):
        count = jnp.where(pick(seg, count + (step - 1)) <= target, count + step, count)
    return jnp.where(pick(seg, count) <= target, count + 1, count)


def column(row):
    return jnp.swapaxes(jnp.broadcast_to(row.astype(F32), (LANES, LANES)), 0, 1)


def invert(hess, damping):
    h00 = hess[0] + damping * (hess[0] + 1.0)
    h01, h02 = hess[1], hess[2]
    h11 = hess[3] + damping * (hess[3] + 1.0)
    h12 = hess[4]
    h22 = hess[5] + damping * (hess[5] + 1.0)
    c00 = h11 * h22 - h12 * h12
    c01 = h02 * h12 - h01 * h22
    c02 = h01 * h12 - h02 * h11
    c11 = h00 * h22 - h02 * h02
    c12 = h01 * h02 - h00 * h12
    c22 = h00 * h11 - h01 * h01
    det = h00 * c00 + h01 * c01 + h02 * c02
    return [c / det for c in (c00, c01, c02, c11, c12, c22)]


def apply_inverse(inv, y):
    return [
        inv[0] * y[0] + inv[1] * y[1] + inv[2] * y[2],
        inv[1] * y[0] + inv[3] * y[1] + inv[4] * y[2],
        inv[2] * y[0] + inv[4] * y[1] + inv[5] * y[2],
    ]


def lane_sum(x):
    while x.ndim > 2:
        x = jnp.sum(x, axis=0)
    return jnp.sum(x, axis=0, keepdims=True)


def kernel(
    slot_s,
    jc_h,
    jp_h,
    rs_h,
    cam_h,
    pt_h,
    count_h,
    tcam_h,
    tpts_h,
    start_h,
    cpar_h,
    ppar_h,
    cam_o,
    pt_o,
    res_o,
    cost_o,
    jc,
    jp,
    rs,
    rs_in,
    obs_cam,
    obs_pt,
    count_r,
    tcam_r,
    tpts_r,
    start_r,
    cam_r,
    pt_r,
    jct,
    jpt,
    seg_t,
    scan_a,
    scan_b,
    perm,
    endi,
    smask,
    hit_p,
    hit_c,
    pair_m,
    valid_m,
    idx_c,
    onehot,
    table,
    gg,
    bk,
    mv,
    contrib,
    recv_c,
    contrib_h,
    recv_h,
    contrib_y,
    recv_y,
    wsrc,
    recv_s,
    wsrc_w,
    recv_w,
    wsrc_2,
    recv_2,
    hess_b,
    inv_b,
    ybuf,
    wbuf,
    camvec,
    camacc,
    ar_src,
    arx,
    px_src,
    px_dst,
    py_src,
    py_dst,
    in_sem,
    row_s,
    cs_sem,
    cr_sem,
    hs_sem,
    hr_sem,
    ys_sem,
    yr_sem,
    ss_sem,
    sr_sem,
    ws_sem,
    wr_sem,
    s2_sem,
    r2_sem,
    as_sem,
    ar_sem,
    pxs_sem,
    pxr_sem,
    pys_sem,
    pyr_sem,
):
    me_x = lax.axis_index("gx")
    me_y = lax.axis_index("gy")

    def at(dx, dy):
        return (lax.rem(me_x + (dx + GX), GX), lax.rem(me_y + (dy + GY), GY))

    me = me_x * GY + me_y
    here = {}
    for n in OTHERS:
        a, b = divmod(n, 3)
        x, y = me_x + (a - 1), me_y + (b - 1)
        here[n] = (x >= 0) & (x < GX) & (y >= 0) & (y < GY)

    def to_all(act):
        def row(j, carry):
            dy = lax.rem(j + 5, GY - 1) + 1
            for dx in (4, 3, 5, 2, 6, 1, 7, 0):
                act(dx, dy)
            return carry

        lax.fori_loop(0, GY - 1, row, 0)
        for dx in (4, 3, 5, 2, 6, 1, 7):
            act(dx, 0)

    pairs = [
        (pt_h, obs_pt),
        (jp_h, jp),
        (jc_h, jc),
        (cam_h, obs_cam),
        (rs_h, rs_in),
        (tcam_h, tcam_r),
        (count_h, count_r),
        (tpts_h, tpts_r),
        (start_h, start_r),
        (cpar_h, cam_r),
        (ppar_h, pt_r),
    ]
    copies = [
        pltpu.make_async_copy(src, dst, in_sem.at[i]) for i, (src, dst) in enumerate(pairs)
    ]
    for copy in copies:
        copy.start()

    for r, n in enumerate(OTHERS):

        @pl.when(jnp.logical_not(here[n]))
        def _(r=r, n=n):
            recv_c[r] = jnp.zeros_like(recv_c[r])
            recv_h[r] = jnp.zeros_like(recv_h[r])
            recv_y[r] = jnp.zeros_like(recv_y[r])
            for buf in (recv_s, recv_w, recv_2):
                per = buf.shape[0] // 9
                buf[n * per : (n + 1) * per, :] = jnp.zeros((per, LANES), F32)

    barrier = pltpu.get_barrier_semaphore()
    greeted = [(-1, -1), (-1, 1), (1, -1), (1, 1)]
    greeted += [(0, d) for d in range(1, GY)] + [(d, 0) for d in range(1, GX)]
    for dx, dy in greeted:
        pl.semaphore_signal(barrier, inc=1, device_id=at(dx, dy), device_id_type=MESH)

    seg_t[0:PAD, :] = jnp.full((PAD, LANES), -1.0, F32)
    for k in range(CPAR):
        scan_a[k, 0:PAD, :] = jnp.zeros((PAD, LANES), F32)
        scan_b[k, 0:PAD, :] = jnp.zeros((PAD, LANES), F32)
    lane = lane_ids(TILES)

    def order(kind, ids, target):
        key = sort_lanes(ids * LANES + lane)
        perm[kind] = key & (LANES - 1)
        seg = key >> 7
        count = last_at_most(seg, target)
        last = jnp.maximum(count - 1, 0)
        endi[kind] = last
        found = (count > 0) & (pick(seg, last) == target)
        seg_t[PAD : PAD + LANES, :] = jnp.swapaxes(seg.astype(F32), 0, 1)
        for i, d in enumerate(STEPS):
            same = seg_t[PAD : PAD + LANES, :] == seg_t[PAD - d : PAD + LANES - d, :]
            smask[kind, i] = jnp.where(same, 1.0, 0.0)
        return found

    def sorted_t(x, kind):
        return jnp.swapaxes(pick(x, perm[kind]), 0, 1)

    def summed(values, kind):
        count = len(values)
        src, dst = scan_a, scan_b
        for k in range(count):
            src[k, PAD : PAD + LANES, :] = values[k]
        for i, d in enumerate(STEPS):
            for k in range(count):
                dst[k, PAD : PAD + LANES, :] = (
                    src[k, PAD : PAD + LANES, :]
                    + src[k, PAD - d : PAD + LANES - d, :] * smask[kind, i]
                )
            src, dst = dst, src
        return [
            pick(jnp.swapaxes(src[k, PAD : PAD + LANES, :], 0, 1), endi[kind])
            for k in range(count)
        ]

    def put_points(values, dest):
        sums = jnp.concatenate([v * hit_p[...] for v in summed(values, 0)], axis=1)
        high = sums.astype(BF16)
        rest = sums - high.astype(F32)
        mid = rest.astype(BF16)
        low = (rest - mid.astype(F32)).astype(BF16)
        parts = jnp.concatenate([high, mid, low], axis=0)
        out = jnp.dot(onehot[...], parts, preferred_element_type=F32)
        for n in range(9):
            for m in range(len(values)):
                dest[n, m] = out[n * NBLK : (n + 1) * NBLK, m * LANES : (m + 1) * LANES]

    def put_cams(values):
        for k, sums in enumerate(summed(values, 1)):
            top = lane_sum(sums * hit_c[0])
            bottom = lane_sum(sums * hit_c[1])
            camacc[k] = jnp.concatenate([top, bottom], axis=0)
        return camacc[...]

    def take_cams(vector, b):
        camvec[...] = vector
        rows = 32

        def one(chunk, carry):
            where = pl.ds(pl.multiple_of(chunk * rows, rows), rows)
            idx = idx_c[where, :]
            second = pair_m[where, :] == 1
            e0 = jnp.zeros((rows, LANES), F32)
            e1 = jnp.zeros((rows, LANES), F32)
            for k in range(CPAR):
                v = camvec[k]
                src = jnp.where(
                    second,
                    jnp.broadcast_to(v[1:2], (rows, LANES)),
                    jnp.broadcast_to(v[0:1], (rows, LANES)),
                )
                got = pick(src, idx)
                e0 = e0 + jc[k, where, :] * got
                e1 = e1 + jc[CPAR + k, where, :] * got
            gg[b, 0, where, :] = e0 * valid_m[where, :]
            gg[b, 1, where, :] = e1 * valid_m[where, :]
            return carry

        lax.fori_loop(0, TILES // rows, one, 0)

    def to_points(e0, e1):
        t0, t1 = sorted_t(e0, 0), sorted_t(e1, 0)
        return [jpt[m] * t0 + jpt[3 + m] * t1 for m in range(3)]

    def collect_start(comps, src, dst, send_sem, recv_sem):
        for r, n in ORDER:
            a, b = divmod(n, 3)

            @pl.when(here[n])
            def _(r=r, n=n, a=a, b=b):
                pltpu.make_async_remote_copy(
                    src_ref=src.at[n, pl.ds(0, comps)],
                    dst_ref=dst.at[r, pl.ds(0, comps)],
                    send_sem=send_sem.at[r],
                    recv_sem=recv_sem.at[r],
                    device_id=at(a - 1, b - 1),
                    device_id_type=MESH,
                ).start()

    def collect_wait(comps, src, dst, send_sem, recv_sem):
        for sem, flip in ((recv_sem, True), (send_sem, False)):
            for r, n in enumerate(OTHERS):

                @pl.when(here[8 - n] if flip else here[n])
                def _(r=r, n=n, sem=sem):
                    pltpu.make_async_copy(
                        src.at[n, pl.ds(0, comps)], dst.at[r, pl.ds(0, comps)], sem.at[r]
                    ).wait()

        total = []
        for m in range(comps):
            s = src[4, m]
            for r in range(8):
                s = s + dst[r, m]
            total.append(s)
        return total

    pts = (contrib, recv_c, cs_sem, cr_sem)
    pts_h = (contrib_h, recv_h, hs_sem, hr_sem)
    pts_y = (contrib_y, recv_y, ys_sem, yr_sem)
    out_s = (wsrc, recv_s, ss_sem, sr_sem)
    out_w = (wsrc_w, recv_w, ws_sem, wr_sem)
    out_2 = (wsrc_2, recv_2, s2_sem, r2_sem)

    def spread_start(values, src, dst, send_sem, recv_sem):
        per = src.shape[0]
        for m, v in enumerate(values):
            src[m * NBLK : (m + 1) * NBLK, :] = v
            dst[4 * per + m * NBLK : 4 * per + (m + 1) * NBLK, :] = v
        for r, n in ORDER:
            a, b = divmod(n, 3)

            @pl.when(here[n])
            def _(r=r, n=n, a=a, b=b):
                pltpu.make_async_remote_copy(
                    src_ref=src,
                    dst_ref=dst.at[pl.ds((8 - n) * per, per)],
                    send_sem=send_sem.at[r],
                    recv_sem=recv_sem.at[r],
                    device_id=at(a - 1, b - 1),
                    device_id_type=MESH,
                ).start()

    def spread_wait(src, dst, send_sem, recv_sem):
        per = src.shape[0]
        for sem, flip in ((recv_sem, True), (send_sem, False)):
            for r, n in enumerate(OTHERS):

                @pl.when(here[8 - n] if flip else here[n])
                def _(r=r, n=n, sem=sem):
                    pltpu.make_async_copy(
                        src, dst.at[pl.ds((8 - n) * per, per)], sem.at[r]
                    ).wait()

    def take_points(src, first=0):
        per = src.shape[0] // 9

        def one(chunk, carry):
            for i in range(16):
                t = chunk * 16 + i
                row = row_s[0 if per == 3 * NBLK else 1, t] + first * NBLK
                for m in range(3):
                    table[m, pl.ds(t, 1), :] = src[pl.ds(row + m * NBLK, 1), :]
            return carry

        lax.fori_loop(0, TILES // 16, one, 0)
        return [pick(table[m], obs_pt[...]) for m in range(3)]

    def eliminate(e0, e1, near, b):
        bk[b, 0] = e0 - (jp[0] * near[0] + jp[1] * near[1] + jp[2] * near[2])
        bk[b, 1] = e1 - (jp[3] * near[0] + jp[4] * near[1] + jp[5] * near[2])

    def back_to_cams(b):
        t0, t1 = sorted_t(bk[b, 0], 1), sorted_t(bk[b, 1], 1)
        return put_cams([jct[k] * t0 + jct[CPAR + k] * t1 for k in range(CPAR)])

    def lane_row(rows):
        held = jnp.concatenate(rows + [jnp.zeros((16 - len(rows), LANES), F32)], axis=0)
        sums = jnp.sum(held, axis=1, keepdims=True)
        own = lax.broadcasted_iota(jnp.int32, (16, LANES), 0)
        return jnp.sum(jnp.where(lane_ids(16) == own, sums, 0.0), axis=0, keepdims=True)

    def apart(row, count):
        lane1 = lane_ids(1)
        return [
            jnp.sum(jnp.where(lane1 == i, row, 0.0), axis=1, keepdims=True) for i in range(count)
        ]

    def pass_start(src, dst, spot, peers, send_sem, recv_sem):
        for dx, dy in peers:
            pltpu.make_async_remote_copy(
                src_ref=src,
                dst_ref=dst.at[pl.ds(spot, 1)],
                send_sem=send_sem,
                recv_sem=recv_sem,
                device_id=at(dx, dy),
                device_id_type=MESH,
            ).start()

    def hidden_start(a, rows):
        row = lane_row(rows)
        px_src[a] = row
        px_dst[a, pl.ds(me_x, 1), :] = row
        peers = [(d, 0) for d in (4, 3, 5, 2, 6, 1, 7)]
        pass_start(px_src.at[a], px_dst.at[a], me_x, peers, pxs_sem.at[a], pxr_sem.at[a])

    def hidden_turn(a):
        rest = px_dst.at[a, pl.ds(0, GX - 1)]
        pltpu.make_async_copy(rest, rest, pxr_sem.at[a]).wait()
        row = jnp.sum(px_dst[a], axis=0, keepdims=True)
        py_src[a] = row
        py_dst[a, pl.ds(me_y, 1), :] = row
        peers = [(0, d) for d in (8, 7, 9, 6, 10, 5, 11, 4, 12, 3, 13, 2, 14, 1, 15)]
        pass_start(py_src.at[a], py_dst.at[a], me_y, peers, pys_sem.at[a], pyr_sem.at[a])

    def hidden_wait(a):
        rest = py_dst.at[a, pl.ds(0, GY - 1)]
        pltpu.make_async_copy(rest, rest, pyr_sem.at[a]).wait()
        return apart(jnp.sum(py_dst[a], axis=0, keepdims=True), 3)

    def hidden_drain(a):
        rest = px_dst.at[a, pl.ds(0, GX - 1)]
        pltpu.make_async_copy(rest, rest, pxs_sem.at[a]).wait()
        rest = py_dst.at[a, pl.ds(0, GY - 1)]
        pltpu.make_async_copy(rest, rest, pys_sem.at[a]).wait()

    def total_start(a, rows):
        row = lane_row(rows)
        ar_src[a] = row
        arx[a, pl.ds(me, 1), :] = row

        def send(dx, dy):
            pltpu.make_async_remote_copy(
                src_ref=ar_src.at[a],
                dst_ref=arx.at[a, pl.ds(me, 1)],
                send_sem=as_sem.at[a],
                recv_sem=ar_sem.at[a],
                device_id=at(dx, dy),
                device_id_type=MESH,
            ).start()

        to_all(send)

    def total_wait(a):
        pltpu.make_async_copy(
            arx.at[a, pl.ds(0, 127)], arx.at[a, pl.ds(0, 127)], ar_sem.at[a]
        ).wait()
        return apart(jnp.sum(arx[a], axis=0, keepdims=True), 9)

    def total_drain(a):
        pltpu.make_async_copy(
            arx.at[a, pl.ds(0, 127)], arx.at[a, pl.ds(0, 127)], as_sem.at[a]
        ).wait()

    copies[0].wait()
    hit_p[...] = jnp.where(order(0, obs_pt[...], lane), 1.0, 0.0)
    for copy in copies[1:]:
        copy.wait()
    slot_row = lax.broadcasted_iota(jnp.int32, (SLOTS, TILES), 0)
    hot = jnp.where(slot_row == tpts_r[...], 1.0, 0.0).astype(BF16)
    for i in range(3):
        onehot[:, i * TILES : (i + 1) * TILES] = hot
    valid_m[...] = jnp.where(lane < column(count_r[...]).astype(jnp.int32), 1.0, 0.0)
    valid = valid_m[...]
    tcam = column(tcam_r[...]).astype(jnp.int32)
    parity = tcam & 1
    pair = tcam >> 1
    pair_m[...] = pair
    idx_c[...] = parity * 64 + obs_cam[...]

    for k in range(2):
        rs[k] = rs_in[pl.ds(k, TILES, stride=2), :] * valid
    for k in range(6):
        jp[k] = jp[k] * valid
        jpt[k] = sorted_t(jp[k], 0)
    square = [jpt[i] * jpt[j] + jpt[3 + i] * jpt[3 + j] for i, j in PAIRS]
    put_points(square, contrib_h)
    pl.semaphore_wait(barrier, len(greeted))
    collect_start(6, *pts_h)

    start = jnp.concatenate(
        [
            jnp.concatenate([start_r[:, 2 * p, :], start_r[:, 2 * p + 1, :]], axis=1)[:, None, :]
            for p in range(2)
        ],
        axis=1,
    )
    take_cams(start, 0)
    for k in range(2):
        mv[k] = rs[k] + gg[0, k]
    put_points(to_points(mv[0], mv[1]), contrib)
    collect_start(3, *pts)
    put_points(to_points(gg[0, 0], gg[0, 1]), contrib_y)
    collect_start(3, *pts_y)
    def rows_of(t, carry):
        slot = slot_s[t]
        n, q = slot >> 4, slot & 15
        row_s[0, t] = n * (3 * NBLK) + q
        row_s[1, t] = n * (6 * NBLK) + q
        return carry

    lax.fori_loop(0, TILES, rows_of, 0)
    found = order(1, obs_cam[...], lane & 63)
    mine = found & ((lane >> 6) == parity)
    hit_c[0] = jnp.where(mine & (pair == 0), 1.0, 0.0)
    hit_c[1] = jnp.where(mine & (pair == 1), 1.0, 0.0)
    for k in range(18):
        jct[k] = sorted_t(jc[k] * valid, 1)
    diag = put_cams([jct[k] * jct[k] + jct[CPAR + k] * jct[CPAR + k] for k in range(CPAR)])
    cost_row = lane_sum(rs[...] * rs[...])
    hess = collect_wait(6, *pts_h)
    for c in range(6):
        hess_b[c] = hess[c]
    inv = invert(hess, LAMBDAS[0])
    for c in range(6):
        inv_b[0, c] = inv[c]
    ybuf[0] = jnp.stack(collect_wait(3, *pts))

    costs = []
    update = start
    upd_sum = jnp.zeros_like(start)
    step_sum = jnp.zeros((3, NBLK, LANES), F32)

    def weighted(w):
        h = [hess_b[c] for c in range(6)]
        return [
            h[0] * w[0] + h[1] * w[1] + h[2] * w[2],
            h[1] * w[0] + h[3] * w[1] + h[4] * w[2],
            h[2] * w[0] + h[4] * w[1] + h[5] * w[2],
        ]

    def inner(u, v):
        return lane_sum(u[0] * v[0] + u[1] * v[1] + u[2] * v[2])

    def three(buf, b):
        return [buf[b, m] for m in range(3)]

    def mix(p, u, q, v):
        return [p * u[m] + q * v[m] for m in range(3)]

    w0 = apply_inverse(inv, three(ybuf, 0))
    wbuf[0] = jnp.stack(w0)
    spread_start(w0, *out_s)
    inv = invert(hess, LAMBDAS[1])
    for c in range(6):
        inv_b[1, c] = inv[c]
    spread_wait(*out_s)
    near = take_points(recv_s)

    for step in range(2):
        damping = LAMBDAS[step]
        last = step == 1
        cam_damp = damping * (diag + 1.0)
        precond = diag + cam_damp
        if step == 0:
            eliminate(mv[0], mv[1], near, 0)
        r0 = -back_to_cams(0) - cam_damp * update
        z0 = r0 / precond

        take_cams(z0, 1)
        put_points(to_points(gg[1, 0], gg[1, 1]), contrib)
        collect_start(3, *pts)
        if last:
            spread_wait(*out_2)
            near = take_points(recv_2)
            for r in range(2):
                shift = jp[3 * r] * near[0] + jp[3 * r + 1] * near[1] + jp[3 * r + 2] * near[2]
                res = rs[r] - cb * shift
                rs[r] = res
                mv[r] = mv[r] + res
            cost_row = lane_sum(rs[...] * rs[...])
        y = collect_wait(3, *pts)
        ybuf[1] = jnp.stack(y)
        w = apply_inverse([inv_b[step, c] for c in range(6)], y)
        wbuf[1] = jnp.stack(w)
        spread_start(w, *out_s)
        g1_sq = lane_sum(gg[1, 0] * gg[1, 0] + gg[1, 1] * gg[1, 1])
        yw1 = inner(y, w)
        hidden_start(
            step,
            [lane_sum(r0 * z0), g1_sq - yw1 + lane_sum(cam_damp * (z0 * z0)), cost_row],
        )
        spread_wait(*out_s)
        near = take_points(recv_s)
        eliminate(gg[1, 0], gg[1, 1], near, 1)
        c0 = back_to_cams(1) + cam_damp * z0
        hidden_turn(step)
        u = c0 / precond

        take_cams(u, 2)
        put_points(to_points(gg[2, 0], gg[2, 1]), contrib)
        collect_start(3, *pts)

        dots = hidden_wait(step)
        resid_dot, curve = dots[0], dots[1]
        costs.append(0.5 * dots[2])
        alpha = resid_dot / curve
        r1 = r0 - alpha * c0
        z1 = r1 / precond
        turn = [gg[1, r] - alpha * gg[2, r] for r in range(2)]
        turn_sq = lane_sum(turn[0] * turn[0] + turn[1] * turn[1])
        turn_damp = lane_sum(cam_damp * (z1 * z1))
        rows = [lane_sum(r1 * z1), lane_sum(z1 * c0)]
        if last:
            base = [mv[r] + alpha * gg[1, r] for r in range(2)]
            y_base = mix(1.0, three(ybuf, 0), alpha, three(ybuf, 1))
            w_base = mix(1.0, three(wbuf, 0), alpha, three(wbuf, 1))
            hw_base = weighted(w_base)
            w1 = three(wbuf, 1)
            hw_one = weighted(w1)
            y1 = three(ybuf, 1)
            rows += [
                lane_sum(base[0] * base[0] + base[1] * base[1])
                - 2.0 * inner(y_base, w_base)
                + inner(w_base, hw_base),
                lane_sum(base[0] * gg[1, 0] + base[1] * gg[1, 1])
                - inner(y_base, w1)
                - inner(y1, w_base)
                + inner(w_base, hw_one),
                g1_sq - 2.0 * yw1 + inner(w1, hw_one),
            ]
            base_turn = lane_sum(base[0] * turn[0] + base[1] * turn[1])
            one_turn = lane_sum(gg[1, 0] * turn[0] + gg[1, 1] * turn[1])
        else:
            scale = [damping * (hess[c] + 1.0) for c in (0, 3, 5)]
            y_start = collect_wait(3, *pts_y)
            inv_next = [inv_b[1, c] for c in range(6)]
            held = [
                [scale[m] * wbuf[0, m] + y_start[m] for m in range(3)],
                [scale[m] * wbuf[1, m] + ybuf[1, m] for m in range(3)],
            ]
            ahead = [apply_inverse(inv_next, v) for v in held]
            spread_start(mix(1.0, ahead[0], alpha, ahead[1]) + ahead[1], *out_w)

        y = collect_wait(3, *pts)
        ybuf[2] = jnp.stack(y)
        w = apply_inverse([inv_b[step, c] for c in range(6)], y)
        wbuf[2] = jnp.stack(w)
        if last:
            spread_start(w, *out_s)
        else:
            held.append([scale[m] * w[m] + y[m] for m in range(3)])
            ahead.append(apply_inverse(inv_next, held[2]))
            spread_start([-alpha * (ahead[2][m] + w[m]) for m in range(3)], *out_s)
        y_turn = mix(1.0, three(ybuf, 1), -alpha, y)
        w_turn = mix(1.0, three(wbuf, 1), -alpha, w)
        yw = inner(y_turn, w_turn)
        rows.append(turn_sq - yw + turn_damp)
        if last:
            hw_turn = weighted(w_turn)
            rows += [
                base_turn
                - inner(y_base, w_turn)
                - inner(y_turn, w_base)
                + inner(w_base, hw_turn),
                one_turn - inner(y1, w_turn) - inner(y_turn, w1) + inner(w1, hw_turn),
                turn_sq - 2.0 * yw + inner(w_turn, hw_turn),
            ]
        total_start(step, rows)
        if not last:
            spread_start(w, *out_2)
            spread_wait(*out_w)
            near_fix = take_points(recv_w)
            near_one = take_points(recv_w, 3)
            spread_wait(*out_s)
            near_move = take_points(recv_s)
        else:
            spread_wait(*out_s)
            near = take_points(recv_s)
            eliminate(gg[2, 0], gg[2, 1], near, 2)
        dots = total_wait(step)
        fresh, cross = dots[0], dots[1]
        beta = fresh / resid_dot
        more = 1.0 + beta
        curve1 = dots[5 if last else 2] + 2.0 * beta * cross + beta * beta * curve
        alpha1 = fresh / curve1
        ca = alpha + alpha1 * more
        cb = -(alpha1 * alpha)
        update = update + alpha * z0 + alpha1 * (z1 + beta * z0)
        upd_sum = upd_sum + update
        step_sum = step_sum - (wbuf[0] + ca * wbuf[1] + cb * wbuf[2])
        if not last:
            step1 = alpha1 * more
            near = [
                near_fix[m] + step1 * near_one[m] + alpha1 * near_move[m] for m in range(3)
            ]
            for r in range(2):
                rs[r] = bk[0, r] + ca * bk[1, r] + cb * gg[2, r]
                mv[r] = gg[0, r] + ca * gg[1, r] + cb * gg[2, r]
            eliminate(rs[0] + mv[0], rs[1] + mv[1], near, 0)
            ybuf[0] = jnp.stack([held[0][m] + ca * held[1][m] + cb * held[2][m] for m in range(3)])
            wbuf[0] = jnp.stack(
                [ahead[0][m] + ca * ahead[1][m] + cb * ahead[2][m] for m in range(3)]
            )
        else:
            for r in range(2):
                res_o[pl.ds(r, TILES, stride=2), :] = bk[0, r] + ca * bk[1, r] + cb * bk[2, r]
            base_sq, base_one, one_sq = dots[2], dots[3], dots[4]
            base_dot, one_dot, turn_dot = dots[6], dots[7], dots[8]
            square = turn_dot + 2.0 * beta * one_dot + beta * beta * one_sq
            costs.append(
                0.5
                * (
                    base_sq
                    + 2.0 * alpha1 * (base_dot + beta * base_one)
                    + alpha1 * alpha1 * square
                )
            )
    for p in range(2):
        both = upd_sum[:, p, :]
        cam_o[:, 2 * p, :] = cam_r[:, 2 * p, :] + both[:, 0:64]
        cam_o[:, 2 * p + 1, :] = cam_r[:, 2 * p + 1, :] + both[:, 64:128]
    pt_o[...] = pt_r[...] + step_sum
    third = lax.broadcasted_iota(jnp.int32, (1, 3), 1)
    cost_o[...] = jnp.where(third == 0, costs[0], jnp.where(third == 1, costs[1], costs[2]))
    for a in range(2):
        hidden_drain(a)
        total_drain(a)


def hand_over(cam_i, pt_i, res_i, cost_i, cam_o, pt_o, res_o, cost_o):
    res_o[...] = res_i[...]
    cam_o[...] = cam_i[...]
    pt_o[...] = pt_i[...]
    cost_o[...] = cost_i[...]


def body(
    jac_cam,
    jac_pt,
    resid0,
    obs_count,
    tile_camera,
    tile_points,
    obs_camera,
    obs_point,
    cam_params,
    pt_params,
    cg_start,
):
    vmem = pl.BlockSpec(memory_space=pltpu.VMEM)
    hbm = pl.BlockSpec(memory_space=pltpu.HBM)
    big = (TILES, LANES)
    blk = (NBLK, LANES)
    dma = pltpu.SemaphoreType.DMA
    shapes = [
        jax.ShapeDtypeStruct((CPAR, 4, 64), F32),
        jax.ShapeDtypeStruct((3,) + blk, F32),
        jax.ShapeDtypeStruct((2 * TILES, LANES), F32),
        jax.ShapeDtypeStruct((1, 3), F32),
    ]
    results = pl.pallas_call(
        kernel,
        out_shape=shapes,
        in_specs=[pl.BlockSpec(memory_space=pltpu.SMEM)] + [hbm] * 11,
        out_specs=[vmem] * 4,
        scratch_shapes=[
            pltpu.VMEM((18,) + big, F32),
            pltpu.VMEM((6,) + big, F32),
            pltpu.VMEM((2,) + big, F32),
            pltpu.VMEM((2 * TILES, LANES), F32),
            pltpu.VMEM(big, jnp.int32),
            pltpu.VMEM(big, jnp.int32),
            pltpu.VMEM((1, LANES), jnp.int32),
            pltpu.VMEM((1, LANES), jnp.int32),
            pltpu.VMEM((1, LANES), jnp.int32),
            pltpu.VMEM((CPAR, 4, 64), F32),
            pltpu.VMEM((CPAR, 4, 64), F32),
            pltpu.VMEM((3,) + blk, F32),
            pltpu.VMEM((18,) + big, F32),
            pltpu.VMEM((6,) + big, F32),
            pltpu.VMEM((PAD + LANES, LANES), F32),
            pltpu.VMEM((CPAR, PAD + LANES, LANES), F32),
            pltpu.VMEM((CPAR, PAD + LANES, LANES), F32),
            pltpu.VMEM((2,) + big, jnp.int32),
            pltpu.VMEM((2,) + big, jnp.int32),
            pltpu.VMEM((2, 7) + big, F32),
            pltpu.VMEM(big, F32),
            pltpu.VMEM((2,) + big, F32),
            pltpu.VMEM(big, jnp.int32),
            pltpu.VMEM(big, F32),
            pltpu.VMEM(big, jnp.int32),
            pltpu.VMEM((SLOTS, 3 * TILES), BF16),
            pltpu.VMEM((3,) + big, F32),
            pltpu.VMEM((3, 2) + big, F32),
            pltpu.VMEM((3, 2) + big, F32),
            pltpu.VMEM((2,) + big, F32),
            pltpu.VMEM((9, 3) + blk, F32),
            pltpu.VMEM((8, 3) + blk, F32),
            pltpu.VMEM((9, 6) + blk, F32),
            pltpu.VMEM((8, 6) + blk, F32),
            pltpu.VMEM((9, 3) + blk, F32),
            pltpu.VMEM((8, 3) + blk, F32),
            pltpu.VMEM((3 * NBLK, LANES), F32),
            pltpu.VMEM((27 * NBLK, LANES), F32),
            pltpu.VMEM((6 * NBLK, LANES), F32),
            pltpu.VMEM((54 * NBLK, LANES), F32),
            pltpu.VMEM((3 * NBLK, LANES), F32),
            pltpu.VMEM((27 * NBLK, LANES), F32),
            pltpu.VMEM((6,) + blk, F32),
            pltpu.VMEM((2, 6) + blk, F32),
            pltpu.VMEM((3, 3) + blk, F32),
            pltpu.VMEM((3, 3) + blk, F32),
            pltpu.VMEM((CPAR, 2, LANES), F32),
            pltpu.VMEM((CPAR, 2, LANES), F32),
            pltpu.VMEM((2, 1, LANES), F32),
            pltpu.VMEM((2, GX * GY, LANES), F32),
            pltpu.VMEM((2, 1, LANES), F32),
            pltpu.VMEM((2, GX, LANES), F32),
            pltpu.VMEM((2, 1, LANES), F32),
            pltpu.VMEM((2, GY, LANES), F32),
            dma((11,)),
            pltpu.SMEM((2, LANES), jnp.int32),
        ]
        + [dma((8,))] * 12
        + [dma((2,))] * 6,
        compiler_params=pltpu.CompilerParams(
            collective_id=0, has_side_effects=True, vmem_limit_bytes=62 * 1024 * 1024
        ),
    )(
        tile_points[0, 0],
        jnp.transpose(jac_cam[0, 0], (1, 0, 2)),
        jnp.transpose(jac_pt[0, 0], (1, 0, 2)),
        resid0.reshape(2 * TILES, LANES),
        obs_camera[0, 0],
        obs_point[0, 0],
        obs_count[0],
        tile_camera[0],
        tile_points[0],
        jnp.transpose(cg_start[0, 0], (1, 0, 2)),
        jnp.transpose(cam_params[0, 0], (1, 0, 2)),
        jnp.transpose(pt_params[0, 0], (1, 0, 2)),
    )
    cam, pt, res, costs = pl.pallas_call(
        hand_over,
        out_shape=shapes,
        in_specs=[vmem] * 4,
        out_specs=[vmem] * 4,
    )(*results)
    cam_out = jnp.transpose(cam, (1, 0, 2))[None, None]
    pt_out = jnp.transpose(pt, (1, 0, 2))[None, None]
    return cam_out, pt_out, res.reshape(1, 1, TILES, 2, LANES), costs.reshape(3)


def solution(mesh):
    wide = P("gx", "gy", None, None, None)
    in_specs = (
        wide,
        wide,
        wide,
        P("gx", "gy", None),
        P("gx", "gy", None),
        P("gx", "gy", None),
        P("gx", "gy", None, None),
        P("gx", "gy", None, None),
        wide,
        wide,
        wide,
    )
    out_specs = (wide, wide, wide, P())
    return jax.shard_map(body, mesh=mesh, in_specs=in_specs, out_specs=out_specs, check_vma=False)
```

```python
import jax
import jax.numpy as jnp
from jax import lax
from jax.experimental import pallas as pl
from jax.experimental.pallas import tpu as pltpu
from jax.sharding import PartitionSpec as P

MESH = pl.DeviceIdType.MESH
CPAR = 9
NBLK = 16
LANES = 128
TILES = 128
SLOTS = 9 * NBLK
GX = 8
GY = 16
PAD = 64
STEPS = (1, 2, 4, 8, 16, 32, 64)
LAMBDAS = (1.0, 0.25)
PAIRS = ((0, 0), (0, 1), (0, 2), (1, 1), (1, 2), (2, 2))
OTHERS = (0, 1, 2, 3, 5, 6, 7, 8)
ORDER = tuple((OTHERS.index(n), n) for n in (0, 2, 6, 8, 3, 5, 1, 7))
F32 = jnp.float32
BF16 = jnp.bfloat16
GATHER = lax.GatherDimensionNumbers(
    offset_dims=(),
    collapsed_slice_dims=(1,),
    start_index_map=(1,),
    operand_batching_dims=(0,),
    start_indices_batching_dims=(0,),
)


def pick(x, idx):
    return lax.gather(
        x, idx[:, :, None], GATHER, (1, 1), mode=lax.GatherScatterMode.PROMISE_IN_BOUNDS
    )


def lane_ids(rows):
    return lax.broadcasted_iota(jnp.int32, (rows, LANES), 1)


def sort_lanes(key):
    flat = jnp.swapaxes(key.astype(F32), 0, 1).reshape(16, 8, LANES)
    regs = [flat[v] for v in range(16)]
    sub = lax.broadcasted_iota(jnp.int32, (8, LANES), 0)
    before = None
    size = 2
    while size <= LANES:
        if size >= 16:
            bit = size // 16
            sign = jnp.where((sub & bit) == 0, 1.0, -1.0)
            turn = sign if before is None else sign * before
            regs = [x * turn for x in regs]
            before = sign
        gap = size // 2
        while gap >= 1:
            if gap < 16:
                for v in range(16):
                    if v & gap == 0:
                        low = jnp.minimum(regs[v], regs[v + gap])
                        high = jnp.maximum(regs[v], regs[v + gap])
                        up = size >= 16 or v & size == 0
                        regs[v], regs[v + gap] = (low, high) if up else (high, low)
            else:
                g = gap // 16
                first = (sub & g) == 0
                for v in range(16):
                    x = regs[v]
                    other = jnp.where(
                        first, pltpu.roll(x, 8 - g, axis=0), pltpu.roll(x, g, axis=0)
                    )
                    regs[v] = jnp.where(first, jnp.minimum(x, other), jnp.maximum(x, other))
            gap //= 2
        size *= 2
    rows = jnp.swapaxes(jnp.concatenate(regs, axis=0), 0, 1)
    lane = lane_ids(LANES)
    return pick(rows, (lane & 15) * 8 + (lane >> 4)).astype(jnp.int32)


def last_at_most(seg, target):
    count = jnp.zeros_like(target)
    for step in (64, 32, 16, 8, 4, 2, 1):
        count = jnp.where(pick(seg, count + (step - 1)) <= target, count + step, count)
    return jnp.where(pick(seg, count) <= target, count + 1, count)


def column(row):
    return jnp.swapaxes(jnp.broadcast_to(row.astype(F32), (LANES, LANES)), 0, 1)


def invert(hess, damping):
    h00 = hess[0] + damping * (hess[0] + 1.0)
    h01, h02 = hess[1], hess[2]
    h11 = hess[3] + damping * (hess[3] + 1.0)
    h12 = hess[4]
    h22 = hess[5] + damping * (hess[5] + 1.0)
    c00 = h11 * h22 - h12 * h12
    c01 = h02 * h12 - h01 * h22
    c02 = h01 * h12 - h02 * h11
    c11 = h00 * h22 - h02 * h02
    c12 = h01 * h02 - h00 * h12
    c22 = h00 * h11 - h01 * h01
    det = h00 * c00 + h01 * c01 + h02 * c02
    return [c / det for c in (c00, c01, c02, c11, c12, c22)]


def apply_inverse(inv, y):
    return [
        inv[0] * y[0] + inv[1] * y[1] + inv[2] * y[2],
        inv[1] * y[0] + inv[3] * y[1] + inv[4] * y[2],
        inv[2] * y[0] + inv[4] * y[1] + inv[5] * y[2],
    ]


def lane_sum(x):
    while x.ndim > 2:
        x = jnp.sum(x, axis=0)
    return jnp.sum(x, axis=0, keepdims=True)


def kernel(
    slot_s,
    jc_h,
    jp_h,
    rs_h,
    cam_h,
    pt_h,
    count_h,
    tcam_h,
    tpts_h,
    start_h,
    cpar_h,
    ppar_h,
    cam_o,
    pt_o,
    res_o,
    cost_o,
    jc,
    jp,
    rs,
    rs_in,
    obs_cam,
    obs_pt,
    count_r,
    tcam_r,
    tpts_r,
    start_r,
    cam_r,
    pt_r,
    jct,
    jpt,
    seg_t,
    scan_a,
    scan_b,
    perm,
    endi,
    smask,
    hit_p,
    hit_c,
    pair_m,
    valid_m,
    idx_c,
    onehot,
    table,
    gg,
    bk,
    mv,
    contrib,
    recv_c,
    contrib_h,
    recv_h,
    contrib_y,
    recv_y,
    wsrc,
    recv_s,
    wsrc_w,
    recv_w,
    wsrc_2,
    recv_2,
    hess_b,
    inv_b,
    ybuf,
    wbuf,
    camvec,
    camacc,
    ar_src,
    arx,
    px_src,
    px_dst,
    py_src,
    py_dst,
    in_sem,
    row_s,
    cs_sem,
    cr_sem,
    hs_sem,
    hr_sem,
    ys_sem,
    yr_sem,
    ss_sem,
    sr_sem,
    ws_sem,
    wr_sem,
    s2_sem,
    r2_sem,
    as_sem,
    ar_sem,
    pxs_sem,
    pxr_sem,
    pys_sem,
    pyr_sem,
):
    me_x = lax.axis_index("gx")
    me_y = lax.axis_index("gy")

    def at(dx, dy):
        return (lax.rem(me_x + (dx + GX), GX), lax.rem(me_y + (dy + GY), GY))

    me = me_x * GY + me_y
    here = {}
    for n in OTHERS:
        a, b = divmod(n, 3)
        x, y = me_x + (a - 1), me_y + (b - 1)
        here[n] = (x >= 0) & (x < GX) & (y >= 0) & (y < GY)

    columns = {dx: lax.rem(me_x + dx, GX) for dx in range(GX)}

    def to_all(act):
        def row(j, carry):
            y = lax.rem(me_y + (lax.rem(j + 5, GY - 1) + 1), GY)
            for dx in (4, 3, 5, 2, 6, 1, 7, 0):
                act((columns[dx], y))
            return carry

        lax.fori_loop(0, GY - 1, row, 0)
        for dx in (4, 3, 5, 2, 6, 1, 7):
            act((columns[dx], me_y))

    pairs = [
        (pt_h, obs_pt),
        (jp_h, jp),
        (jc_h, jc),
        (cam_h, obs_cam),
        (rs_h, rs_in),
        (tcam_h, tcam_r),
        (count_h, count_r),
        (tpts_h, tpts_r),
        (start_h, start_r),
        (cpar_h, cam_r),
        (ppar_h, pt_r),
    ]
    copies = [
        pltpu.make_async_copy(src, dst, in_sem.at[i]) for i, (src, dst) in enumerate(pairs)
    ]
    for copy in copies:
        copy.start()

    for r, n in enumerate(OTHERS):

        @pl.when(jnp.logical_not(here[n]))
        def _(r=r, n=n):
            recv_c[r] = jnp.zeros_like(recv_c[r])
            recv_h[r] = jnp.zeros_like(recv_h[r])
            recv_y[r] = jnp.zeros_like(recv_y[r])
            for buf in (recv_s, recv_w, recv_2):
                per = buf.shape[0] // 9
                buf[n * per : (n + 1) * per, :] = jnp.zeros((per, LANES), F32)

    barrier = pltpu.get_barrier_semaphore()
    greeted = [(-1, -1), (-1, 1), (1, -1), (1, 1)]
    greeted += [(0, d) for d in range(1, GY)] + [(d, 0) for d in range(1, GX)]
    for dx, dy in greeted:
        pl.semaphore_signal(barrier, inc=1, device_id=at(dx, dy), device_id_type=MESH)

    seg_t[0:PAD, :] = jnp.full((PAD, LANES), -1.0, F32)
    for k in range(CPAR):
        scan_a[k, 0:PAD, :] = jnp.zeros((PAD, LANES), F32)
        scan_b[k, 0:PAD, :] = jnp.zeros((PAD, LANES), F32)
    lane = lane_ids(TILES)

    def order(kind, ids, target):
        key = sort_lanes(ids * LANES + lane)
        perm[kind] = key & (LANES - 1)
        seg = key >> 7
        count = last_at_most(seg, target)
        last = jnp.maximum(count - 1, 0)
        endi[kind] = last
        found = (count > 0) & (pick(seg, last) == target)
        seg_t[PAD : PAD + LANES, :] = jnp.swapaxes(seg.astype(F32), 0, 1)
        for i, d in enumerate(STEPS):
            same = seg_t[PAD : PAD + LANES, :] == seg_t[PAD - d : PAD + LANES - d, :]
            smask[kind, i] = jnp.where(same, 1.0, 0.0)
        return found

    def sorted_t(x, kind):
        return jnp.swapaxes(pick(x, perm[kind]), 0, 1)

    def summed(values, kind):
        count = len(values)
        src, dst = scan_a, scan_b
        for k in range(count):
            src[k, PAD : PAD + LANES, :] = values[k]
        for i, d in enumerate(STEPS):
            for k in range(count):
                dst[k, PAD : PAD + LANES, :] = (
                    src[k, PAD : PAD + LANES, :]
                    + src[k, PAD - d : PAD + LANES - d, :] * smask[kind, i]
                )
            src, dst = dst, src
        return [
            pick(jnp.swapaxes(src[k, PAD : PAD + LANES, :], 0, 1), endi[kind])
            for k in range(count)
        ]

    def put_points(values, dest):
        sums = jnp.concatenate([v * hit_p[...] for v in summed(values, 0)], axis=1)
        high = sums.astype(BF16)
        rest = sums - high.astype(F32)
        mid = rest.astype(BF16)
        low = (rest - mid.astype(F32)).astype(BF16)
        parts = jnp.concatenate([high, mid, low], axis=0)
        out = jnp.dot(onehot[...], parts, preferred_element_type=F32)
        for n in range(9):
            for m in range(len(values)):
                dest[n, m] = out[n * NBLK : (n + 1) * NBLK, m * LANES : (m + 1) * LANES]

    def put_cams(values):
        for k, sums in enumerate(summed(values, 1)):
            top = lane_sum(sums * hit_c[0])
            bottom = lane_sum(sums * hit_c[1])
            camacc[k] = jnp.concatenate([top, bottom], axis=0)
        return camacc[...]

    def take_cams(vector, b):
        camvec[...] = vector
        rows = 32

        def one(chunk, carry):
            where = pl.ds(pl.multiple_of(chunk * rows, rows), rows)
            idx = idx_c[where, :]
            second = pair_m[where, :] == 1
            e0 = jnp.zeros((rows, LANES), F32)
            e1 = jnp.zeros((rows, LANES), F32)
            for k in range(CPAR):
                v = camvec[k]
                src = jnp.where(
                    second,
                    jnp.broadcast_to(v[1:2], (rows, LANES)),
                    jnp.broadcast_to(v[0:1], (rows, LANES)),
                )
                got = pick(src, idx)
                e0 = e0 + jc[k, where, :] * got
                e1 = e1 + jc[CPAR + k, where, :] * got
            gg[b, 0, where, :] = e0 * valid_m[where, :]
            gg[b, 1, where, :] = e1 * valid_m[where, :]
            return carry

        lax.fori_loop(0, TILES // rows, one, 0)

    def to_points(e0, e1):
        t0, t1 = sorted_t(e0, 0), sorted_t(e1, 0)
        return [jpt[m] * t0 + jpt[3 + m] * t1 for m in range(3)]

    def collect_start(comps, src, dst, send_sem, recv_sem):
        for r, n in ORDER:
            a, b = divmod(n, 3)

            @pl.when(here[n])
            def _(r=r, n=n, a=a, b=b):
                pltpu.make_async_remote_copy(
                    src_ref=src.at[n, pl.ds(0, comps)],
                    dst_ref=dst.at[r, pl.ds(0, comps)],
                    send_sem=send_sem.at[r],
                    recv_sem=recv_sem.at[r],
                    device_id=at(a - 1, b - 1),
                    device_id_type=MESH,
                ).start()

    def collect_wait(comps, src, dst, send_sem, recv_sem):
        for sem, flip in ((recv_sem, True), (send_sem, False)):
            for r, n in enumerate(OTHERS):

                @pl.when(here[8 - n] if flip else here[n])
                def _(r=r, n=n, sem=sem):
                    pltpu.make_async_copy(
                        src.at[n, pl.ds(0, comps)], dst.at[r, pl.ds(0, comps)], sem.at[r]
                    ).wait()

        total = []
        for m in range(comps):
            s = src[4, m]
            for r in range(8):
                s = s + dst[r, m]
            total.append(s)
        return total

    pts = (contrib, recv_c, cs_sem, cr_sem)
    pts_h = (contrib_h, recv_h, hs_sem, hr_sem)
    pts_y = (contrib_y, recv_y, ys_sem, yr_sem)
    out_s = (wsrc, recv_s, ss_sem, sr_sem)
    out_w = (wsrc_w, recv_w, ws_sem, wr_sem)
    out_2 = (wsrc_2, recv_2, s2_sem, r2_sem)

    def spread_start(values, src, dst, send_sem, recv_sem):
        per = src.shape[0]
        for m, v in enumerate(values):
            src[m * NBLK : (m + 1) * NBLK, :] = v
            dst[4 * per + m * NBLK : 4 * per + (m + 1) * NBLK, :] = v
        for r, n in ORDER:
            a, b = divmod(n, 3)

            @pl.when(here[n])
            def _(r=r, n=n, a=a, b=b):
                pltpu.make_async_remote_copy(
                    src_ref=src,
                    dst_ref=dst.at[pl.ds((8 - n) * per, per)],
                    send_sem=send_sem.at[r],
                    recv_sem=recv_sem.at[r],
                    device_id=at(a - 1, b - 1),
                    device_id_type=MESH,
                ).start()

    def spread_wait(src, dst, send_sem, recv_sem):
        per = src.shape[0]
        for sem, flip in ((recv_sem, True), (send_sem, False)):
            for r, n in enumerate(OTHERS):

                @pl.when(here[8 - n] if flip else here[n])
                def _(r=r, n=n, sem=sem):
                    pltpu.make_async_copy(
                        src, dst.at[pl.ds((8 - n) * per, per)], sem.at[r]
                    ).wait()

    def take_points(src, first=0):
        per = src.shape[0] // 9

        def one(chunk, carry):
            for i in range(16):
                t = chunk * 16 + i
                row = row_s[0 if per == 3 * NBLK else 1, t] + first * NBLK
                for m in range(3):
                    table[m, pl.ds(t, 1), :] = src[pl.ds(row + m * NBLK, 1), :]
            return carry

        lax.fori_loop(0, TILES // 16, one, 0)
        return [pick(table[m], obs_pt[...]) for m in range(3)]

    def eliminate(e0, e1, near, b):
        bk[b, 0] = e0 - (jp[0] * near[0] + jp[1] * near[1] + jp[2] * near[2])
        bk[b, 1] = e1 - (jp[3] * near[0] + jp[4] * near[1] + jp[5] * near[2])

    def back_to_cams(b):
        t0, t1 = sorted_t(bk[b, 0], 1), sorted_t(bk[b, 1], 1)
        return put_cams([jct[k] * t0 + jct[CPAR + k] * t1 for k in range(CPAR)])

    def lane_row(rows):
        held = jnp.concatenate(rows + [jnp.zeros((16 - len(rows), LANES), F32)], axis=0)
        sums = jnp.sum(held, axis=1, keepdims=True)
        own = lax.broadcasted_iota(jnp.int32, (16, LANES), 0)
        return jnp.sum(jnp.where(lane_ids(16) == own, sums, 0.0), axis=0, keepdims=True)

    def apart(row, count):
        lane1 = lane_ids(1)
        return [
            jnp.sum(jnp.where(lane1 == i, row, 0.0), axis=1, keepdims=True) for i in range(count)
        ]

    def pass_start(src, dst, spot, peers, send_sem, recv_sem):
        for dx, dy in peers:
            pltpu.make_async_remote_copy(
                src_ref=src,
                dst_ref=dst.at[pl.ds(spot, 1)],
                send_sem=send_sem,
                recv_sem=recv_sem,
                device_id=at(dx, dy),
                device_id_type=MESH,
            ).start()

    def hidden_start(a, rows):
        row = lane_row(rows)
        px_src[a] = row
        px_dst[a, pl.ds(me_x, 1), :] = row
        peers = [(d, 0) for d in (4, 3, 5, 2, 6, 1, 7)]
        pass_start(px_src.at[a], px_dst.at[a], me_x, peers, pxs_sem.at[a], pxr_sem.at[a])

    def hidden_turn(a):
        rest = px_dst.at[a, pl.ds(0, GX - 1)]
        pltpu.make_async_copy(rest, rest, pxr_sem.at[a]).wait()
        row = jnp.sum(px_dst[a], axis=0, keepdims=True)
        py_src[a] = row
        py_dst[a, pl.ds(me_y, 1), :] = row
        peers = [(0, d) for d in (8, 7, 9, 6, 10, 5, 11, 4, 12, 3, 13, 2, 14, 1, 15)]
        pass_start(py_src.at[a], py_dst.at[a], me_y, peers, pys_sem.at[a], pyr_sem.at[a])

    def hidden_wait(a):
        rest = py_dst.at[a, pl.ds(0, GY - 1)]
        pltpu.make_async_copy(rest, rest, pyr_sem.at[a]).wait()
        return apart(jnp.sum(py_dst[a], axis=0, keepdims=True), 3)

    def hidden_drain(a):
        rest = px_dst.at[a, pl.ds(0, GX - 1)]
        pltpu.make_async_copy(rest, rest, pxs_sem.at[a]).wait()
        rest = py_dst.at[a, pl.ds(0, GY - 1)]
        pltpu.make_async_copy(rest, rest, pys_sem.at[a]).wait()

    def total_start(a, rows):
        row = lane_row(rows)
        ar_src[a] = row
        arx[a, pl.ds(me, 1), :] = row

        def send(device):
            pltpu.make_async_remote_copy(
                src_ref=ar_src.at[a],
                dst_ref=arx.at[a, pl.ds(me, 1)],
                send_sem=as_sem.at[a],
                recv_sem=ar_sem.at[a],
                device_id=device,
                device_id_type=MESH,
            ).start()

        to_all(send)

    def total_wait(a):
        pltpu.make_async_copy(
            arx.at[a, pl.ds(0, 127)], arx.at[a, pl.ds(0, 127)], ar_sem.at[a]
        ).wait()
        return apart(jnp.sum(arx[a], axis=0, keepdims=True), 9)

    def total_drain(a):
        pltpu.make_async_copy(
            arx.at[a, pl.ds(0, 127)], arx.at[a, pl.ds(0, 127)], as_sem.at[a]
        ).wait()

    copies[0].wait()
    hit_p[...] = jnp.where(order(0, obs_pt[...], lane), 1.0, 0.0)
    for copy in copies[1:]:
        copy.wait()
    slot_row = lax.broadcasted_iota(jnp.int32, (SLOTS, TILES), 0)
    hot = jnp.where(slot_row == tpts_r[...], 1.0, 0.0).astype(BF16)
    for i in range(3):
        onehot[:, i * TILES : (i + 1) * TILES] = hot
    valid_m[...] = jnp.where(lane < column(count_r[...]).astype(jnp.int32), 1.0, 0.0)
    valid = valid_m[...]
    tcam = column(tcam_r[...]).astype(jnp.int32)
    parity = tcam & 1
    pair = tcam >> 1
    pair_m[...] = pair
    idx_c[...] = parity * 64 + obs_cam[...]

    for k in range(2):
        rs[k] = rs_in[pl.ds(k, TILES, stride=2), :] * valid
    for k in range(6):
        jp[k] = jp[k] * valid
        jpt[k] = sorted_t(jp[k], 0)
    square = [jpt[i] * jpt[j] + jpt[3 + i] * jpt[3 + j] for i, j in PAIRS]
    put_points(square, contrib_h)
    pl.semaphore_wait(barrier, len(greeted))
    collect_start(6, *pts_h)

    start = jnp.concatenate(
        [
            jnp.concatenate([start_r[:, 2 * p, :], start_r[:, 2 * p + 1, :]], axis=1)[:, None, :]
            for p in range(2)
        ],
        axis=1,
    )
    take_cams(start, 0)
    for k in range(2):
        mv[k] = rs[k] + gg[0, k]
    put_points(to_points(mv[0], mv[1]), contrib)
    collect_start(3, *pts)
    put_points(to_points(gg[0, 0], gg[0, 1]), contrib_y)
    collect_start(3, *pts_y)
    def rows_of(t, carry):
        slot = slot_s[t]
        n, q = slot >> 4, slot & 15
        row_s[0, t] = n * (3 * NBLK) + q
        row_s[1, t] = n * (6 * NBLK) + q
        return carry

    lax.fori_loop(0, TILES, rows_of, 0)
    found = order(1, obs_cam[...], lane & 63)
    mine = found & ((lane >> 6) == parity)
    hit_c[0] = jnp.where(mine & (pair == 0), 1.0, 0.0)
    hit_c[1] = jnp.where(mine & (pair == 1), 1.0, 0.0)
    for k in range(18):
        jct[k] = sorted_t(jc[k] * valid, 1)
    cost_row = lane_sum(rs[...] * rs[...])
    hess = collect_wait(6, *pts_h)
    for c in range(6):
        hess_b[c] = hess[c]
    inv = invert(hess, LAMBDAS[0])
    for c in range(6):
        inv_b[0, c] = inv[c]
    ybuf[0] = jnp.stack(collect_wait(3, *pts))

    costs = []
    update = start
    upd_sum = jnp.zeros_like(start)
    step_sum = jnp.zeros((3, NBLK, LANES), F32)

    def weighted(w):
        h = [hess_b[c] for c in range(6)]
        return [
            h[0] * w[0] + h[1] * w[1] + h[2] * w[2],
            h[1] * w[0] + h[3] * w[1] + h[4] * w[2],
            h[2] * w[0] + h[4] * w[1] + h[5] * w[2],
        ]

    def inner(u, v):
        return lane_sum(u[0] * v[0] + u[1] * v[1] + u[2] * v[2])

    def three(buf, b):
        return [buf[b, m] for m in range(3)]

    def mix(p, u, q, v):
        return [p * u[m] + q * v[m] for m in range(3)]

    w0 = apply_inverse(inv, three(ybuf, 0))
    wbuf[0] = jnp.stack(w0)
    spread_start(w0, *out_s)
    diag = put_cams([jct[k] * jct[k] + jct[CPAR + k] * jct[CPAR + k] for k in range(CPAR)])
    inv = invert(hess, LAMBDAS[1])
    for c in range(6):
        inv_b[1, c] = inv[c]
    spread_wait(*out_s)
    near = take_points(recv_s)

    for step in range(2):
        damping = LAMBDAS[step]
        last = step == 1
        cam_damp = damping * (diag + 1.0)
        precond = diag + cam_damp
        if step == 0:
            eliminate(mv[0], mv[1], near, 0)
        r0 = -back_to_cams(0) - cam_damp * update
        z0 = r0 / precond

        take_cams(z0, 1)
        put_points(to_points(gg[1, 0], gg[1, 1]), contrib)
        collect_start(3, *pts)
        if last:
            spread_wait(*out_2)
            near = take_points(recv_2)
            for r in range(2):
                shift = jp[3 * r] * near[0] + jp[3 * r + 1] * near[1] + jp[3 * r + 2] * near[2]
                res = rs[r] - cb * shift
                rs[r] = res
                mv[r] = mv[r] + res
            cost_row = lane_sum(rs[...] * rs[...])
        y = collect_wait(3, *pts)
        ybuf[1] = jnp.stack(y)
        w = apply_inverse([inv_b[step, c] for c in range(6)], y)
        wbuf[1] = jnp.stack(w)
        spread_start(w, *out_s)
        g1_sq = lane_sum(gg[1, 0] * gg[1, 0] + gg[1, 1] * gg[1, 1])
        yw1 = inner(y, w)
        hidden_start(
            step,
            [lane_sum(r0 * z0), g1_sq - yw1 + lane_sum(cam_damp * (z0 * z0)), cost_row],
        )
        spread_wait(*out_s)
        near = take_points(recv_s)
        eliminate(gg[1, 0], gg[1, 1], near, 1)
        c0 = back_to_cams(1) + cam_damp * z0
        hidden_turn(step)
        u = c0 / precond

        take_cams(u, 2)
        put_points(to_points(gg[2, 0], gg[2, 1]), contrib)
        collect_start(3, *pts)

        dots = hidden_wait(step)
        resid_dot, curve = dots[0], dots[1]
        costs.append(0.5 * dots[2])
        alpha = resid_dot / curve
        r1 = r0 - alpha * c0
        z1 = r1 / precond
        turn = [gg[1, r] - alpha * gg[2, r] for r in range(2)]
        turn_sq = lane_sum(turn[0] * turn[0] + turn[1] * turn[1])
        turn_damp = lane_sum(cam_damp * (z1 * z1))
        rows = [lane_sum(r1 * z1), lane_sum(z1 * c0)]
        if last:
            base = [mv[r] + alpha * gg[1, r] for r in range(2)]
            y_base = mix(1.0, three(ybuf, 0), alpha, three(ybuf, 1))
            w_base = mix(1.0, three(wbuf, 0), alpha, three(wbuf, 1))
            hw_base = weighted(w_base)
            w1 = three(wbuf, 1)
            hw_one = weighted(w1)
            y1 = three(ybuf, 1)
            rows += [
                lane_sum(base[0] * base[0] + base[1] * base[1])
                - 2.0 * inner(y_base, w_base)
                + inner(w_base, hw_base),
                lane_sum(base[0] * gg[1, 0] + base[1] * gg[1, 1])
                - inner(y_base, w1)
                - inner(y1, w_base)
                + inner(w_base, hw_one),
                g1_sq - 2.0 * yw1 + inner(w1, hw_one),
            ]
            base_turn = lane_sum(base[0] * turn[0] + base[1] * turn[1])
            one_turn = lane_sum(gg[1, 0] * turn[0] + gg[1, 1] * turn[1])
        else:
            scale = [damping * (hess[c] + 1.0) for c in (0, 3, 5)]
            y_start = collect_wait(3, *pts_y)
            inv_next = [inv_b[1, c] for c in range(6)]
            held = [
                [scale[m] * wbuf[0, m] + y_start[m] for m in range(3)],
                [scale[m] * wbuf[1, m] + ybuf[1, m] for m in range(3)],
            ]
            ahead = [apply_inverse(inv_next, v) for v in held]
            spread_start(mix(1.0, ahead[0], alpha, ahead[1]) + ahead[1], *out_w)

        y = collect_wait(3, *pts)
        ybuf[2] = jnp.stack(y)
        w = apply_inverse([inv_b[step, c] for c in range(6)], y)
        wbuf[2] = jnp.stack(w)
        if not last:
            held.append([scale[m] * w[m] + y[m] for m in range(3)])
            ahead.append(apply_inverse(inv_next, held[2]))
        y_turn = mix(1.0, three(ybuf, 1), -alpha, y)
        w_turn = mix(1.0, three(wbuf, 1), -alpha, w)
        yw = inner(y_turn, w_turn)
        rows.append(turn_sq - yw + turn_damp)
        if last:
            hw_turn = weighted(w_turn)
            rows += [
                base_turn
                - inner(y_base, w_turn)
                - inner(y_turn, w_base)
                + inner(w_base, hw_turn),
                one_turn - inner(y1, w_turn) - inner(y_turn, w1) + inner(w1, hw_turn),
                turn_sq - 2.0 * yw + inner(w_turn, hw_turn),
            ]
        total_start(step, rows)
        if last:
            spread_start(w, *out_s)
        else:
            spread_start([-alpha * (ahead[2][m] + w[m]) for m in range(3)], *out_s)
        if not last:
            spread_wait(*out_w)
            near_fix = take_points(recv_w)
            near_one = take_points(recv_w, 3)
            spread_wait(*out_s)
            spread_start(w, *out_2)
            near_move = take_points(recv_s)
        else:
            spread_wait(*out_s)
            near = take_points(recv_s)
            eliminate(gg[2, 0], gg[2, 1], near, 2)
        dots = total_wait(step)
        fresh, cross = dots[0], dots[1]
        beta = fresh / resid_dot
        more = 1.0 + beta
        curve1 = dots[5 if last else 2] + 2.0 * beta * cross + beta * beta * curve
        alpha1 = fresh / curve1
        ca = alpha + alpha1 * more
        cb = -(alpha1 * alpha)
        update = update + alpha * z0 + alpha1 * (z1 + beta * z0)
        upd_sum = upd_sum + update
        step_sum = step_sum - (wbuf[0] + ca * wbuf[1] + cb * wbuf[2])
        if not last:
            step1 = alpha1 * more
            near = [
                near_fix[m] + step1 * near_one[m] + alpha1 * near_move[m] for m in range(3)
            ]
            for r in range(2):
                rs[r] = bk[0, r] + ca * bk[1, r] + cb * gg[2, r]
                mv[r] = gg[0, r] + ca * gg[1, r] + cb * gg[2, r]
            eliminate(rs[0] + mv[0], rs[1] + mv[1], near, 0)
            ybuf[0] = jnp.stack([held[0][m] + ca * held[1][m] + cb * held[2][m] for m in range(3)])
            wbuf[0] = jnp.stack(
                [ahead[0][m] + ca * ahead[1][m] + cb * ahead[2][m] for m in range(3)]
            )
        else:
            for r in range(2):
                res_o[pl.ds(r, TILES, stride=2), :] = bk[0, r] + ca * bk[1, r] + cb * bk[2, r]
            base_sq, base_one, one_sq = dots[2], dots[3], dots[4]
            base_dot, one_dot, turn_dot = dots[6], dots[7], dots[8]
            square = turn_dot + 2.0 * beta * one_dot + beta * beta * one_sq
            costs.append(
                0.5
                * (
                    base_sq
                    + 2.0 * alpha1 * (base_dot + beta * base_one)
                    + alpha1 * alpha1 * square
                )
            )
    for p in range(2):
        both = upd_sum[:, p, :]
        cam_o[:, 2 * p, :] = cam_r[:, 2 * p, :] + both[:, 0:64]
        cam_o[:, 2 * p + 1, :] = cam_r[:, 2 * p + 1, :] + both[:, 64:128]
    pt_o[...] = pt_r[...] + step_sum
    third = lax.broadcasted_iota(jnp.int32, (1, 3), 1)
    cost_o[...] = jnp.where(third == 0, costs[0], jnp.where(third == 1, costs[1], costs[2]))
    for a in range(2):
        hidden_drain(a)
        total_drain(a)


def hand_over(cam_i, pt_i, res_i, cost_i, cam_o, pt_o, res_o, cost_o):
    res_o[...] = res_i[...]
    cam_o[...] = cam_i[...]
    pt_o[...] = pt_i[...]
    cost_o[...] = cost_i[...]


def body(
    jac_cam,
    jac_pt,
    resid0,
    obs_count,
    tile_camera,
    tile_points,
    obs_camera,
    obs_point,
    cam_params,
    pt_params,
    cg_start,
):
    vmem = pl.BlockSpec(memory_space=pltpu.VMEM)
    hbm = pl.BlockSpec(memory_space=pltpu.HBM)
    big = (TILES, LANES)
    blk = (NBLK, LANES)
    dma = pltpu.SemaphoreType.DMA
    shapes = [
        jax.ShapeDtypeStruct((CPAR, 4, 64), F32),
        jax.ShapeDtypeStruct((3,) + blk, F32),
        jax.ShapeDtypeStruct((2 * TILES, LANES), F32),
        jax.ShapeDtypeStruct((1, 3), F32),
    ]
    results = pl.pallas_call(
        kernel,
        out_shape=shapes,
        in_specs=[pl.BlockSpec(memory_space=pltpu.SMEM)] + [hbm] * 11,
        out_specs=[vmem] * 4,
        scratch_shapes=[
            pltpu.VMEM((18,) + big, F32),
            pltpu.VMEM((6,) + big, F32),
            pltpu.VMEM((2,) + big, F32),
            pltpu.VMEM((2 * TILES, LANES), F32),
            pltpu.VMEM(big, jnp.int32),
            pltpu.VMEM(big, jnp.int32),
            pltpu.VMEM((1, LANES), jnp.int32),
            pltpu.VMEM((1, LANES), jnp.int32),
            pltpu.VMEM((1, LANES), jnp.int32),
            pltpu.VMEM((CPAR, 4, 64), F32),
            pltpu.VMEM((CPAR, 4, 64), F32),
            pltpu.VMEM((3,) + blk, F32),
            pltpu.VMEM((18,) + big, F32),
            pltpu.VMEM((6,) + big, F32),
            pltpu.VMEM((PAD + LANES, LANES), F32),
            pltpu.VMEM((CPAR, PAD + LANES, LANES), F32),
            pltpu.VMEM((CPAR, PAD + LANES, LANES), F32),
            pltpu.VMEM((2,) + big, jnp.int32),
            pltpu.VMEM((2,) + big, jnp.int32),
            pltpu.VMEM((2, 7) + big, F32),
            pltpu.VMEM(big, F32),
            pltpu.VMEM((2,) + big, F32),
            pltpu.VMEM(big, jnp.int32),
            pltpu.VMEM(big, F32),
            pltpu.VMEM(big, jnp.int32),
            pltpu.VMEM((SLOTS, 3 * TILES), BF16),
            pltpu.VMEM((3,) + big, F32),
            pltpu.VMEM((3, 2) + big, F32),
            pltpu.VMEM((3, 2) + big, F32),
            pltpu.VMEM((2,) + big, F32),
            pltpu.VMEM((9, 3) + blk, F32),
            pltpu.VMEM((8, 3) + blk, F32),
            pltpu.VMEM((9, 6) + blk, F32),
            pltpu.VMEM((8, 6) + blk, F32),
            pltpu.VMEM((9, 3) + blk, F32),
            pltpu.VMEM((8, 3) + blk, F32),
            pltpu.VMEM((3 * NBLK, LANES), F32),
            pltpu.VMEM((27 * NBLK, LANES), F32),
            pltpu.VMEM((6 * NBLK, LANES), F32),
            pltpu.VMEM((54 * NBLK, LANES), F32),
            pltpu.VMEM((3 * NBLK, LANES), F32),
            pltpu.VMEM((27 * NBLK, LANES), F32),
            pltpu.VMEM((6,) + blk, F32),
            pltpu.VMEM((2, 6) + blk, F32),
            pltpu.VMEM((3, 3) + blk, F32),
            pltpu.VMEM((3, 3) + blk, F32),
            pltpu.VMEM((CPAR, 2, LANES), F32),
            pltpu.VMEM((CPAR, 2, LANES), F32),
            pltpu.VMEM((2, 1, LANES), F32),
            pltpu.VMEM((2, GX * GY, LANES), F32),
            pltpu.VMEM((2, 1, LANES), F32),
            pltpu.VMEM((2, GX, LANES), F32),
            pltpu.VMEM((2, 1, LANES), F32),
            pltpu.VMEM((2, GY, LANES), F32),
            dma((11,)),
            pltpu.SMEM((2, LANES), jnp.int32),
        ]
        + [dma((8,))] * 12
        + [dma((2,))] * 6,
        compiler_params=pltpu.CompilerParams(
            collective_id=0, has_side_effects=True, vmem_limit_bytes=62 * 1024 * 1024
        ),
    )(
        tile_points[0, 0],
        jnp.transpose(jac_cam[0, 0], (1, 0, 2)),
        jnp.transpose(jac_pt[0, 0], (1, 0, 2)),
        resid0.reshape(2 * TILES, LANES),
        obs_camera[0, 0],
        obs_point[0, 0],
        obs_count[0],
        tile_camera[0],
        tile_points[0],
        jnp.transpose(cg_start[0, 0], (1, 0, 2)),
        jnp.transpose(cam_params[0, 0], (1, 0, 2)),
        jnp.transpose(pt_params[0, 0], (1, 0, 2)),
    )
    cam, pt, res, costs = pl.pallas_call(
        hand_over,
        out_shape=shapes,
        in_specs=[vmem] * 4,
        out_specs=[vmem] * 4,
    )(*results)
    cam_out = jnp.transpose(cam, (1, 0, 2))[None, None]
    pt_out = jnp.transpose(pt, (1, 0, 2))[None, None]
    return cam_out, pt_out, res.reshape(1, 1, TILES, 2, LANES), costs.reshape(3)


def solution(mesh):
    wide = P("gx", "gy", None, None, None)
    in_specs = (
        wide,
        wide,
        wide,
        P("gx", "gy", None),
        P("gx", "gy", None),
        P("gx", "gy", None),
        P("gx", "gy", None, None),
        P("gx", "gy", None, None),
        wide,
        wide,
        wide,
    )
    out_specs = (wide, wide, wide, P())
    return jax.shard_map(body, mesh=mesh, in_specs=in_specs, out_specs=out_specs, check_vma=False)
```

```python
import jax
import jax.numpy as jnp
from jax import lax
from jax.experimental import pallas as pl
from jax.experimental.pallas import tpu as pltpu
from jax.sharding import PartitionSpec as P

MESH = pl.DeviceIdType.MESH
CPAR = 9
NBLK = 16
LANES = 128
TILES = 128
SLOTS = 9 * NBLK
GX = 8
GY = 16
CHIPS = GX * GY // 2
PAD = 64
STEPS = (1, 2, 4, 8, 16, 32, 64)
LAMBDAS = (1.0, 0.25)
PAIRS = ((0, 0), (0, 1), (0, 2), (1, 1), (1, 2), (2, 2))
OTHERS = (0, 1, 2, 3, 5, 6, 7, 8)
ORDER = tuple((OTHERS.index(n), n) for n in (0, 2, 6, 8, 3, 5, 1, 7))
F32 = jnp.float32
BF16 = jnp.bfloat16
GATHER = lax.GatherDimensionNumbers(
    offset_dims=(),
    collapsed_slice_dims=(1,),
    start_index_map=(1,),
    operand_batching_dims=(0,),
    start_indices_batching_dims=(0,),
)


def pick(x, idx):
    return lax.gather(
        x, idx[:, :, None], GATHER, (1, 1), mode=lax.GatherScatterMode.PROMISE_IN_BOUNDS
    )


def lane_ids(rows):
    return lax.broadcasted_iota(jnp.int32, (rows, LANES), 1)


def sort_lanes(key):
    flat = jnp.swapaxes(key.astype(F32), 0, 1).reshape(16, 8, LANES)
    regs = [flat[v] for v in range(16)]
    sub = lax.broadcasted_iota(jnp.int32, (8, LANES), 0)
    before = None
    size = 2
    while size <= LANES:
        if size >= 16:
            bit = size // 16
            sign = jnp.where((sub & bit) == 0, 1.0, -1.0)
            turn = sign if before is None else sign * before
            regs = [x * turn for x in regs]
            before = sign
        gap = size // 2
        while gap >= 1:
            if gap < 16:
                for v in range(16):
                    if v & gap == 0:
                        low = jnp.minimum(regs[v], regs[v + gap])
                        high = jnp.maximum(regs[v], regs[v + gap])
                        up = size >= 16 or v & size == 0
                        regs[v], regs[v + gap] = (low, high) if up else (high, low)
            else:
                g = gap // 16
                first = (sub & g) == 0
                for v in range(16):
                    x = regs[v]
                    other = jnp.where(
                        first, pltpu.roll(x, 8 - g, axis=0), pltpu.roll(x, g, axis=0)
                    )
                    regs[v] = jnp.where(first, jnp.minimum(x, other), jnp.maximum(x, other))
            gap //= 2
        size *= 2
    rows = jnp.swapaxes(jnp.concatenate(regs, axis=0), 0, 1)
    lane = lane_ids(LANES)
    return pick(rows, (lane & 15) * 8 + (lane >> 4)).astype(jnp.int32)


def last_at_most(seg, target):
    count = jnp.zeros_like(target)
    for step in (64, 32, 16, 8, 4, 2, 1):
        count = jnp.where(pick(seg, count + (step - 1)) <= target, count + step, count)
    return jnp.where(pick(seg, count) <= target, count + 1, count)


def column(row):
    return jnp.swapaxes(jnp.broadcast_to(row.astype(F32), (LANES, LANES)), 0, 1)


def invert(hess, damping):
    h00 = hess[0] + damping * (hess[0] + 1.0)
    h01, h02 = hess[1], hess[2]
    h11 = hess[3] + damping * (hess[3] + 1.0)
    h12 = hess[4]
    h22 = hess[5] + damping * (hess[5] + 1.0)
    c00 = h11 * h22 - h12 * h12
    c01 = h02 * h12 - h01 * h22
    c02 = h01 * h12 - h02 * h11
    c11 = h00 * h22 - h02 * h02
    c12 = h01 * h02 - h00 * h12
    c22 = h00 * h11 - h01 * h01
    det = h00 * c00 + h01 * c01 + h02 * c02
    return [c / det for c in (c00, c01, c02, c11, c12, c22)]


def apply_inverse(inv, y):
    return [
        inv[0] * y[0] + inv[1] * y[1] + inv[2] * y[2],
        inv[1] * y[0] + inv[3] * y[1] + inv[4] * y[2],
        inv[2] * y[0] + inv[4] * y[1] + inv[5] * y[2],
    ]


def lane_sum(x):
    while x.ndim > 2:
        x = jnp.sum(x, axis=0)
    return jnp.sum(x, axis=0, keepdims=True)


def kernel(
    slot_s,
    jc_h,
    jp_h,
    rs_h,
    cam_h,
    pt_h,
    count_h,
    tcam_h,
    tpts_h,
    start_h,
    cpar_h,
    ppar_h,
    cam_o,
    pt_o,
    res_o,
    cost_o,
    jc,
    jp,
    rs,
    rs_in,
    obs_cam,
    obs_pt,
    count_r,
    tcam_r,
    tpts_r,
    start_r,
    cam_r,
    pt_r,
    jct,
    jpt,
    seg_t,
    scan_a,
    scan_b,
    perm,
    endi,
    smask,
    hit_p,
    hit_c,
    pair_m,
    valid_m,
    idx_c,
    onehot,
    table,
    gg,
    bk,
    mv,
    contrib,
    recv_c,
    contrib_h,
    recv_h,
    contrib_y,
    recv_y,
    wsrc,
    recv_s,
    wsrc_w,
    recv_w,
    wsrc_2,
    recv_2,
    hess_b,
    inv_b,
    ybuf,
    wbuf,
    camvec,
    camacc,
    pair_src,
    pair_dst,
    ar_src,
    arx,
    px_src,
    px_dst,
    py_src,
    py_dst,
    in_sem,
    row_s,
    cs_sem,
    cr_sem,
    hs_sem,
    hr_sem,
    ys_sem,
    yr_sem,
    ss_sem,
    sr_sem,
    ws_sem,
    wr_sem,
    s2_sem,
    r2_sem,
    ps_sem,
    pr_sem,
    as_sem,
    ar_sem,
    pxs_sem,
    pxr_sem,
    pys_sem,
    pyr_sem,
):
    me_x = lax.axis_index("gx")
    me_y = lax.axis_index("gy")

    def at(dx, dy):
        return (lax.rem(me_x + (dx + GX), GX), lax.rem(me_y + (dy + GY), GY))

    me = me_x * GY + me_y
    here = {}
    for n in OTHERS:
        a, b = divmod(n, 3)
        x, y = me_x + (a - 1), me_y + (b - 1)
        here[n] = (x >= 0) & (x < GX) & (y >= 0) & (y < GY)

    partner = (me_x + 1 - 2 * lax.rem(me_x, 2), me_y)
    chip = (me_x // 2) * GY + me_y
    columns = {dx: lax.rem(me_x + dx, GX) for dx in range(0, GX, 2)}

    def to_chips(act):
        def row(j, carry):
            y = lax.rem(me_y + (lax.rem(j + 5, GY - 1) + 1), GY)
            for dx in (4, 2, 6, 0):
                act((columns[dx], y))
            return carry

        lax.fori_loop(0, GY - 1, row, 0)
        for dx in (4, 2, 6):
            act((columns[dx], me_y))

    pairs = [
        (pt_h, obs_pt),
        (jp_h, jp),
        (jc_h, jc),
        (cam_h, obs_cam),
        (rs_h, rs_in),
        (tcam_h, tcam_r),
        (count_h, count_r),
        (tpts_h, tpts_r),
        (start_h, start_r),
        (cpar_h, cam_r),
        (ppar_h, pt_r),
    ]
    copies = [
        pltpu.make_async_copy(src, dst, in_sem.at[i]) for i, (src, dst) in enumerate(pairs)
    ]
    for copy in copies:
        copy.start()

    for r, n in enumerate(OTHERS):

        @pl.when(jnp.logical_not(here[n]))
        def _(r=r, n=n):
            recv_c[r] = jnp.zeros_like(recv_c[r])
            recv_h[r] = jnp.zeros_like(recv_h[r])
            recv_y[r] = jnp.zeros_like(recv_y[r])
            for buf in (recv_s, recv_w, recv_2):
                per = buf.shape[0] // 9
                buf[n * per : (n + 1) * per, :] = jnp.zeros((per, LANES), F32)

    barrier = pltpu.get_barrier_semaphore()
    greeted = [(-1, -1), (-1, 1), (1, -1), (1, 1)]
    greeted += [(0, d) for d in range(1, GY)] + [(d, 0) for d in range(1, GX)]
    for dx, dy in greeted:
        pl.semaphore_signal(barrier, inc=1, device_id=at(dx, dy), device_id_type=MESH)

    seg_t[0:PAD, :] = jnp.full((PAD, LANES), -1.0, F32)
    for k in range(CPAR):
        scan_a[k, 0:PAD, :] = jnp.zeros((PAD, LANES), F32)
        scan_b[k, 0:PAD, :] = jnp.zeros((PAD, LANES), F32)
    lane = lane_ids(TILES)

    def order(kind, ids, target):
        key = sort_lanes(ids * LANES + lane)
        perm[kind] = key & (LANES - 1)
        seg = key >> 7
        count = last_at_most(seg, target)
        last = jnp.maximum(count - 1, 0)
        endi[kind] = last
        found = (count > 0) & (pick(seg, last) == target)
        seg_t[PAD : PAD + LANES, :] = jnp.swapaxes(seg.astype(F32), 0, 1)
        for i, d in enumerate(STEPS):
            same = seg_t[PAD : PAD + LANES, :] == seg_t[PAD - d : PAD + LANES - d, :]
            smask[kind, i] = jnp.where(same, 1.0, 0.0)
        return found

    def sorted_t(x, kind):
        return jnp.swapaxes(pick(x, perm[kind]), 0, 1)

    def summed(values, kind):
        count = len(values)
        src, dst = scan_a, scan_b
        for k in range(count):
            src[k, PAD : PAD + LANES, :] = values[k]
        for i, d in enumerate(STEPS):
            for k in range(count):
                dst[k, PAD : PAD + LANES, :] = (
                    src[k, PAD : PAD + LANES, :]
                    + src[k, PAD - d : PAD + LANES - d, :] * smask[kind, i]
                )
            src, dst = dst, src
        return [
            pick(jnp.swapaxes(src[k, PAD : PAD + LANES, :], 0, 1), endi[kind])
            for k in range(count)
        ]

    def put_points(values, dest):
        sums = jnp.concatenate([v * hit_p[...] for v in summed(values, 0)], axis=1)
        high = sums.astype(BF16)
        rest = sums - high.astype(F32)
        mid = rest.astype(BF16)
        low = (rest - mid.astype(F32)).astype(BF16)
        parts = jnp.concatenate([high, mid, low], axis=0)
        out = jnp.dot(onehot[...], parts, preferred_element_type=F32)
        for n in range(9):
            for m in range(len(values)):
                dest[n, m] = out[n * NBLK : (n + 1) * NBLK, m * LANES : (m + 1) * LANES]

    def put_cams(values):
        for k, sums in enumerate(summed(values, 1)):
            top = lane_sum(sums * hit_c[0])
            bottom = lane_sum(sums * hit_c[1])
            camacc[k] = jnp.concatenate([top, bottom], axis=0)
        return camacc[...]

    def take_cams(vector, b):
        camvec[...] = vector
        rows = 32

        def one(chunk, carry):
            where = pl.ds(pl.multiple_of(chunk * rows, rows), rows)
            idx = idx_c[where, :]
            second = pair_m[where, :] == 1
            e0 = jnp.zeros((rows, LANES), F32)
            e1 = jnp.zeros((rows, LANES), F32)
            for k in range(CPAR):
                v = camvec[k]
                src = jnp.where(
                    second,
                    jnp.broadcast_to(v[1:2], (rows, LANES)),
                    jnp.broadcast_to(v[0:1], (rows, LANES)),
                )
                got = pick(src, idx)
                e0 = e0 + jc[k, where, :] * got
                e1 = e1 + jc[CPAR + k, where, :] * got
            gg[b, 0, where, :] = e0 * valid_m[where, :]
            gg[b, 1, where, :] = e1 * valid_m[where, :]
            return carry

        lax.fori_loop(0, TILES // rows, one, 0)

    def to_points(e0, e1):
        t0, t1 = sorted_t(e0, 0), sorted_t(e1, 0)
        return [jpt[m] * t0 + jpt[3 + m] * t1 for m in range(3)]

    def collect_start(comps, src, dst, send_sem, recv_sem):
        for r, n in ORDER:
            a, b = divmod(n, 3)

            @pl.when(here[n])
            def _(r=r, n=n, a=a, b=b):
                pltpu.make_async_remote_copy(
                    src_ref=src.at[n, pl.ds(0, comps)],
                    dst_ref=dst.at[r, pl.ds(0, comps)],
                    send_sem=send_sem.at[r],
                    recv_sem=recv_sem.at[r],
                    device_id=at(a - 1, b - 1),
                    device_id_type=MESH,
                ).start()

    def collect_wait(comps, src, dst, send_sem, recv_sem):
        for sem, flip in ((recv_sem, True), (send_sem, False)):
            for r, n in enumerate(OTHERS):

                @pl.when(here[8 - n] if flip else here[n])
                def _(r=r, n=n, sem=sem):
                    pltpu.make_async_copy(
                        src.at[n, pl.ds(0, comps)], dst.at[r, pl.ds(0, comps)], sem.at[r]
                    ).wait()

        total = []
        for m in range(comps):
            s = src[4, m]
            for r in range(8):
                s = s + dst[r, m]
            total.append(s)
        return total

    pts = (contrib, recv_c, cs_sem, cr_sem)
    pts_h = (contrib_h, recv_h, hs_sem, hr_sem)
    pts_y = (contrib_y, recv_y, ys_sem, yr_sem)
    out_s = (wsrc, recv_s, ss_sem, sr_sem)
    out_w = (wsrc_w, recv_w, ws_sem, wr_sem)
    out_2 = (wsrc_2, recv_2, s2_sem, r2_sem)

    def spread_start(values, src, dst, send_sem, recv_sem):
        per = src.shape[0]
        for m, v in enumerate(values):
            src[m * NBLK : (m + 1) * NBLK, :] = v
            dst[4 * per + m * NBLK : 4 * per + (m + 1) * NBLK, :] = v
        for r, n in ORDER:
            a, b = divmod(n, 3)

            @pl.when(here[n])
            def _(r=r, n=n, a=a, b=b):
                pltpu.make_async_remote_copy(
                    src_ref=src,
                    dst_ref=dst.at[pl.ds((8 - n) * per, per)],
                    send_sem=send_sem.at[r],
                    recv_sem=recv_sem.at[r],
                    device_id=at(a - 1, b - 1),
                    device_id_type=MESH,
                ).start()

    def spread_wait(src, dst, send_sem, recv_sem):
        per = src.shape[0]
        for sem, flip in ((recv_sem, True), (send_sem, False)):
            for r, n in enumerate(OTHERS):

                @pl.when(here[8 - n] if flip else here[n])
                def _(r=r, n=n, sem=sem):
                    pltpu.make_async_copy(
                        src, dst.at[pl.ds((8 - n) * per, per)], sem.at[r]
                    ).wait()

    def take_points(src, first=0):
        per = src.shape[0] // 9

        def one(chunk, carry):
            for i in range(16):
                t = chunk * 16 + i
                row = row_s[0 if per == 3 * NBLK else 1, t] + first * NBLK
                for m in range(3):
                    table[m, pl.ds(t, 1), :] = src[pl.ds(row + m * NBLK, 1), :]
            return carry

        lax.fori_loop(0, TILES // 16, one, 0)
        return [pick(table[m], obs_pt[...]) for m in range(3)]

    def eliminate(e0, e1, near, b):
        bk[b, 0] = e0 - (jp[0] * near[0] + jp[1] * near[1] + jp[2] * near[2])
        bk[b, 1] = e1 - (jp[3] * near[0] + jp[4] * near[1] + jp[5] * near[2])

    def back_to_cams(b):
        t0, t1 = sorted_t(bk[b, 0], 1), sorted_t(bk[b, 1], 1)
        return put_cams([jct[k] * t0 + jct[CPAR + k] * t1 for k in range(CPAR)])

    def lane_row(rows):
        held = jnp.concatenate(rows + [jnp.zeros((16 - len(rows), LANES), F32)], axis=0)
        sums = jnp.sum(held, axis=1, keepdims=True)
        own = lax.broadcasted_iota(jnp.int32, (16, LANES), 0)
        return jnp.sum(jnp.where(lane_ids(16) == own, sums, 0.0), axis=0, keepdims=True)

    def apart(row, count):
        lane1 = lane_ids(1)
        return [
            jnp.sum(jnp.where(lane1 == i, row, 0.0), axis=1, keepdims=True) for i in range(count)
        ]

    def pass_start(src, dst, spot, peers, send_sem, recv_sem):
        for dx, dy in peers:
            pltpu.make_async_remote_copy(
                src_ref=src,
                dst_ref=dst.at[pl.ds(spot, 1)],
                send_sem=send_sem,
                recv_sem=recv_sem,
                device_id=at(dx, dy),
                device_id_type=MESH,
            ).start()

    def hidden_start(a, rows):
        row = lane_row(rows)
        px_src[a] = row
        px_dst[a, pl.ds(me_x, 1), :] = row
        peers = [(d, 0) for d in (4, 3, 5, 2, 6, 1, 7)]
        pass_start(px_src.at[a], px_dst.at[a], me_x, peers, pxs_sem.at[a], pxr_sem.at[a])

    def hidden_turn(a):
        rest = px_dst.at[a, pl.ds(0, GX - 1)]
        pltpu.make_async_copy(rest, rest, pxr_sem.at[a]).wait()
        row = jnp.sum(px_dst[a], axis=0, keepdims=True)
        py_src[a] = row
        py_dst[a, pl.ds(me_y, 1), :] = row
        peers = [(0, d) for d in (8, 7, 9, 6, 10, 5, 11, 4, 12, 3, 13, 2, 14, 1, 15)]
        pass_start(py_src.at[a], py_dst.at[a], me_y, peers, pys_sem.at[a], pyr_sem.at[a])

    def hidden_wait(a):
        rest = py_dst.at[a, pl.ds(0, GY - 1)]
        pltpu.make_async_copy(rest, rest, pyr_sem.at[a]).wait()
        return apart(jnp.sum(py_dst[a], axis=0, keepdims=True), 3)

    def hidden_drain(a):
        rest = px_dst.at[a, pl.ds(0, GX - 1)]
        pltpu.make_async_copy(rest, rest, pxs_sem.at[a]).wait()
        rest = py_dst.at[a, pl.ds(0, GY - 1)]
        pltpu.make_async_copy(rest, rest, pys_sem.at[a]).wait()

    def total_start(a, rows):
        row = lane_row(rows)
        pair_src[a] = row
        pltpu.make_async_remote_copy(
            src_ref=pair_src.at[a],
            dst_ref=pair_dst.at[a],
            send_sem=ps_sem.at[a],
            recv_sem=pr_sem.at[a],
            device_id=partner,
            device_id_type=MESH,
        ).start()

    def total_turn(a):
        pltpu.make_async_copy(pair_src.at[a], pair_dst.at[a], pr_sem.at[a]).wait()
        row = pair_src[a] + pair_dst[a]
        ar_src[a] = row
        arx[a, pl.ds(chip, 1), :] = row

        def send(device):
            pltpu.make_async_remote_copy(
                src_ref=ar_src.at[a],
                dst_ref=arx.at[a, pl.ds(chip, 1)],
                send_sem=as_sem.at[a],
                recv_sem=ar_sem.at[a],
                device_id=device,
                device_id_type=MESH,
            ).start()

        to_chips(send)

    def total_wait(a):
        rest = arx.at[a, pl.ds(0, CHIPS - 1)]
        pltpu.make_async_copy(rest, rest, ar_sem.at[a]).wait()
        return apart(jnp.sum(arx[a], axis=0, keepdims=True), 9)

    def total_drain(a):
        pltpu.make_async_copy(pair_src.at[a], pair_dst.at[a], ps_sem.at[a]).wait()
        rest = arx.at[a, pl.ds(0, CHIPS - 1)]
        pltpu.make_async_copy(rest, rest, as_sem.at[a]).wait()

    copies[0].wait()
    hit_p[...] = jnp.where(order(0, obs_pt[...], lane), 1.0, 0.0)
    for copy in copies[1:]:
        copy.wait()
    slot_row = lax.broadcasted_iota(jnp.int32, (SLOTS, TILES), 0)
    hot = jnp.where(slot_row == tpts_r[...], 1.0, 0.0).astype(BF16)
    for i in range(3):
        onehot[:, i * TILES : (i + 1) * TILES] = hot
    valid_m[...] = jnp.where(lane < column(count_r[...]).astype(jnp.int32), 1.0, 0.0)
    valid = valid_m[...]
    tcam = column(tcam_r[...]).astype(jnp.int32)
    parity = tcam & 1
    pair = tcam >> 1
    pair_m[...] = pair
    idx_c[...] = parity * 64 + obs_cam[...]

    for k in range(2):
        rs[k] = rs_in[pl.ds(k, TILES, stride=2), :] * valid
    for k in range(6):
        jp[k] = jp[k] * valid
        jpt[k] = sorted_t(jp[k], 0)
    square = [jpt[i] * jpt[j] + jpt[3 + i] * jpt[3 + j] for i, j in PAIRS]
    put_points(square, contrib_h)
    pl.semaphore_wait(barrier, len(greeted))
    collect_start(6, *pts_h)

    start = jnp.concatenate(
        [
            jnp.concatenate([start_r[:, 2 * p, :], start_r[:, 2 * p + 1, :]], axis=1)[:, None, :]
            for p in range(2)
        ],
        axis=1,
    )
    take_cams(start, 0)
    for k in range(2):
        mv[k] = rs[k] + gg[0, k]
    put_points(to_points(mv[0], mv[1]), contrib)
    collect_start(3, *pts)
    put_points(to_points(gg[0, 0], gg[0, 1]), contrib_y)
    collect_start(3, *pts_y)
    def rows_of(t, carry):
        slot = slot_s[t]
        n, q = slot >> 4, slot & 15
        row_s[0, t] = n * (3 * NBLK) + q
        row_s[1, t] = n * (6 * NBLK) + q
        return carry

    lax.fori_loop(0, TILES, rows_of, 0)
    found = order(1, obs_cam[...], lane & 63)
    mine = found & ((lane >> 6) == parity)
    hit_c[0] = jnp.where(mine & (pair == 0), 1.0, 0.0)
    hit_c[1] = jnp.where(mine & (pair == 1), 1.0, 0.0)
    for k in range(18):
        jct[k] = sorted_t(jc[k] * valid, 1)
    cost_row = lane_sum(rs[...] * rs[...])
    hess = collect_wait(6, *pts_h)
    for c in range(6):
        hess_b[c] = hess[c]
    inv = invert(hess, LAMBDAS[0])
    for c in range(6):
        inv_b[0, c] = inv[c]
    ybuf[0] = jnp.stack(collect_wait(3, *pts))

    costs = []
    update = start
    upd_sum = jnp.zeros_like(start)
    step_sum = jnp.zeros((3, NBLK, LANES), F32)

    def weighted(w):
        h = [hess_b[c] for c in range(6)]
        return [
            h[0] * w[0] + h[1] * w[1] + h[2] * w[2],
            h[1] * w[0] + h[3] * w[1] + h[4] * w[2],
            h[2] * w[0] + h[4] * w[1] + h[5] * w[2],
        ]

    def inner(u, v):
        return lane_sum(u[0] * v[0] + u[1] * v[1] + u[2] * v[2])

    def three(buf, b):
        return [buf[b, m] for m in range(3)]

    def mix(p, u, q, v):
        return [p * u[m] + q * v[m] for m in range(3)]

    w0 = apply_inverse(inv, three(ybuf, 0))
    wbuf[0] = jnp.stack(w0)
    spread_start(w0, *out_s)
    diag = put_cams([jct[k] * jct[k] + jct[CPAR + k] * jct[CPAR + k] for k in range(CPAR)])
    inv = invert(hess, LAMBDAS[1])
    for c in range(6):
        inv_b[1, c] = inv[c]
    spread_wait(*out_s)
    near = take_points(recv_s)

    for step in range(2):
        damping = LAMBDAS[step]
        last = step == 1
        cam_damp = damping * (diag + 1.0)
        precond = diag + cam_damp
        if step == 0:
            eliminate(mv[0], mv[1], near, 0)
        r0 = -back_to_cams(0) - cam_damp * update
        z0 = r0 / precond

        take_cams(z0, 1)
        put_points(to_points(gg[1, 0], gg[1, 1]), contrib)
        collect_start(3, *pts)
        if last:
            spread_wait(*out_2)
            near = take_points(recv_2)
            for r in range(2):
                shift = jp[3 * r] * near[0] + jp[3 * r + 1] * near[1] + jp[3 * r + 2] * near[2]
                res = rs[r] - cb * shift
                rs[r] = res
                mv[r] = mv[r] + res
            cost_row = lane_sum(rs[...] * rs[...])
        y = collect_wait(3, *pts)
        ybuf[1] = jnp.stack(y)
        w = apply_inverse([inv_b[step, c] for c in range(6)], y)
        wbuf[1] = jnp.stack(w)
        spread_start(w, *out_s)
        g1_sq = lane_sum(gg[1, 0] * gg[1, 0] + gg[1, 1] * gg[1, 1])
        yw1 = inner(y, w)
        hidden_start(
            step,
            [lane_sum(r0 * z0), g1_sq - yw1 + lane_sum(cam_damp * (z0 * z0)), cost_row],
        )
        spread_wait(*out_s)
        near = take_points(recv_s)
        eliminate(gg[1, 0], gg[1, 1], near, 1)
        c0 = back_to_cams(1) + cam_damp * z0
        hidden_turn(step)
        u = c0 / precond

        take_cams(u, 2)
        put_points(to_points(gg[2, 0], gg[2, 1]), contrib)
        collect_start(3, *pts)

        dots = hidden_wait(step)
        resid_dot, curve = dots[0], dots[1]
        costs.append(0.5 * dots[2])
        alpha = resid_dot / curve
        r1 = r0 - alpha * c0
        z1 = r1 / precond
        turn = [gg[1, r] - alpha * gg[2, r] for r in range(2)]
        turn_sq = lane_sum(turn[0] * turn[0] + turn[1] * turn[1])
        turn_damp = lane_sum(cam_damp * (z1 * z1))
        rows = [lane_sum(r1 * z1), lane_sum(z1 * c0)]
        if last:
            base = [mv[r] + alpha * gg[1, r] for r in range(2)]
            y_base = mix(1.0, three(ybuf, 0), alpha, three(ybuf, 1))
            w_base = mix(1.0, three(wbuf, 0), alpha, three(wbuf, 1))
            hw_base = weighted(w_base)
            w1 = three(wbuf, 1)
            hw_one = weighted(w1)
            y1 = three(ybuf, 1)
            rows += [
                lane_sum(base[0] * base[0] + base[1] * base[1])
                - 2.0 * inner(y_base, w_base)
                + inner(w_base, hw_base),
                lane_sum(base[0] * gg[1, 0] + base[1] * gg[1, 1])
                - inner(y_base, w1)
                - inner(y1, w_base)
                + inner(w_base, hw_one),
                g1_sq - 2.0 * yw1 + inner(w1, hw_one),
            ]
            base_turn = lane_sum(base[0] * turn[0] + base[1] * turn[1])
            one_turn = lane_sum(gg[1, 0] * turn[0] + gg[1, 1] * turn[1])
        else:
            scale = [damping * (hess[c] + 1.0) for c in (0, 3, 5)]
            y_start = collect_wait(3, *pts_y)
            inv_next = [inv_b[1, c] for c in range(6)]
            held = [
                [scale[m] * wbuf[0, m] + y_start[m] for m in range(3)],
                [scale[m] * wbuf[1, m] + ybuf[1, m] for m in range(3)],
            ]
            ahead = [apply_inverse(inv_next, v) for v in held]
            spread_start(mix(1.0, ahead[0], alpha, ahead[1]) + ahead[1], *out_w)

        y = collect_wait(3, *pts)
        ybuf[2] = jnp.stack(y)
        w = apply_inverse([inv_b[step, c] for c in range(6)], y)
        wbuf[2] = jnp.stack(w)
        y_turn = mix(1.0, three(ybuf, 1), -alpha, y)
        w_turn = mix(1.0, three(wbuf, 1), -alpha, w)
        yw = inner(y_turn, w_turn)
        rows.append(turn_sq - yw + turn_damp)
        if last:
            hw_turn = weighted(w_turn)
            rows += [
                base_turn
                - inner(y_base, w_turn)
                - inner(y_turn, w_base)
                + inner(w_base, hw_turn),
                one_turn - inner(y1, w_turn) - inner(y_turn, w1) + inner(w1, hw_turn),
                turn_sq - 2.0 * yw + inner(w_turn, hw_turn),
            ]
        total_start(step, rows)
        if not last:
            held.append([scale[m] * w[m] + y[m] for m in range(3)])
            ahead.append(apply_inverse(inv_next, held[2]))
            w_move = [-alpha * (ahead[2][m] + w[m]) for m in range(3)]
        total_turn(step)
        if last:
            spread_start(w, *out_s)
        else:
            spread_start(w_move, *out_s)
        if not last:
            spread_wait(*out_w)
            near_fix = take_points(recv_w)
            near_one = take_points(recv_w, 3)
            spread_wait(*out_s)
            spread_start(w, *out_2)
            near_move = take_points(recv_s)
        else:
            spread_wait(*out_s)
            near = take_points(recv_s)
            eliminate(gg[2, 0], gg[2, 1], near, 2)
        dots = total_wait(step)
        fresh, cross = dots[0], dots[1]
        beta = fresh / resid_dot
        more = 1.0 + beta
        curve1 = dots[5 if last else 2] + 2.0 * beta * cross + beta * beta * curve
        alpha1 = fresh / curve1
        ca = alpha + alpha1 * more
        cb = -(alpha1 * alpha)
        update = update + alpha * z0 + alpha1 * (z1 + beta * z0)
        upd_sum = upd_sum + update
        step_sum = step_sum - (wbuf[0] + ca * wbuf[1] + cb * wbuf[2])
        if not last:
            step1 = alpha1 * more
            near = [
                near_fix[m] + step1 * near_one[m] + alpha1 * near_move[m] for m in range(3)
            ]
            for r in range(2):
                rs[r] = bk[0, r] + ca * bk[1, r] + cb * gg[2, r]
                mv[r] = gg[0, r] + ca * gg[1, r] + cb * gg[2, r]
            eliminate(rs[0] + mv[0], rs[1] + mv[1], near, 0)
            ybuf[0] = jnp.stack([held[0][m] + ca * held[1][m] + cb * held[2][m] for m in range(3)])
            wbuf[0] = jnp.stack(
                [ahead[0][m] + ca * ahead[1][m] + cb * ahead[2][m] for m in range(3)]
            )
        else:
            for r in range(2):
                res_o[pl.ds(r, TILES, stride=2), :] = bk[0, r] + ca * bk[1, r] + cb * bk[2, r]
            base_sq, base_one, one_sq = dots[2], dots[3], dots[4]
            base_dot, one_dot, turn_dot = dots[6], dots[7], dots[8]
            square = turn_dot + 2.0 * beta * one_dot + beta * beta * one_sq
            costs.append(
                0.5
                * (
                    base_sq
                    + 2.0 * alpha1 * (base_dot + beta * base_one)
                    + alpha1 * alpha1 * square
                )
            )
    for p in range(2):
        both = upd_sum[:, p, :]
        cam_o[:, 2 * p, :] = cam_r[:, 2 * p, :] + both[:, 0:64]
        cam_o[:, 2 * p + 1, :] = cam_r[:, 2 * p + 1, :] + both[:, 64:128]
    pt_o[...] = pt_r[...] + step_sum
    third = lax.broadcasted_iota(jnp.int32, (1, 3), 1)
    cost_o[...] = jnp.where(third == 0, costs[0], jnp.where(third == 1, costs[1], costs[2]))
    for a in range(2):
        hidden_drain(a)
        total_drain(a)


def hand_over(cam_i, pt_i, res_i, cost_i, cam_o, pt_o, res_o, cost_o):
    res_o[...] = res_i[...]
    cam_o[...] = cam_i[...]
    pt_o[...] = pt_i[...]
    cost_o[...] = cost_i[...]


def body(
    jac_cam,
    jac_pt,
    resid0,
    obs_count,
    tile_camera,
    tile_points,
    obs_camera,
    obs_point,
    cam_params,
    pt_params,
    cg_start,
):
    vmem = pl.BlockSpec(memory_space=pltpu.VMEM)
    hbm = pl.BlockSpec(memory_space=pltpu.HBM)
    big = (TILES, LANES)
    blk = (NBLK, LANES)
    dma = pltpu.SemaphoreType.DMA
    shapes = [
        jax.ShapeDtypeStruct((CPAR, 4, 64), F32),
        jax.ShapeDtypeStruct((3,) + blk, F32),
        jax.ShapeDtypeStruct((2 * TILES, LANES), F32),
        jax.ShapeDtypeStruct((1, 3), F32),
    ]
    results = pl.pallas_call(
        kernel,
        out_shape=shapes,
        in_specs=[pl.BlockSpec(memory_space=pltpu.SMEM)] + [hbm] * 11,
        out_specs=[vmem] * 4,
        scratch_shapes=[
            pltpu.VMEM((18,) + big, F32),
            pltpu.VMEM((6,) + big, F32),
            pltpu.VMEM((2,) + big, F32),
            pltpu.VMEM((2 * TILES, LANES), F32),
            pltpu.VMEM(big, jnp.int32),
            pltpu.VMEM(big, jnp.int32),
            pltpu.VMEM((1, LANES), jnp.int32),
            pltpu.VMEM((1, LANES), jnp.int32),
            pltpu.VMEM((1, LANES), jnp.int32),
            pltpu.VMEM((CPAR, 4, 64), F32),
            pltpu.VMEM((CPAR, 4, 64), F32),
            pltpu.VMEM((3,) + blk, F32),
            pltpu.VMEM((18,) + big, F32),
            pltpu.VMEM((6,) + big, F32),
            pltpu.VMEM((PAD + LANES, LANES), F32),
            pltpu.VMEM((CPAR, PAD + LANES, LANES), F32),
            pltpu.VMEM((CPAR, PAD + LANES, LANES), F32),
            pltpu.VMEM((2,) + big, jnp.int32),
            pltpu.VMEM((2,) + big, jnp.int32),
            pltpu.VMEM((2, 7) + big, F32),
            pltpu.VMEM(big, F32),
            pltpu.VMEM((2,) + big, F32),
            pltpu.VMEM(big, jnp.int32),
            pltpu.VMEM(big, F32),
            pltpu.VMEM(big, jnp.int32),
            pltpu.VMEM((SLOTS, 3 * TILES), BF16),
            pltpu.VMEM((3,) + big, F32),
            pltpu.VMEM((3, 2) + big, F32),
            pltpu.VMEM((3, 2) + big, F32),
            pltpu.VMEM((2,) + big, F32),
            pltpu.VMEM((9, 3) + blk, F32),
            pltpu.VMEM((8, 3) + blk, F32),
            pltpu.VMEM((9, 6) + blk, F32),
            pltpu.VMEM((8, 6) + blk, F32),
            pltpu.VMEM((9, 3) + blk, F32),
            pltpu.VMEM((8, 3) + blk, F32),
            pltpu.VMEM((3 * NBLK, LANES), F32),
            pltpu.VMEM((27 * NBLK, LANES), F32),
            pltpu.VMEM((6 * NBLK, LANES), F32),
            pltpu.VMEM((54 * NBLK, LANES), F32),
            pltpu.VMEM((3 * NBLK, LANES), F32),
            pltpu.VMEM((27 * NBLK, LANES), F32),
            pltpu.VMEM((6,) + blk, F32),
            pltpu.VMEM((2, 6) + blk, F32),
            pltpu.VMEM((3, 3) + blk, F32),
            pltpu.VMEM((3, 3) + blk, F32),
            pltpu.VMEM((CPAR, 2, LANES), F32),
            pltpu.VMEM((CPAR, 2, LANES), F32),
            pltpu.VMEM((2, 1, LANES), F32),
            pltpu.VMEM((2, 1, LANES), F32),
            pltpu.VMEM((2, 1, LANES), F32),
            pltpu.VMEM((2, CHIPS, LANES), F32),
            pltpu.VMEM((2, 1, LANES), F32),
            pltpu.VMEM((2, GX, LANES), F32),
            pltpu.VMEM((2, 1, LANES), F32),
            pltpu.VMEM((2, GY, LANES), F32),
            dma((11,)),
            pltpu.SMEM((2, LANES), jnp.int32),
        ]
        + [dma((8,))] * 12
        + [dma((2,))] * 8,
        compiler_params=pltpu.CompilerParams(
            collective_id=0, has_side_effects=True, vmem_limit_bytes=62 * 1024 * 1024
        ),
    )(
        tile_points[0, 0],
        jnp.transpose(jac_cam[0, 0], (1, 0, 2)),
        jnp.transpose(jac_pt[0, 0], (1, 0, 2)),
        resid0.reshape(2 * TILES, LANES),
        obs_camera[0, 0],
        obs_point[0, 0],
        obs_count[0],
        tile_camera[0],
        tile_points[0],
        jnp.transpose(cg_start[0, 0], (1, 0, 2)),
        jnp.transpose(cam_params[0, 0], (1, 0, 2)),
        jnp.transpose(pt_params[0, 0], (1, 0, 2)),
    )
    cam, pt, res, costs = pl.pallas_call(
        hand_over,
        out_shape=shapes,
        in_specs=[vmem] * 4,
        out_specs=[vmem] * 4,
    )(*results)
    cam_out = jnp.transpose(cam, (1, 0, 2))[None, None]
    pt_out = jnp.transpose(pt, (1, 0, 2))[None, None]
    return cam_out, pt_out, res.reshape(1, 1, TILES, 2, LANES), costs.reshape(3)


def solution(mesh):
    wide = P("gx", "gy", None, None, None)
    in_specs = (
        wide,
        wide,
        wide,
        P("gx", "gy", None),
        P("gx", "gy", None),
        P("gx", "gy", None),
        P("gx", "gy", None, None),
        P("gx", "gy", None, None),
        wide,
        wide,
        wide,
    )
    out_specs = (wide, wide, wide, P())
    return jax.shard_map(body, mesh=mesh, in_specs=in_specs, out_specs=out_specs, check_vma=False)
```
